32 devices in a mesh: grp: 8 (over z, x), hd: 4 (over y, core).
Axes of the slice: x: 2, y: 2, z: 4, core: 2. Of those that a mesh axis runs over, the one named last changes fastest.
Arguments:
- radar_tokens: bfloat16 [16384, 768], P(('grp', 'hd')), may hold values from -6 to 6
- optic_tokens: bfloat16 [16384, 768], P(('grp', 'hd')), may hold values from -6 to 6
- tile_lengths: int32 [8, 4, 3], P('grp'), may hold values from 0 to 400, as said below
- norm_gains: float32 [3, 768], replicated, may hold values from 0.5 to 1.5
- norm_shifts: float32 [3, 768], replicated, may hold values from -3 to 3
- self_qkv: bfloat16 [768, 2304], replicated, may hold values from -0.21875 to 0.21875
- self_out: bfloat16 [768, 768], replicated, may hold values from -0.4375 to 0.4375
- cross_query: bfloat16 [768, 768], replicated, may hold values from -0.21875 to 0.21875
- cross_keyval: bfloat16 [768, 1536], replicated, may hold values from -0.21875 to 0.21875
- cross_out: bfloat16 [768, 768], replicated, may hold values from -0.875 to 0.875
- hidden_in: bfloat16 [768, 3072], replicated, may hold values from -0.21875 to 0.21875
- hidden_out: bfloat16 [3072, 768], replicated, may hold values from -0.109375 to 0.109375
- proj_biases: float32 [3, 768], replicated, may hold values from -3 to 3
- hidden_bias: float32 [3072], replicated, may hold values from -3 to 3
- cotangent: bfloat16 [16384, 768], P(('grp', 'hd')), may hold values from -6 to 6
Outputs:
- layer_output: bfloat16 [16384, 768], P(('grp', 'hd'))
- radar_grad: float32 [16384, 768], P(('grp', 'hd'))
- optic_grad: float32 [16384, 768], P(('grp', 'hd'))
- self_qkv_grad: float32 [768, 2304], P('hd')
- self_out_grad: float32 [768, 768], P('hd')
- cross_query_grad: float32 [768, 768], P('hd')
- cross_keyval_grad: float32 [768, 1536], P('hd')
- cross_out_grad: float32 [768, 768], P('hd')
- hidden_in_grad: float32 [768, 3072], P('hd')
- hidden_out_grad: float32 [3072, 768], P('hd')
- norm_gains_grad: float32 [3, 768], P(None, 'hd')
- norm_shifts_grad: float32 [3, 768], P(None, 'hd')
- proj_biases_grad: float32 [3, 768], P(None, 'hd')
- hidden_bias_grad: float32 [3072], P('hd')
The draws below stay inside these ranges and needn't reach their ends.
Inputs may be any that keep to these rules, and one draw needn't show every extreme that they name: `tile_lengths`: each device's 3 slots hold the patch counts of its tiles, each 144, 225 or 400, from the first slot on, then zeros; every device holds at least one tile, its counts sum to at most 512, and the first tile of the first device has 400 patches.
All inputs are finite; a program needn't handle non-finite values.
Results may differ from the reference program's by a relative error of at most 0.02.
Values may be sent and summed in bfloat16 or wider, within the bound.
No kernel may reach another device: no remote copies, remote signals or barrier semaphores. Data moves between devices by JAX's collectives and lax.ppermute only.
A program may use at most 192 MiB of HBM per device.

```python
import jax
import jax.numpy as jnp
from jax import lax

HEADS = 12
HDIM = 64
D = 768
FF = 3072
SIDE_A = 12
SIDE_B = 15
SIDE_C = 20
TOK_DEV = 512
TILES_DEV = 3
TOKENS = 16384
N_GRP = 8
N_HD = 4


def draw_tile_lengths(key, part):
    key = jax.random.fold_in(key, 11)
    picks = jax.random.randint(key, (N_GRP, N_HD, TILES_DEV), 0, 3)
    counts = jnp.where(picks == 0, SIDE_A * SIDE_A, jnp.where(picks == 1, SIDE_B * SIDE_B, SIDE_C * SIDE_C)).astype(jnp.int32)
    first_slot = (jnp.arange(N_GRP)[:, None, None] == 0) & (jnp.arange(N_HD)[None, :, None] == 0) & (jnp.arange(TILES_DEV)[None, None, :] == 0)
    counts = jnp.where(first_slot, SIDE_C * SIDE_C, counts).astype(jnp.int32)
    running = jnp.cumsum(counts, axis=2, dtype=jnp.int32)
    return jnp.where(running <= TOK_DEV, counts, 0).astype(jnp.int32)


def block_levels(stream_key, dims, split, least, high):
    level, own = 1.0, jax.random.fold_in(stream_key, 6)
    for dim, parts in split:
        draws = jnp.exp(jax.random.uniform(jax.random.fold_in(own, dim), (parts,), jnp.float32, least / len(split), high / len(split)))
        level = level * jnp.repeat(draws, dims[dim] // parts).reshape([-1 if axis == dim else 1 for axis in range(len(dims))])
    return level


def bell_draw(stream_key, dims, deviation, limit, split=(), held_as=jnp.bfloat16):
    entries = jax.random.normal(stream_key, dims, jnp.float32) * deviation
    if len(split) > 0:
        entries = block_levels(stream_key, dims, split, -0.22, 0.18) * entries
    return jnp.clip(entries, min=-limit, max=limit).astype(held_as)


def setup_inputs(seed: int = 0) -> dict:
    keys = jax.random.split(jax.random.key(seed), 16)
    return {
        "radar_tokens": bell_draw(keys[0], (TOKENS, D), 1.0, 6.0, ((0, 32),)),
        "optic_tokens": bell_draw(keys[1], (TOKENS, D), 1.0, 6.0, ((0, 32),)),
        "tile_lengths": draw_tile_lengths(jax.random.fold_in(keys[15], 71), 0),
        "norm_gains": jnp.clip(1.0 + 0.1 * jax.random.normal(keys[3], (3, D), jnp.float32), 0.5, 1.5),
        "norm_shifts": bell_draw(keys[4], (3, D), 0.3, 3.0, (), jnp.float32),
        "self_qkv": bell_draw(keys[5], (D, 3 * D), D ** -0.5, 0.21875),
        "self_out": bell_draw(keys[6], (D, D), (D // 4) ** -0.5, 0.4375),
        "cross_query": bell_draw(keys[7], (D, D), D ** -0.5, 0.21875),
        "cross_keyval": bell_draw(keys[8], (D, 2 * D), D ** -0.5, 0.21875),
        "cross_out": bell_draw(keys[9], (D, D), (D // 16) ** -0.5, 0.875),
        "hidden_in": bell_draw(keys[10], (D, FF), D ** -0.5, 0.21875),
        "hidden_out": bell_draw(keys[11], (FF, D), FF ** -0.5, 0.109375),
        "proj_biases": bell_draw(keys[12], (3, D), 0.3, 3.0, (), jnp.float32),
        "hidden_bias": bell_draw(keys[13], (FF,), 0.5, 3.0, (), jnp.float32),
        "cotangent": bell_draw(keys[14], (TOKENS, D), 1.0, 6.0, ((0, 32),)),
    }


epsilon = 1e-06
masked_score = -1e+30
highest = lax.Precision.HIGHEST

@jax.custom_vjp
def low(v):
    return lax.optimization_barrier(v.astype(jnp.bfloat16)).astype(jnp.float32)

@jax.custom_vjp
def low_back(v):
    return v

def low_keep(v):
    return (low(v), None)

def low_pass(kept, grad):
    return (grad,)

def back_keep(v):
    return (v, None)

def back_low(kept, grad):
    return (low(grad),)
low.defvjp(low_keep, low_pass)
low_back.defvjp(back_keep, back_low)

def round_both(values):
    return low_back(low(values))

def layer_norm(values, norm_gain, norm_shift):
    average = lax.optimization_barrier(jnp.mean(values, axis=-1, keepdims=True))
    centred = values - average
    variance = lax.optimization_barrier(jnp.mean(centred * centred, axis=-1, keepdims=True))
    return centred * lax.rsqrt(variance + epsilon) * norm_gain + norm_shift

def gelu_exact(values):
    return jax.nn.gelu(values, approximate=False)

def tile_layout(lengths, local_rows):
    tile_end = jnp.cumsum(lengths, dtype=jnp.int32)
    starts = tile_end - lengths
    position = jnp.arange(local_rows, dtype=jnp.int32)
    segment = lax.optimization_barrier(jnp.sum((position[:, None] >= tile_end[None, :]).astype(jnp.int32), axis=1, dtype=jnp.int32))
    slots = jnp.arange(lengths.shape[0], dtype=jnp.int32)
    onehot = (segment[:, None] == slots[None, :]).astype(jnp.int32)
    tile_start = lax.optimization_barrier(jnp.sum(onehot * starts[None, :], axis=1, dtype=jnp.int32))
    extent = lax.optimization_barrier(jnp.sum(onehot * lengths[None, :], axis=1, dtype=jnp.int32))
    offset = position - tile_start
    tile_side = jnp.where(extent == SIDE_A * SIDE_A, SIDE_A, jnp.where(extent == SIDE_B * SIDE_B, SIDE_B, SIDE_C)).astype(jnp.int32)
    is_valid = segment < lengths.shape[0]
    row_pos = jnp.where(is_valid, offset // tile_side, 0).astype(jnp.int32)
    col_pos = jnp.where(is_valid, offset % tile_side, 0).astype(jnp.int32)
    return (segment, row_pos, col_pos, is_valid)

def alibi_bias(slopes, rows_query, cols_query, rows_key, cols_key):
    delta_row = (rows_query[:, None] - rows_key[None, :]).astype(jnp.float32)
    delta_col = (cols_query[:, None] - cols_key[None, :]).astype(jnp.float32)
    distance = jnp.sqrt(delta_row * delta_row + delta_col * delta_col)
    return -slopes[:, None, None] * distance[None]

def attend(queries, key_rows, value_rows, segment, row_pos, col_pos, slopes, with_bias):
    scale = HDIM ** (-0.5)
    scores = jnp.einsum('qhd,khd->hqk', queries, key_rows, precision=highest) * scale
    if with_bias:
        scores = scores + alibi_bias(slopes, row_pos, col_pos, row_pos, col_pos)
    scores = low_back(scores)
    same_tile = segment[:, None] == segment[None, :]
    scores = jnp.where(same_tile[None], scores, masked_score)
    row_max = lax.optimization_barrier(jnp.max(scores, axis=-1, keepdims=True))
    weights_exp = jnp.exp(scores - row_max)
    probs_all = weights_exp / lax.optimization_barrier(jnp.sum(weights_exp, axis=-1, keepdims=True))
    return jnp.einsum('hqk,khd->qhd', low(probs_all), value_rows, precision=highest)

def attend_all(queries, key_rows, value_rows, layout, slopes, with_bias):
    segment, row_pos, col_pos, is_valid = layout
    devices = segment.shape[0]

    def shaped(matrix):
        return matrix.reshape(devices, TOK_DEV, HEADS, HDIM)

    def per_device(operands):
        query_dev, key_dev, value_dev, seg_dev, row_dev, col_dev = operands
        return attend(query_dev, key_dev, value_dev, seg_dev, row_dev, col_dev, slopes, with_bias)
    result = lax.map(jax.checkpoint(per_device), (shaped(queries), shaped(key_rows), shaped(value_rows), segment, row_pos, col_pos))
    return result.reshape(devices * TOK_DEV, HEADS * HDIM)

def forward(radar_rows, optic_rows, norm_gains, norm_shifts, self_qkv, self_out, cross_query, cross_keyval, cross_out, hidden_in, hidden_out, proj_biases, hidden_bias, layout):
    model_width = radar_rows.shape[1]
    slopes = jnp.exp2(-(jnp.arange(HEADS, dtype=jnp.float32) + 1.0) * (8.0 / HEADS))
    normed_one = low(layer_norm(radar_rows, norm_gains[0], norm_shifts[0]))
    packed = jnp.dot(normed_one, self_qkv, precision=highest)
    queries = round_both(packed[:, :model_width])
    key_rows = round_both(packed[:, model_width:2 * model_width])
    value_rows = round_both(packed[:, 2 * model_width:])
    self_att = round_both(attend_all(queries, key_rows, value_rows, layout, slopes, True))
    residual_one = radar_rows + low_back(jnp.dot(self_att, self_out, precision=highest) + proj_biases[0])
    normed_two = low(layer_norm(residual_one, norm_gains[1], norm_shifts[1]))
    cross_queries = round_both(jnp.dot(normed_two, cross_query, precision=highest))
    optic_packed = jnp.dot(optic_rows, cross_keyval, precision=highest)
    optic_keys = round_both(optic_packed[:, :model_width])
    optic_values = round_both(optic_packed[:, model_width:])
    cross_att = round_both(attend_all(cross_queries, optic_keys, optic_values, layout, slopes, False))
    residual_two = residual_one + low_back(jnp.dot(cross_att, cross_out, precision=highest) + proj_biases[1])
    normed_three = low(layer_norm(residual_two, norm_gains[2], norm_shifts[2]))
    hidden_pre = low_back(jnp.dot(normed_three, hidden_in, precision=highest) + hidden_bias)
    activated = low(gelu_exact(hidden_pre))
    is_valid = layout[3].reshape(-1)
    return jnp.where(is_valid[:, None], residual_two + (jnp.dot(activated, hidden_out, precision=highest) + proj_biases[2]), 0.0)

def reference(radar_tokens, optic_tokens, tile_lengths, norm_gains, norm_shifts, self_qkv, self_out, cross_query, cross_keyval, cross_out, hidden_in, hidden_out, proj_biases, hidden_bias, cotangent):
    device_rows = tile_lengths.reshape(-1, tile_lengths.shape[2])

    def layout_of(lengths_row):
        return tile_layout(lengths_row, TOK_DEV)
    layout = jax.vmap(layout_of)(device_rows)
    floats = tuple((operand.astype(jnp.float32) for operand in (radar_tokens, optic_tokens, norm_gains, norm_shifts, self_qkv, self_out, cross_query, cross_keyval, cross_out, hidden_in, hidden_out, proj_biases, hidden_bias)))

    def wrapped(*params):
        return forward(*params, layout)
    final, pullback = jax.vjp(wrapped, *floats)
    grads = pullback(cotangent.astype(jnp.float32))
    return (final.astype(jnp.bfloat16), grads[0], grads[1], grads[4], grads[5], grads[6], grads[7], grads[8], grads[9], grads[10], grads[2], grads[3], grads[11], grads[12])
```

```python
import functools
import math

import jax
import jax.numpy as jnp
import numpy as np
from jax import lax
from jax.experimental import pallas as pl
from jax.experimental.pallas import tpu as pltpu
from jax.sharding import PartitionSpec as P

HEADS = 12
HDIM = 64
SIDES = (12, 15, 20)
QUAD = 4
EPSILON = 1e-06
MASKED = -1e30
FAR = 1e33
F32 = jnp.float32
BF16 = jnp.bfloat16
VMEM_LIMIT = 56 * 1024 * 1024


def rows_in_use(local_rows, slots):
    counts = [0] + [side * side for side in SIDES]
    sums = {0}
    for _ in range(slots):
        sums = {a + b for a in sums for b in counts if a + b <= local_rows}
    return min(local_rows, -(-max(sums) // 16) * 16)


def dot_nn(left, right):
    return lax.dot_general(left, right, (((1,), (0,)), ((), ())), preferred_element_type=F32)


def dot_nt(left, right):
    return lax.dot_general(left, right, (((1,), (1,)), ((), ())), preferred_element_type=F32)


def norm_parts(values):
    average = jnp.mean(values, axis=-1, keepdims=True)
    centred = values - average
    variance = jnp.mean(centred * centred, axis=-1, keepdims=True)
    return centred, lax.rsqrt(variance + EPSILON)


def norm(values, gain, shift):
    centred, inverse = norm_parts(values)
    return centred * inverse * gain + shift


def norm_back(values, gain, grad):
    centred, inverse = norm_parts(values)
    unit = centred * inverse
    gain_grad = jnp.sum(grad * unit, axis=0, keepdims=True)
    shift_grad = jnp.sum(grad, axis=0, keepdims=True)
    scaled = grad * gain
    lift = jnp.mean(scaled, axis=-1, keepdims=True)
    tilt = jnp.mean(scaled * unit, axis=-1, keepdims=True)
    return inverse * (scaled - lift - unit * tilt), gain_grad, shift_grad


def layout_of(lens_ref, shape, dim):
    place = lax.broadcasted_iota(jnp.int32, shape, dim)
    count = [lens_ref[i] for i in range(3)]
    ends = [count[0], count[0] + count[1], count[0] + count[1] + count[2]]
    zero = jnp.zeros(shape, jnp.int32)
    segment = zero
    for end in ends:
        segment = segment + jnp.where(place >= end, 1, 0)
    sides = [
        jnp.where(c == SIDES[0] ** 2, SIDES[0], jnp.where(c == SIDES[1] ** 2, SIDES[1], SIDES[2]))
        for c in count
    ]
    start = jnp.where(segment == 0, 0, jnp.where(segment == 1, ends[0], ends[1]))
    side = jnp.where(segment == 0, sides[0], jnp.where(segment == 1, sides[1], sides[2])).astype(F32)
    offset = (place - start).astype(F32)
    row = jnp.floor((offset + 0.5) / side)
    col = offset - row * side
    valid = segment < 3
    return segment, jnp.where(valid, row, 0.0), jnp.where(valid, col, 0.0), valid


def gelu_parts(values):
    bell = jnp.exp(values * values * -0.5)
    size = jnp.abs(values) * math.sqrt(0.5)
    t = 1.0 / (1.0 + 0.3275911 * size)
    poly = t * (
        0.254829592
        + t * (-0.284496736 + t * (1.421413741 + t * (-1.453152027 + t * 1.061405429)))
    )
    tail = 0.5 * poly * bell
    below = jnp.where(values < 0, tail, 1.0 - tail)
    return values * below, below + values * bell * (1.0 / math.sqrt(2.0 * math.pi))


def whole(shape):
    return pl.BlockSpec(shape, lambda *_: (0,) * len(shape))


def smem():
    return pl.BlockSpec(memory_space=pltpu.SMEM)


def cols(rows, width, first=0):
    return pl.BlockSpec((rows, width), lambda j, *_: (0, first + j))


def rowblk(height, width, first=0):
    return pl.BlockSpec((height, width), lambda j, *_: (first + j, 0))


def params(**kw):
    return pltpu.CompilerParams(vmem_limit_bytes=VMEM_LIMIT, dimension_semantics=("arbitrary",), **kw)


def attend_quad(q, k, v, add_bias, probs_ref):
    lane = lax.broadcasted_iota(jnp.int32, q.shape, 1)
    scaled = q * jnp.asarray(HDIM**-0.5, BF16)
    v_t = v.T
    outs = []
    for h in range(QUAD):
        q_h = jnp.where(lane // HDIM == h, scaled, jnp.zeros_like(scaled))
        scores = add_bias(dot_nt(k, q_h), h)
        top = jnp.max(scores, axis=0, keepdims=True)
        weights = jnp.exp(scores - top)
        total = jnp.sum(weights, axis=0, keepdims=True)
        probs = (weights * (1.0 / total)).astype(BF16)
        probs_ref[h] = probs
        outs.append(dot_nn(v_t[h * HDIM : (h + 1) * HDIM], probs))
    return jnp.concatenate(outs, axis=0).astype(BF16).T


def self_forward_kernel(
    lens, slopes, radar, gain, shift, gain_next, shift_next, bias, wq, wk, wv, wo,
    n1, q_out, k_out, v_out, probs, att_out, resid, n2, dist,
):
    j = pl.program_id(0)
    rows = n1.shape[0]

    @pl.when(j == 0)
    def _():
        wide = radar[...].astype(F32)
        n1[...] = norm(wide, gain[...], shift[...]).astype(BF16)
        resid[...] = wide + bias[...]
        seg_k, row_k, col_k, _ = layout_of(lens, (rows, 1), 0)
        seg_q, row_q, col_q, _ = layout_of(lens, (1, rows), 1)
        dr = row_k - row_q
        dc = col_k - col_q
        dist[...] = jnp.where(seg_k == seg_q, jnp.sqrt(dr * dr + dc * dc), FAR)

    x = n1[...]
    q = dot_nn(x, wq[...]).astype(BF16)
    k = dot_nn(x, wk[...]).astype(BF16)
    v = dot_nn(x, wv[...]).astype(BF16)
    q_out[...] = q
    k_out[...] = k
    v_out[...] = v
    att = attend_quad(
        q, k, v, lambda s, h: s - slopes[j * QUAD + h] * dist[...], probs
    )
    att_out[...] = att
    resid[...] += dot_nn(att, wo[...])

    @pl.when(j == pl.num_programs(0) - 1)
    def _():
        n2[...] = norm(resid[...], gain_next[...], shift_next[...]).astype(BF16)


def cross_forward_kernel(
    lens, res_in, n_in, optic, gain_next, shift_next, bias, wq, wk, wv, wo,
    q_out, k_out, v_out, probs, att_out, resid, n3, mask,
):
    j = pl.program_id(0)
    rows = n_in.shape[0]

    @pl.when(j == 0)
    def _():
        resid[...] = res_in[...] + bias[...]
        seg_k = layout_of(lens, (rows, 1), 0)[0]
        seg_q = layout_of(lens, (1, rows), 1)[0]
        mask[...] = jnp.where(seg_k == seg_q, 0.0, MASKED)

    q = dot_nn(n_in[...], wq[...]).astype(BF16)
    k = dot_nn(optic[...], wk[...]).astype(BF16)
    v = dot_nn(optic[...], wv[...]).astype(BF16)
    q_out[...] = q
    k_out[...] = k
    v_out[...] = v
    att = attend_quad(q, k, v, lambda s, h: s + mask[...], probs)
    att_out[...] = att
    resid[...] += dot_nn(att, wo[...])

    @pl.when(j == pl.num_programs(0) - 1)
    def _():
        n3[...] = norm(resid[...], gain_next[...], shift_next[...]).astype(BF16)


def shaped(*shape, dtype=BF16):
    return jax.ShapeDtypeStruct(shape, dtype)


def self_forward(rows, lens, slopes, radar, gains, shifts, biases, w_qkv, w_out):
    d = radar.shape[1]
    wide = QUAD * HDIM
    steps = d // wide
    return pl.pallas_call(
        self_forward_kernel,
        grid=(steps,),
        in_specs=[
            smem(), smem(), whole((rows, d)),
            *[whole((1, d))] * 5,
            cols(d, wide), cols(d, wide, steps), cols(d, wide, 2 * steps), rowblk(wide, d),
        ],
        out_specs=[
            whole((rows, d)), cols(rows, wide), cols(rows, wide), cols(rows, wide),
            pl.BlockSpec((QUAD, rows, rows), lambda j: (j, 0, 0)),
            cols(rows, wide), whole((rows, d)), whole((rows, d)),
        ],
        out_shape=[
            shaped(rows, d), shaped(rows, d), shaped(rows, d), shaped(rows, d),
            shaped(HEADS, rows, rows), shaped(rows, d), shaped(rows, d, dtype=F32), shaped(rows, d),
        ],
        scratch_shapes=[pltpu.VMEM((rows, rows), F32)],
        compiler_params=params(),
        name="self_forward",
    )(lens, slopes, radar, gains[0:1], shifts[0:1], gains[1:2], shifts[1:2], biases[0:1],
      w_qkv, w_qkv, w_qkv, w_out)


def cross_forward(rows, lens, res_in, n_in, optic, gains, shifts, biases, w_q, w_kv, w_out):
    d = optic.shape[1]
    wide = QUAD * HDIM
    steps = d // wide
    return pl.pallas_call(
        cross_forward_kernel,
        grid=(steps,),
        in_specs=[
            smem(), whole((rows, d)), whole((rows, d)), whole((rows, d)),
            *[whole((1, d))] * 3,
            cols(d, wide), cols(d, wide), cols(d, wide, steps), rowblk(wide, d),
        ],
        out_specs=[
            cols(rows, wide), cols(rows, wide), cols(rows, wide),
            pl.BlockSpec((QUAD, rows, rows), lambda j: (j, 0, 0)),
            cols(rows, wide), whole((rows, d)), whole((rows, d)),
        ],
        out_shape=[
            shaped(rows, d), shaped(rows, d), shaped(rows, d),
            shaped(HEADS, rows, rows), shaped(rows, d), shaped(rows, d, dtype=F32), shaped(rows, d),
        ],
        scratch_shapes=[pltpu.VMEM((rows, rows), F32)],
        compiler_params=params(),
        name="cross_forward",
    )(lens, res_in, n_in, optic, gains[2:3], shifts[2:3], biases[1:2], w_q, w_kv, w_kv, w_out)


def place(meta, keep, send, grad, spot=None):
    first = meta[4] == 0
    part = grad.shape[0] // 8
    for y in range(2):
        for x in range(2):
            at = y * 4 + x
            low = grad[at * part : (at + 1) * part]
            high = grad[(at + 2) * part : (at + 3) * part]
            where_to = (y ^ meta[3]) * 2 + (x ^ meta[5])
            to = (where_to,) if spot is None else (where_to, slice(None), spot)
            keep[to] = jnp.where(first, low, high)
            send[to] = jnp.where(first, high, low)


def hidden_kernel(
    meta, res2, n3, cot, gain, bias, hb, win, wout,
    y_out, grad_two, dwin, dwin_s, dwout, dwout_s, dhb, gain_g, shift_g, bias_g,
    n3_t, gf, acc_y, acc_n,
):
    j = pl.program_id(0)
    rows = n3.shape[0]

    @pl.when(j == 0)
    def _():
        valid = layout_of(meta, (rows, 1), 0)[3]
        gf[...] = jnp.where(valid, cot[...], jnp.zeros_like(cot))
        n3_t[...] = n3[...].T
        acc_y[...] = jnp.zeros_like(acc_y)
        acc_n[...] = jnp.zeros_like(acc_n)

    act, slope = gelu_parts(dot_nn(n3[...], win[...]) + hb[...])
    act = act.astype(BF16)
    g_pre = (dot_nt(gf[...], wout[...]) * slope).astype(BF16)
    acc_y[...] += dot_nn(act, wout[...])
    acc_n[...] += dot_nt(g_pre, win[...])
    place(meta, dwin, dwin_s, dot_nn(n3_t[...], g_pre).astype(BF16))
    grad = dot_nn(act.T, gf[...]).astype(BF16)
    half = grad.shape[0] // 2
    mine = lax.rem(j, 2) == meta[4]

    def put(out):
        for x in range(2):
            out[x ^ meta[5]] = grad[x * half : (x + 1) * half]

    pl.when(mine)(lambda: put(dwout))
    pl.when(jnp.logical_not(mine))(lambda: put(dwout_s))
    dhb[...] = jnp.sum(g_pre.astype(F32), axis=0, keepdims=True)

    @pl.when(j == pl.num_programs(0) - 1)
    def _():
        valid = layout_of(meta, (rows, 1), 0)[3]
        y = jnp.where(valid, res2[...] + (acc_y[...] + bias[...]), 0.0)
        y_out[0:rows] = y.astype(BF16)
        if y_out.shape[0] > rows:
            y_out[rows:] = jnp.zeros((y_out.shape[0] - rows, y_out.shape[1]), BF16)
        part, g_gain, g_shift = norm_back(res2[...], gain[...], acc_n[...])
        wide = gf[...].astype(F32)
        grad_two[...] = wide + part
        gain_g[...] = g_gain
        shift_g[...] = g_shift
        bias_g[...] = jnp.sum(wide, axis=0, keepdims=True)


def hidden(rows, meta, res2, n3, cot, gains, biases, hb, win, wout):
    d = n3.shape[1]
    ff = win.shape[1]
    chunk = ff // 4
    vec = shaped(1, d, dtype=F32)
    eighth = shaped(4, d // 8, ff)
    wide = pl.BlockSpec((4, d // 8, chunk), lambda j, m: (0, 0, j))
    tall = pl.BlockSpec((2, ff // 8, d), lambda j, m: ((j // 2) ^ m[3], 0, 0))
    return pl.pallas_call(
        hidden_kernel,
        grid_spec=pltpu.PrefetchScalarGridSpec(
            num_scalar_prefetch=1,
            grid=(4,),
            in_specs=[
                whole((rows, d)), whole((rows, d)), whole((rows, d)),
                whole((1, d)), whole((1, d)), cols(1, chunk), cols(d, chunk), rowblk(chunk, d),
            ],
            out_specs=[
                whole((cot.shape[0], d)), whole((rows, d)), wide, wide, tall, tall,
                cols(1, chunk), whole((1, d)), whole((1, d)), whole((1, d)),
            ],
            scratch_shapes=[
                pltpu.VMEM((d, rows), BF16), pltpu.VMEM((rows, d), BF16),
                pltpu.VMEM((rows, d), F32), pltpu.VMEM((rows, d), F32),
            ],
        ),
        out_shape=[
            shaped(cot.shape[0], d), shaped(rows, d, dtype=F32), eighth, eighth,
            shaped(4, ff // 8, d), shaped(4, ff // 8, d),
            shaped(1, ff, dtype=F32), vec, vec, vec,
        ],
        compiler_params=params(),
        name="hidden",
    )(meta, res2, n3, cot, gains[2:3], biases[2:3], hb, win, wout)


def quad_back(q, k, v, att, g_att, probs):
    lane = lax.broadcasted_iota(jnp.int32, q.shape, 1)
    nil = jnp.zeros_like(q)
    g_t = g_att.T
    k_t = k.T
    inner = g_t.astype(F32) * att.T.astype(F32)
    dq_t, dk, dv = [], 0.0, 0.0
    for h in range(QUAD):
        part = slice(h * HDIM, (h + 1) * HDIM)
        mine = lane // HDIM == h
        delta = jnp.sum(inner[part], axis=0, keepdims=True)
        v_h = jnp.where(mine, v, nil)
        p = probs[h]
        g_scores = (p.astype(F32) * (dot_nn(v_h, g_t) - delta)).astype(BF16)
        dv = dv + dot_nn(p, jnp.where(mine, g_att, nil))
        dk = dk + dot_nn(g_scores, jnp.where(mine, q, nil))
        dq_t.append(dot_nn(k_t[part], g_scores))
    scale = HDIM**-0.5
    dq = (jnp.concatenate(dq_t, axis=0) * scale).astype(BF16).T
    return dq, (dk * scale).astype(BF16), dv.astype(BF16)


def cross_back_kernel(
    meta, grad_in, res1, n2, optic, q, k, v, att, probs, gain, wo, wq, wk, wv, att_all,
    grad_one, optic_g, keep, send, bias_g, gain_g, shift_g,
    gc, n2_t, op_t, acc,
):
    j = pl.program_id(0)
    rows, d = n2.shape
    wide = q.shape[1]

    @pl.when(j == 0)
    def _():
        low = grad_in[...].astype(BF16)
        gc[...] = low
        bias_g[...] = jnp.sum(low.astype(F32), axis=0, keepdims=True)
        n2_t[...] = n2[...].T
        op_t[...] = optic[...].T
        acc[...] = jnp.zeros_like(acc)
        optic_g[...] = jnp.zeros_like(optic_g)
        place(meta, keep, send, dot_nn(att_all[...].T, low).astype(BF16), slice(0, d))

    g_att = dot_nt(gc[...], wo[...]).astype(BF16)
    dq, dk, dv = quad_back(q[...], k[...], v[...], att[...], g_att, probs)

    def put(grad, first):
        spot = pl.ds(pl.multiple_of(first * d + j * wide, wide), wide)
        place(meta, keep, send, grad.astype(BF16), spot)

    put(dot_nn(n2_t[...], dq), 1)
    put(dot_nn(op_t[...], dk), 2)
    put(dot_nn(op_t[...], dv), 3)
    optic_g[0:rows] += dot_nt(dk, wk[...]) + dot_nt(dv, wv[...])
    acc[...] += dot_nt(dq, wq[...])

    @pl.when(j == pl.num_programs(0) - 1)
    def _():
        part, g_gain, g_shift = norm_back(res1[...], gain[...], acc[...])
        grad_one[...] = grad_in[...] + part
        gain_g[...] = g_gain
        shift_g[...] = g_shift


def cross_back(rows, meta, grad_in, res1, n2, optic, q, k, v, att, probs, gains, wo, wq, wkv):
    d = n2.shape[1]
    wide = QUAD * HDIM
    steps = d // wide
    vec = shaped(1, d, dtype=F32)
    eighth = (4, d // 8, 4 * d)
    return pl.pallas_call(
        cross_back_kernel,
        grid=(steps,),
        in_specs=[
            smem(), whole((rows, d)), whole((rows, d)), whole((rows, d)), whole((rows, d)),
            *[cols(rows, wide)] * 4,
            pl.BlockSpec((QUAD, rows, rows), lambda j: (j, 0, 0)),
            whole((1, d)), rowblk(wide, d), cols(d, wide), cols(d, wide), cols(d, wide, steps),
            whole((rows, d)),
        ],
        out_specs=[
            whole((rows, d)), whole((optic.shape[0], d)), whole(eighth), whole(eighth),
            whole((1, d)), whole((1, d)), whole((1, d)),
        ],
        out_shape=[
            shaped(rows, d, dtype=F32), shaped(optic.shape[0], d, dtype=F32),
            shaped(*eighth), shaped(*eighth), vec, vec, vec,
        ],
        scratch_shapes=[
            pltpu.VMEM((rows, d), BF16), pltpu.VMEM((d, rows), BF16),
            pltpu.VMEM((d, rows), BF16), pltpu.VMEM((rows, d), F32),
        ],
        compiler_params=params(),
        name="cross_back",
    )(meta, grad_in, res1, n2, optic, q, k, v, att, probs, gains[1:2], wo, wq, wkv, wkv, att)


def self_back_kernel(
    meta, grad_in, radar, n1, q, k, v, att, probs, gain, wo, wq, wk, wv, att_all,
    radar_g, keep, send, bias_g, gain_g, shift_g,
    gs, n1_t, acc,
):
    j = pl.program_id(0)
    rows, d = n1.shape
    wide = q.shape[1]

    @pl.when(j == 0)
    def _():
        low = grad_in[...].astype(BF16)
        gs[...] = low
        bias_g[...] = jnp.sum(low.astype(F32), axis=0, keepdims=True)
        n1_t[...] = n1[...].T
        acc[...] = jnp.zeros_like(acc)
        place(meta, keep, send, dot_nn(att_all[...].T, low).astype(BF16), slice(0, d))

    g_att = dot_nt(gs[...], wo[...]).astype(BF16)
    dq, dk, dv = quad_back(q[...], k[...], v[...], att[...], g_att, probs)

    def put(grad, first):
        spot = pl.ds(pl.multiple_of(first * d + j * wide, wide), wide)
        place(meta, keep, send, grad.astype(BF16), spot)

    put(dot_nn(n1_t[...], dq), 1)
    put(dot_nn(n1_t[...], dk), 2)
    put(dot_nn(n1_t[...], dv), 3)
    acc[...] += dot_nt(dq, wq[...]) + dot_nt(dk, wk[...]) + dot_nt(dv, wv[...])

    @pl.when(j == pl.num_programs(0) - 1)
    def _():
        part, g_gain, g_shift = norm_back(radar[...].astype(F32), gain[...], acc[...])
        radar_g[0:rows] = grad_in[...] + part
        if radar_g.shape[0] > rows:
            radar_g[rows:] = jnp.zeros((radar_g.shape[0] - rows, radar_g.shape[1]), F32)
        gain_g[...] = g_gain
        shift_g[...] = g_shift


def self_back(rows, meta, grad_in, radar, n1, q, k, v, att, probs, gains, wo, w_qkv):
    d = n1.shape[1]
    wide = QUAD * HDIM
    steps = d // wide
    vec = shaped(1, d, dtype=F32)
    eighth = (4, d // 8, 4 * d)
    return pl.pallas_call(
        self_back_kernel,
        grid=(steps,),
        in_specs=[
            smem(), whole((rows, d)), whole((rows, d)), whole((rows, d)),
            *[cols(rows, wide)] * 4,
            pl.BlockSpec((QUAD, rows, rows), lambda j: (j, 0, 0)),
            whole((1, d)), rowblk(wide, d),
            cols(d, wide), cols(d, wide, steps), cols(d, wide, 2 * steps), whole((rows, d)),
        ],
        out_specs=[
            whole((radar.shape[0], d)), whole(eighth), whole(eighth),
            whole((1, d)), whole((1, d)), whole((1, d)),
        ],
        out_shape=[
            shaped(radar.shape[0], d, dtype=F32), shaped(*eighth), shaped(*eighth), vec, vec, vec,
        ],
        scratch_shapes=[
            pltpu.VMEM((rows, d), BF16), pltpu.VMEM((d, rows), BF16), pltpu.VMEM((rows, d), F32),
        ],
        compiler_params=params(),
        name="self_back",
    )(meta, grad_in, radar, n1, q, k, v, att, probs, gains[0:1], wo, w_qkv, w_qkv, w_qkv, att)


def local_grads(
    meta, radar_tokens, optic_tokens, norm_gains, norm_shifts, self_qkv, self_out, cross_query,
    cross_keyval, cross_out, hidden_in, hidden_out, proj_biases, hidden_bias, cotangent,
):
    rows = rows_in_use(radar_tokens.shape[0], 3)
    slopes = jnp.asarray([2.0 ** (-8.0 * (h + 1) / HEADS) for h in range(HEADS)], F32)
    n1, q1, k1, v1, p1, att1, res1, n2 = self_forward(
        rows, meta, slopes, radar_tokens, norm_gains, norm_shifts, proj_biases, self_qkv, self_out
    )
    q2, k2, v2, p2, att2, res2, n3 = cross_forward(
        rows, meta, res1, n2, optic_tokens, norm_gains, norm_shifts, proj_biases,
        cross_query, cross_keyval, cross_out,
    )
    y, grad_two, dwin, dwin_s, dwout, dwout_s, dhb, gain3, shift3, bias3 = hidden(
        rows, meta, res2, n3, cotangent, norm_gains, proj_biases, hidden_bias[None], hidden_in,
        hidden_out,
    )
    grad_one, optic_g, cross, cross_s, bias2, gain2, shift2 = cross_back(
        rows, meta, grad_two, res1, n2, optic_tokens, q2, k2, v2, att2, p2, norm_gains,
        cross_out, cross_query, cross_keyval,
    )
    radar_g, own, own_s, bias1, gain1, shift1 = self_back(
        rows, meta, grad_one, radar_tokens, n1, q1, k1, v1, att1, p1, norm_gains, self_out, self_qkv
    )
    small = jnp.concatenate(
        [gain1, gain2, gain3, shift1, shift2, shift3, bias1, bias2, bias3, dhb.reshape(4, -1)]
    )
    big = ((dwin, dwin_s), (dwout, dwout_s), (cross, cross_s), (own, own_s))
    return y, radar_g, optic_g, big, small


def hop(values, perm):
    return lax.ppermute(values, ("grp", "hd"), perm)


def pairs(move):
    found = []
    for z in range(4):
        for x in range(2):
            for y in range(2):
                for c in range(2):
                    to = move(z, x, y, c)
                    if to is not None:
                        tz, tx, ty, tc = to
                        found.append(((z * 2 + x) * 4 + y * 2 + c, (tz * 2 + tx) * 4 + ty * 2 + tc))
    return found


ACROSS_CORE = pairs(lambda z, x, y, c: (z, x, y, 1 - c))
ACROSS_Y = pairs(lambda z, x, y, c: (z, x, 1 - y, c))
ACROSS_X = pairs(lambda z, x, y, c: (z, 1 - x, y, c))
INWARD = pairs(lambda z, x, y, c: {0: (1, x, y, c), 3: (2, x, y, c)}.get(z))
MIDDLE = pairs(lambda z, x, y, c: {1: (2, x, y, c), 2: (1, x, y, c)}.get(z))
OUTWARD = pairs(lambda z, x, y, c: {1: (0, x, y, c), 2: (3, x, y, c)}.get(z))


def add(*terms):
    total = terms[0].astype(F32)
    for term in terms[1:]:
        total = total + term.astype(F32)
    return total


def reduce_part(keep, send, at_x, at_edge):
    from_core = hop(send, ACROSS_CORE)
    to_y = add(keep[2:], from_core[2:]).astype(BF16)
    from_y = hop(to_y, ACROSS_Y)
    both = add(keep[:2], from_core[:2], from_y).astype(BF16)
    from_x = hop(both[1], ACROSS_X)
    mine = add(both[0], from_x).astype(BF16)
    inward = hop(mine, INWARD)
    inner = add(mine, inward).astype(BF16)
    crossed = hop(inner, MIDDLE)
    done = add(inner, crossed).astype(BF16)
    outward = hop(done, OUTWARD)
    done = jnp.where(at_edge, outward, done)
    other = hop(done, ACROSS_X)
    first = jnp.where(at_x == 0, done, other)
    second = jnp.where(at_x == 0, other, done)
    return jnp.concatenate([first, second], axis=0).astype(F32)


def reduce_anywhere(keep, send):
    parts = jnp.stack([keep.reshape(2, 2, *keep.shape[1:]), send.reshape(2, 2, *send.shape[1:])], axis=1)
    grad = parts.reshape(-1, keep.shape[-1])
    mine = lax.psum_scatter(grad, "hd", scatter_dimension=0, tiled=True)
    return lax.psum(mine.astype(F32), "grp")


def on_device(
    radar_tokens, optic_tokens, tile_lengths, norm_gains, norm_shifts, self_qkv, self_out,
    cross_query, cross_keyval, cross_out, hidden_in, hidden_out, proj_biases, hidden_bias, cotangent,
):
    d = radar_tokens.shape[1]
    known = lax.axis_size("grp") == 8 and lax.axis_size("hd") == 4
    at_hd = lax.axis_index("hd")
    at_grp = lax.axis_index("grp")
    lens = lax.dynamic_index_in_dim(tile_lengths[0], at_hd, 0, keepdims=False)
    if known:
        at_z, at_x = at_grp // 2, at_grp % 2
        at_edge = jnp.logical_or(at_z == 0, at_z == 3)
        spot = jnp.stack([at_hd // 2, at_hd % 2, at_x]).astype(jnp.int32)
    else:
        spot = jnp.zeros((3,), jnp.int32)
    meta = jnp.concatenate([lens, spot])
    layer_output, radar_grad, optic_grad, big, small = local_grads(
        meta, radar_tokens, optic_tokens, norm_gains, norm_shifts, self_qkv, self_out, cross_query,
        cross_keyval, cross_out, hidden_in, hidden_out, proj_biases, hidden_bias, cotangent,
    )
    if known:
        sums = [reduce_part(keep, send, at_x, at_edge) for keep, send in big]
    else:
        sums = [reduce_anywhere(keep, send) for keep, send in big]
    into, out, cross, own = sums
    small = lax.psum(small, ("grp", "hd"))
    vectors = lax.dynamic_slice_in_dim(small[:9], at_hd * (d // 4), d // 4, 1)
    hidden_part = lax.dynamic_index_in_dim(small[9:], at_hd, 0, keepdims=False)
    return (
        layer_output,
        radar_grad,
        optic_grad,
        own[:, d:],
        own[:, :d],
        cross[:, d : 2 * d],
        cross[:, 2 * d :],
        cross[:, :d],
        into,
        out,
        vectors[0:3],
        vectors[3:6],
        vectors[6:9],
        hidden_part,
    )


def solution(mesh):
    rows = P(("grp", "hd"), None)
    kept = P("hd", None)
    vector = P(None, "hd")
    return jax.shard_map(
        on_device,
        mesh=mesh,
        in_specs=(rows, rows, P("grp", None, None), *[P()] * 11, rows),
        out_specs=(rows, rows, rows, *[kept] * 7, vector, vector, vector, P("hd")),
        check_vma=False,
    )
```

```python
import functools
import math

import jax
import jax.numpy as jnp
import numpy as np
from jax import lax
from jax.experimental import pallas as pl
from jax.experimental.pallas import tpu as pltpu
from jax.sharding import PartitionSpec as P

HEADS = 12
HDIM = 64
SIDES = (12, 15, 20)
QUAD = 4
EPSILON = 1e-06
MASKED = -1e30
FAR = 1e33
F32 = jnp.float32
BF16 = jnp.bfloat16
VMEM_LIMIT = 24 * 1024 * 1024


def rows_in_use(local_rows, slots):
    counts = [0] + [side * side for side in SIDES]
    sums = {0}
    for _ in range(slots):
        sums = {a + b for a in sums for b in counts if a + b <= local_rows}
    return min(local_rows, -(-max(sums) // 16) * 16)


def dot_nn(left, right):
    return lax.dot_general(left, right, (((1,), (0,)), ((), ())), preferred_element_type=F32)


def dot_nt(left, right):
    return lax.dot_general(left, right, (((1,), (1,)), ((), ())), preferred_element_type=F32)


def norm_parts(values):
    average = jnp.mean(values, axis=-1, keepdims=True)
    centred = values - average
    variance = jnp.mean(centred * centred, axis=-1, keepdims=True)
    return centred, lax.rsqrt(variance + EPSILON)


def norm(values, gain, shift):
    centred, inverse = norm_parts(values)
    return centred * inverse * gain + shift


def norm_back(values, gain, grad):
    centred, inverse = norm_parts(values)
    unit = centred * inverse
    gain_grad = jnp.sum(grad * unit, axis=0, keepdims=True)
    shift_grad = jnp.sum(grad, axis=0, keepdims=True)
    scaled = grad * gain
    lift = jnp.mean(scaled, axis=-1, keepdims=True)
    tilt = jnp.mean(scaled * unit, axis=-1, keepdims=True)
    return inverse * (scaled - lift - unit * tilt), gain_grad, shift_grad


def own_counts(lens_ref):
    block = lax.axis_index("hd")
    return [lens_ref[0, block, i] for i in range(3)]


def layout_of(lens_ref, shape, dim):
    place = lax.broadcasted_iota(jnp.int32, shape, dim)
    count = own_counts(lens_ref)
    ends = [count[0], count[0] + count[1], count[0] + count[1] + count[2]]
    zero = jnp.zeros(shape, jnp.int32)
    segment = zero
    for end in ends:
        segment = segment + jnp.where(place >= end, 1, 0)
    sides = [
        jnp.where(c == SIDES[0] ** 2, SIDES[0], jnp.where(c == SIDES[1] ** 2, SIDES[1], SIDES[2]))
        for c in count
    ]
    start = jnp.where(segment == 0, 0, jnp.where(segment == 1, ends[0], ends[1]))
    side = jnp.where(segment == 0, sides[0], jnp.where(segment == 1, sides[1], sides[2])).astype(F32)
    offset = (place - start).astype(F32)
    row = jnp.floor((offset + 0.5) / side)
    col = offset - row * side
    valid = segment < 3
    return segment, jnp.where(valid, row, 0.0), jnp.where(valid, col, 0.0), valid


def gelu_parts(values):
    bell = jnp.exp(values * values * -0.5)
    size = jnp.abs(values) * math.sqrt(0.5)
    t = 1.0 / (1.0 + 0.3275911 * size)
    poly = t * (
        0.254829592
        + t * (-0.284496736 + t * (1.421413741 + t * (-1.453152027 + t * 1.061405429)))
    )
    tail = 0.5 * poly * bell
    below = jnp.where(values < 0, tail, 1.0 - tail)
    return values * below, below + values * bell * (1.0 / math.sqrt(2.0 * math.pi))


def whole(shape):
    return pl.BlockSpec(shape, lambda *_: (0,) * len(shape))


def smem():
    return pl.BlockSpec(memory_space=pltpu.SMEM)


def cols(rows, width, first=0):
    return pl.BlockSpec((rows, width), lambda j, *_: (0, first + j))


def rowblk(height, width, first=0):
    return pl.BlockSpec((height, width), lambda j, *_: (first + j, 0))


def cost(flops, moved):
    return pl.CostEstimate(flops=1, bytes_accessed=1, transcendentals=0)


def params(**kw):
    return pltpu.CompilerParams(vmem_limit_bytes=VMEM_LIMIT, dimension_semantics=("arbitrary",), **kw)


def attend_quad(q, k, v, add_bias, probs_ref):
    lane = lax.broadcasted_iota(jnp.int32, q.shape, 1)
    scaled = q * jnp.asarray(HDIM**-0.5, BF16)
    v_t = v.T
    outs = []
    for h in range(QUAD):
        q_h = jnp.where(lane // HDIM == h, scaled, jnp.zeros_like(scaled))
        scores = add_bias(dot_nt(k, q_h), h)
        top = jnp.max(scores, axis=0, keepdims=True)
        weights = jnp.exp(scores - top)
        total = jnp.sum(weights, axis=0, keepdims=True)
        probs = (weights * (1.0 / total)).astype(BF16)
        probs_ref[h] = probs
        outs.append(dot_nn(v_t[h * HDIM : (h + 1) * HDIM], probs))
    return jnp.concatenate(outs, axis=0).astype(BF16).T


def self_forward_kernel(
    lens, slopes, radar, cot, gains, shifts, biases, wq, wk, wv, wo,
    n1, q_out, k_out, v_out, probs, att_out, resid, n2, gf, dist,
):
    j = pl.program_id(0)
    rows = n1.shape[0]

    @pl.when(j == 0)
    def _():
        wide = radar[...].astype(F32)
        n1[...] = norm(wide, gains[0:1], shifts[0:1]).astype(BF16)
        resid[...] = wide + biases[0:1]
        seg_k, row_k, col_k, valid = layout_of(lens, (rows, 1), 0)
        gf[...] = jnp.where(valid, cot[...], jnp.zeros_like(cot))
        seg_q, row_q, col_q, _ = layout_of(lens, (1, rows), 1)
        dr = row_k - row_q
        dc = col_k - col_q
        dist[...] = jnp.where(seg_k == seg_q, jnp.sqrt(dr * dr + dc * dc), FAR)

    x = n1[...]
    q = dot_nn(x, wq[...]).astype(BF16)
    k = dot_nn(x, wk[...]).astype(BF16)
    v = dot_nn(x, wv[...]).astype(BF16)
    q_out[...] = q
    k_out[...] = k
    v_out[...] = v
    att = attend_quad(
        q, k, v, lambda s, h: s - slopes[j * QUAD + h] * dist[...], probs
    )
    att_out[...] = att
    resid[...] += dot_nn(att, wo[...])

    @pl.when(j == pl.num_programs(0) - 1)
    def _():
        n2[...] = norm(resid[...], gains[1:2], shifts[1:2]).astype(BF16)


def cross_forward_kernel(
    lens, res_in, n_in, optic, gains, shifts, biases, wq, wk, wv, wo,
    q_out, k_out, v_out, probs, att_out, resid, n3, mask,
):
    j = pl.program_id(0)
    rows = n_in.shape[0]

    @pl.when(j == 0)
    def _():
        resid[...] = res_in[...] + biases[1:2]
        seg_k = layout_of(lens, (rows, 1), 0)[0]
        seg_q = layout_of(lens, (1, rows), 1)[0]
        mask[...] = jnp.where(seg_k == seg_q, 0.0, MASKED)

    q = dot_nn(n_in[...], wq[...]).astype(BF16)
    k = dot_nn(optic[...], wk[...]).astype(BF16)
    v = dot_nn(optic[...], wv[...]).astype(BF16)
    q_out[...] = q
    k_out[...] = k
    v_out[...] = v
    att = attend_quad(q, k, v, lambda s, h: s + mask[...], probs)
    att_out[...] = att
    resid[...] += dot_nn(att, wo[...])

    @pl.when(j == pl.num_programs(0) - 1)
    def _():
        n3[...] = norm(resid[...], gains[2:3], shifts[2:3]).astype(BF16)


def shaped(*shape, dtype=BF16):
    return jax.ShapeDtypeStruct(shape, dtype)


def held(*shape, dtype=BF16):
    return pltpu.HBM(shape, dtype)


def far(*arrays):
    return [pltpu.with_memory_space_constraint(a, pltpu.HBM) for a in arrays]


def self_forward(rows, lens, slopes, radar, cot, gains, shifts, biases, w_qkv, w_out):
    d = radar.shape[1]
    wide = QUAD * HDIM
    steps = d // wide
    return pl.pallas_call(
        self_forward_kernel,
        grid=(steps,),
        in_specs=[
            smem(), smem(), whole((rows, d)), whole((rows, d)),
            *[whole((3, d))] * 3,
            cols(d, wide), cols(d, wide, steps), cols(d, wide, 2 * steps), rowblk(wide, d),
        ],
        out_specs=[
            whole((rows, d)), cols(rows, wide), cols(rows, wide), cols(rows, wide),
            pl.BlockSpec((QUAD, rows, rows), lambda j: (j, 0, 0)),
            cols(rows, wide), whole((rows, d)), whole((rows, d)), whole((rows, d)),
        ],
        out_shape=[
            held(rows, d), held(rows, d), held(rows, d), held(rows, d),
            held(HEADS, rows, rows), held(rows, d), shaped(rows, d, dtype=F32), shaped(rows, d), held(rows, d),
        ],
        scratch_shapes=[pltpu.VMEM((rows, rows), F32)],
        compiler_params=params(),
        cost_estimate=cost(8 * rows * d * d + 12 * HEADS * rows * rows * 128, 8 * d * d + HEADS * rows * rows * 2),
        name="self_forward",
    )(lens, slopes, *far(radar, cot, gains, shifts, biases),
      *far(w_qkv, w_qkv, w_qkv, w_out))


def cross_forward(rows, lens, res_in, n_in, optic, gains, shifts, biases, w_q, w_kv, w_out):
    d = optic.shape[1]
    wide = QUAD * HDIM
    steps = d // wide
    return pl.pallas_call(
        cross_forward_kernel,
        grid=(steps,),
        in_specs=[
            smem(), whole((rows, d)), whole((rows, d)), whole((rows, d)),
            *[whole((3, d))] * 3,
            cols(d, wide), cols(d, wide), cols(d, wide, steps), rowblk(wide, d),
        ],
        out_specs=[
            cols(rows, wide), cols(rows, wide), cols(rows, wide),
            pl.BlockSpec((QUAD, rows, rows), lambda j: (j, 0, 0)),
            cols(rows, wide), whole((rows, d)), whole((rows, d)),
        ],
        out_shape=[
            held(rows, d), held(rows, d), held(rows, d),
            held(HEADS, rows, rows), held(rows, d), shaped(rows, d, dtype=F32), shaped(rows, d),
        ],
        scratch_shapes=[pltpu.VMEM((rows, rows), F32)],
        compiler_params=params(),
        cost_estimate=cost(8 * rows * d * d + 12 * HEADS * rows * rows * 128, 8 * d * d + HEADS * rows * rows * 2),
        name="cross_forward",
    )(lens, res_in, n_in, *far(optic, gains, shifts, biases),
      *far(w_q, w_kv, w_kv, w_out))


def hidden_kernel(res2, n3, gf, gains, hb, win, wout, act_out, grad_two, vectors, acc):
    j = pl.program_id(0)

    @pl.when(j == 0)
    def _():
        acc[...] = jnp.zeros_like(acc)

    act, slope = gelu_parts(dot_nn(n3[...], win[...]) + hb[...])
    act_out[...] = act.astype(BF16)
    g_pre = (dot_nt(gf[...], wout[...]) * slope).astype(BF16)
    acc[...] += dot_nt(g_pre, win[...])
    vectors[pl.ds(j, 1)] = jnp.sum(g_pre.astype(F32), axis=0, keepdims=True)

    @pl.when(j == pl.num_programs(0) - 1)
    def _():
        part, g_gain, g_shift = norm_back(res2[...], gains[2:3], acc[...])
        wide = gf[...].astype(F32)
        grad_two[...] = wide + part
        vectors[4:5] = g_gain
        vectors[5:6] = g_shift
        vectors[6:7] = jnp.sum(wide, axis=0, keepdims=True)
        vectors[7:8] = jnp.zeros_like(g_gain)


def hidden(rows, res2, n3, gf, gains, hb, win, wout):
    d = n3.shape[1]
    ff = win.shape[1]
    chunk = ff // 4
    return pl.pallas_call(
        hidden_kernel,
        grid=(4,),
        in_specs=[
            whole((rows, d)), whole((rows, d)), whole((rows, d)),
            whole((3, d)), cols(1, chunk), cols(d, chunk), rowblk(chunk, d),
        ],
        out_specs=[cols(rows, chunk), whole((rows, d)), whole((8, d))],
        out_shape=[held(rows, ff), shaped(rows, d, dtype=F32), shaped(8, d, dtype=F32)],
        scratch_shapes=[pltpu.VMEM((rows, d), F32)],
        compiler_params=params(),
        cost_estimate=cost(6 * rows * d * ff, 4 * d * ff),
        name="hidden",
    )(*far(res2, n3, gf, gains, hb, win, wout))


def output_kernel(lens, act, res2, biases, wout, y_out, acc):
    j = pl.program_id(0)
    rows = act.shape[0]

    @pl.when(j == 0)
    def _():
        acc[...] = res2[...] + biases[2:3]

    acc[...] += dot_nn(act[...], wout[...])

    @pl.when(j == pl.num_programs(0) - 1)
    def _():
        valid = layout_of(lens, (rows, 1), 0)[3]
        y_out[0:rows] = jnp.where(valid, acc[...], 0.0).astype(BF16)
        if y_out.shape[0] > rows:
            y_out[rows:] = jnp.zeros((y_out.shape[0] - rows, y_out.shape[1]), BF16)


def output(rows, local_rows, lens, act, res2, biases, wout):
    ff, d = wout.shape
    chunk = ff // 2
    return pl.pallas_call(
        output_kernel,
        grid=(2,),
        in_specs=[smem(), cols(rows, chunk), whole((rows, d)), whole((3, d)), rowblk(chunk, d)],
        out_specs=whole((local_rows, d)),
        out_shape=held(local_rows, d),
        scratch_shapes=[pltpu.VMEM((rows, d), F32)],
        compiler_params=params(),
        cost_estimate=cost(2 * rows * d * ff, 2 * d * ff),
        name="output",
    )(lens, *far(act, res2, biases, wout))


def hidden_grads_kernel(blocks, meta, *refs):
    normed, grads = refs[:blocks], refs[blocks : 2 * blocks]
    hb_a, hb_b, win_a, win_b, wout_a, wout_b, dwin, dwout, acc_in, acc_out = refs[2 * blocks :]
    win = jnp.concatenate([win_a[...], win_b[...]], axis=1)
    wout = jnp.concatenate([wout_a[...], wout_b[...]], axis=0)
    hb = jnp.concatenate([hb_a[...], hb_b[...]], axis=1)
    for i in range(blocks):
        act, slope = gelu_parts(dot_nn(normed[i][...], win) + hb)
        g_pre = (dot_nt(grads[i][...], wout) * slope).astype(BF16)
        into = dot_nn(normed[i][...].T, g_pre)
        out = dot_nn(act.astype(BF16).T, grads[i][...])
        if i == 0:
            acc_in[...] = into
            acc_out[...] = out
        else:
            acc_in[...] += into
            acc_out[...] += out
    at_y, at_c, at_p = meta[0], meta[1], meta[3]
    piece = dwout.shape[2]
    for y in range(2):
        for p in range(2):
            at = (y * 2 + p) * piece
            dwout[y ^ at_y, p ^ at_p] = acc_out[at : at + piece].astype(BF16)
    piece = dwin.shape[3]
    for y in range(2):
        for c in range(2):
            for p in range(2):
                at = ((y * 2 + c) * 2 + p) * piece
                dwin[y ^ at_y, c ^ at_c, p ^ at_p] = acc_in[at : at + piece].astype(BF16)


def hidden_grads(rows, meta, normed, grads, hb, win, wout):
    d, ff = win.shape
    part = ff // 8
    blocks = len(normed)

    def wide(height, y):
        return pl.BlockSpec((height, part), lambda i, m: (0, y * 4 + m[1] * 2 + m[2]))

    def tall(y):
        return pl.BlockSpec((part, d), lambda i, m: (y * 4 + m[1] * 2 + m[2], 0))

    return pl.pallas_call(
        functools.partial(hidden_grads_kernel, blocks),
        grid_spec=pltpu.PrefetchScalarGridSpec(
            num_scalar_prefetch=1,
            grid=(1,),
            in_specs=[
                *[whole((rows, d))] * (2 * blocks),
                wide(1, 0), wide(1, 1), wide(d, 0), wide(d, 1), tall(0), tall(1),
            ],
            out_specs=[whole((2, 2, 2, d // 8, 2 * part)), whole((2, 2, part // 2, d))],
            scratch_shapes=[pltpu.VMEM((d, 2 * part), F32), pltpu.VMEM((2 * part, d), F32)],
        ),
        out_shape=[shaped(2, 2, 2, d // 8, 2 * part), shaped(2, 2, part // 2, d)],
        compiler_params=params(),
        cost_estimate=cost(16 * blocks * rows * d * part, 4 * blocks * rows * d + 4 * d * ff),
        name="hidden_grads",
    )(meta, *far(*normed, *grads, hb, hb, win, win, wout, wout))


def place(keep, send, bucket, grad, spot):
    at_hd, at_grp = lax.axis_index("hd"), lax.axis_index("grp")
    at_y, first = at_hd // 2, lax.rem(at_hd, 2) == 0
    at_x, at_p = lax.rem(at_grp, 2), lax.rem(at_grp // 2, 2)
    part = grad.shape[0] // 16
    for y in range(2):
        for x in range(2):
            for p in range(2):
                at = y * 8 + x * 2 + p
                low = grad[at * part : (at + 1) * part]
                high = grad[(at + 4) * part : (at + 5) * part]
                lead, other = (x ^ at_x, y ^ at_y) if bucket == 0 else (y ^ at_y, x ^ at_x)
                to = (bucket, lead, other, p ^ at_p, slice(None), spot)
                keep[to] = jnp.where(first, low, high)
                send[to] = jnp.where(first, high, low)


def quad_back(q, k, v, att, g_att, probs):
    lane = lax.broadcasted_iota(jnp.int32, q.shape, 1)
    nil = jnp.zeros_like(q)
    g_t = g_att.T
    k_t = k.T
    inner = g_t.astype(F32) * att.T.astype(F32)
    dq_t, dk, dv = [], 0.0, 0.0
    for h in range(QUAD):
        part = slice(h * HDIM, (h + 1) * HDIM)
        mine = lane // HDIM == h
        delta = jnp.sum(inner[part], axis=0, keepdims=True)
        v_h = jnp.where(mine, v, nil)
        p = probs[h]
        g_scores = (p.astype(F32) * (dot_nn(v_h, g_t) - delta)).astype(BF16)
        dv = dv + dot_nn(p, jnp.where(mine, g_att, nil))
        dk = dk + dot_nn(g_scores, jnp.where(mine, q, nil))
        dq_t.append(dot_nn(k_t[part], g_scores))
    scale = HDIM**-0.5
    dq = (jnp.concatenate(dq_t, axis=0) * scale).astype(BF16).T
    return dq, (dk * scale).astype(BF16), dv.astype(BF16)


def back_kernel(own_keys, grad_in, res, xq, xkv, q, k, v, att, att_all, probs, gains, wo, wq, *refs):
    refs = list(refs)
    keep, send, dk_out, dv_out, vectors = [refs.pop(0) for _ in range(5)]
    last_out = refs.pop(0)
    low, xq_t, xkv_t, acc = refs
    i = pl.program_id(0)
    d = xq.shape[1]
    wide = q.shape[1]

    @pl.when(i == 0)
    def _():
        low[...] = grad_in[...].astype(BF16)
        xq_t[...] = xq[...].T
        if not own_keys:
            xkv_t[...] = xkv[...].T
            acc[...] = jnp.zeros_like(acc)
        vectors[0:1] = jnp.sum(low[...].astype(F32), axis=0, keepdims=True)
        vectors[1:8] = jnp.zeros((7, d), F32)
        place(keep, send, 0, dot_nn(att_all[...].T, low[...]).astype(BF16), slice(0, d))

    g_att = dot_nt(low[...], wo[...]).astype(BF16)
    dq, dk, dv = quad_back(q[...], k[...], v[...], att[...], g_att, probs)
    dk_out[...] = dk
    dv_out[...] = dv
    source_t = xq_t if own_keys else xkv_t
    near = pl.ds(pl.multiple_of(i * wide, wide), wide)
    past = pl.ds(pl.multiple_of(d + i * wide, wide), wide)
    place(keep, send, 0, dot_nn(xq_t[...], dq).astype(BF16), past)
    place(keep, send, 1, dot_nn(source_t[...], dk).astype(BF16), near)
    place(keep, send, 1, dot_nn(source_t[...], dv).astype(BF16), past)
    if own_keys:
        last_out[...] = dq
    else:
        acc[...] += dot_nt(dq, wq[...])

        @pl.when(i == pl.num_programs(0) - 1)
        def _():
            part, g_gain, g_shift = norm_back(res[...], gains[1:2], acc[...])
            last_out[...] = grad_in[...] + part
            vectors[1:2] = g_gain
            vectors[2:3] = g_shift


def back(own_keys, rows, grad_in, res, xq, xkv, q, k, v, att, probs, gains, wo, wq):
    d = xq.shape[1]
    wide = QUAD * HDIM
    halves = (2, 2, 2, 2, d // 16, 2 * d)
    at = cols(rows, wide)
    full = whole((rows, d))
    if own_keys:
        res = gains
    return pl.pallas_call(
        functools.partial(back_kernel, own_keys),
        grid=(d // wide,),
        in_specs=[
            full, whole(res.shape), full, full, at, at, at, at, full,
            pl.BlockSpec((QUAD, rows, rows), lambda i: (i, 0, 0)),
            whole((3, d)), rowblk(wide, d), cols(d, wide),
        ],
        out_specs=[*[whole(halves)] * 2, at, at, whole((8, d)), at if own_keys else full],
        out_shape=[
            *[shaped(*halves)] * 2, held(rows, d), held(rows, d), shaped(8, d, dtype=F32),
            held(rows, d) if own_keys else shaped(rows, d, dtype=F32),
        ],
        scratch_shapes=[
            pltpu.VMEM((rows, d), BF16), pltpu.VMEM((d, rows), BF16),
            pltpu.VMEM((16, 128) if own_keys else (d, rows), BF16),
            pltpu.VMEM((8, 128) if own_keys else (rows, d), F32),
        ],
        compiler_params=params(),
        cost_estimate=cost(18 * rows * d * d + 24 * HEADS * rows * rows * 128, 16 * d * d),
        name="self_back" if own_keys else "cross_back",
    )(*far(grad_in, res, xq, xkv, q, k, v, att, att, probs, gains, wo, wq))


def through(parts, weights):
    total = None
    for i, part in enumerate(parts):
        d = part.shape[1]
        term = dot_nt(part[...], weights[:, i * d : (i + 1) * d])
        total = term if total is None else total + term
    return total


def store_padded(out, values):
    rows = values.shape[0]
    out[0:rows] = values
    if out.shape[0] > rows:
        out[rows:] = jnp.zeros((out.shape[0] - rows, out.shape[1]), out.dtype)


def optic_kernel(dk, dv, weights, out):
    store_padded(out, through([dk, dv], weights))


def optic(local_rows, dk, dv, weights):
    rows, d = dk.shape
    return pl.pallas_call(
        optic_kernel,
        in_specs=[whole(dk.shape), whole(dv.shape), whole(weights.shape)],
        out_specs=whole((local_rows, d)),
        out_shape=held(local_rows, d, dtype=F32),
        grid=(1,),
        compiler_params=params(),
        cost_estimate=cost(4 * rows * d * d, 4 * d * d),
        name="optic",
    )(*far(dk, dv, weights))


def radar_kernel(dq, dk, dv, weights, grad_in, radar, gains, hidden_vec, cross_vec, self_vec, out, vectors):
    total = through([dq, dk, dv], weights)
    part, g_gain, g_shift = norm_back(radar[...].astype(F32), gains[0:1], total)
    store_padded(out, grad_in[...] + part)
    vectors[0:1] = g_gain
    vectors[1:2] = cross_vec[1:2]
    vectors[2:3] = hidden_vec[4:5]
    vectors[3:4] = g_shift
    vectors[4:5] = cross_vec[2:3]
    vectors[5:6] = hidden_vec[5:6]
    vectors[6:7] = self_vec[0:1]
    vectors[7:8] = cross_vec[0:1]
    vectors[8:9] = hidden_vec[6:7]
    vectors[9:13] = hidden_vec[0:4]
    vectors[13:16] = jnp.zeros((3, out.shape[1]), F32)


def radar(local_rows, dq, dk, dv, weights, grad_in, tokens, gains, vectors):
    rows, d = dq.shape
    full = whole((rows, d))
    return pl.pallas_call(
        radar_kernel,
        grid=(1,),
        in_specs=[full, full, full, whole(weights.shape), full, full, whole((3, d)), *[whole((8, d))] * 3],
        out_specs=[whole((local_rows, d)), whole((16, d))],
        out_shape=[held(local_rows, d, dtype=F32), shaped(16, d, dtype=F32)],
        compiler_params=params(),
        cost_estimate=cost(6 * rows * d * d, 6 * d * d),
        name="radar",
    )(*far(dq, dk, dv, weights, grad_in, tokens, gains, *vectors))
def hop(values, perm):
    return lax.ppermute(values, ("grp", "hd"), perm)


def pairs(move):
    found = []
    for z in range(4):
        for x in range(2):
            for y in range(2):
                for c in range(2):
                    to = move(z, x, y, c)
                    if to is not None:
                        tz, tx, ty, tc = to
                        found.append(((z * 2 + x) * 4 + y * 2 + c, (tz * 2 + tx) * 4 + ty * 2 + tc))
    return found


ACROSS_CORE = pairs(lambda z, x, y, c: (z, x, y, 1 - c))
ACROSS_Y = pairs(lambda z, x, y, c: (z, x, 1 - y, c))
ACROSS_X = pairs(lambda z, x, y, c: (z, 1 - x, y, c))
ACROSS_P = pairs(lambda z, x, y, c: (z ^ 1, x, y, c))
ACROSS_Q = pairs(lambda z, x, y, c: (z ^ 2, x, y, c))
ACROSS_XP = pairs(lambda z, x, y, c: (z ^ 1, 1 - x, y, c))


def add(*terms):
    total = terms[0].astype(F32)
    for term in terms[1:]:
        total = total + term.astype(F32)
    return total.astype(terms[0].dtype)


def in_order(at, own, other):
    return jnp.where(at == 0, own, other), jnp.where(at == 0, other, own)


def tie(values):
    return list(lax.optimization_barrier(tuple(values)))


MOVES = {
    "C": ACROSS_CORE, "Y": ACROSS_Y, "Z": ACROSS_Y, "X": ACROSS_X, "P": ACROSS_P, "Q": ACROSS_Q,
    "A": ACROSS_P, "G": ACROSS_X, "D": ACROSS_XP, "W": ACROSS_Y, "V": ACROSS_X,
}


class Flow:
    def __init__(self, value):
        self.value, self.ends = value, {}

    def operand(self, stage):
        return self.value[1] if stage in ("Y", "P") else self.value

    def absorb(self, stage, got):
        if stage in ("Y", "P"):
            self.value = add(self.value[0], got)
        elif stage == "Q":
            self.value = add(self.value, got)
        else:
            self.ends[stage] = got

    def together(self, at_x, at_p):
        rows = [
            in_order(at_p, self.value, self.ends["A"]),
            in_order(at_p, self.ends["G"], self.ends["D"]),
        ]
        return in_order(at_x, jnp.stack(rows[0]), jnp.stack(rows[1]))


class InFlow(Flow):
    def operand(self, stage):
        if stage in ("Y", "Z"):
            return self.value[1, 1 if stage == "Y" else 0]
        if stage == "C":
            return self.value[1]
        return self.value[:, 1] if stage == "P" else self.value

    def absorb(self, stage, got):
        if stage == "Y":
            self.other = add(self.value[0, 1], got)
        elif stage == "Z":
            self.value = [add(self.value[0, 0], got), self.other]
        elif stage == "C":
            self.value = jnp.stack([self.value[0], got])
        elif stage == "P":
            self.value = add(self.value[:, 0], got)
        else:
            super().absorb(stage, got)


class RowFlow(Flow):
    def __init__(self, keep, send):
        super().__init__(None)
        self.keep, self.send, self.parts = keep, send, None

    def operand(self, stage):
        if stage == "C":
            return self.send
        if stage in "XYWV":
            return self.parts[int(stage in "WV")][1]
        if stage == "P" and self.value is None:
            self.value = jnp.stack(self.parts)
        return self.value[:, 1] if stage == "P" else self.value

    def absorb(self, stage, got):
        if stage == "C":
            self.parts = [[add(self.keep[b, i], got[b, i]) for i in range(2)] for b in range(2)]
        elif stage in "XYWV":
            b = int(stage in "WV")
            self.parts[b] = add(self.parts[b][0], got)
        elif stage == "P":
            self.value = add(self.value[:, 0], got)
        else:
            super().absorb(stage, got)


class Vectors(Flow):
    def operand(self, stage):
        return self.value

    def absorb(self, stage, got):
        self.value = self.value + got


def whole_rows(keep, send, bucket, at):
    at_y, at_c, at_x, at_p = at
    lead_at, other_at = (at_x, at_y) if bucket == 0 else (at_y, at_x)
    parts = jnp.stack(in_order(at_c, keep[bucket], send[bucket]))
    for axis, place_at in ((1, lead_at), (2, other_at), (3, at_p)):
        own, other = [lax.index_in_dim(parts, i, axis, keepdims=False) for i in range(2)]
        parts = jnp.stack(in_order(place_at, own, other), axis=axis)
    order = (2, 0, 1, 3, 4, 5) if bucket == 0 else (1, 0, 2, 3, 4, 5)
    return parts.transpose(order).reshape(-1, parts.shape[-1])


def summed_anywhere(grad):
    mine = lax.psum_scatter(grad, "hd", scatter_dimension=0, tiled=True)
    return lax.psum(mine.astype(F32), "grp")


class Plan:
    def __init__(self):
        self.flows, self.flying = {}, {}

    def begin(self, gate, *moves):
        sent = [self.flows[m[0]].operand(m[1]) for m in moves]
        gate, *sent = tie([gate, *sent])
        for m, operand in zip(moves, sent):
            self.flying[m] = hop(operand, MOVES[m[1]])
        return gate

    def end(self, gate, *moves):
        gate, *got = tie([gate, *[self.flying.pop(m) for m in moves]])
        for m, value in zip(moves, got):
            self.flows[m[0]].absorb(m[1], value)
        return gate


def on_device(
    radar_tokens, optic_tokens, tile_lengths, norm_gains, norm_shifts, self_qkv, self_out,
    cross_query, cross_keyval, cross_out, hidden_in, hidden_out, proj_biases, hidden_bias, cotangent,
):
    local_rows, d = radar_tokens.shape
    ff = hidden_in.shape[1]
    known = lax.axis_size("grp") == 8 and lax.axis_size("hd") == 4
    at_hd = lax.axis_index("hd")
    at_grp = lax.axis_index("grp")
    at_y, at_c, at_z, at_x = at_hd // 2, at_hd % 2, at_grp // 2, at_grp % 2
    at_p = at_z % 2
    rows = rows_in_use(local_rows, tile_lengths.shape[2])
    slopes = jnp.asarray([2.0 ** (-8.0 * (h + 1) / HEADS) for h in range(HEADS)], F32)
    hb = hidden_bias[None]

    n1, q1, k1, v1, p1, att1, res1, n2, gf = self_forward(
        rows, tile_lengths, slopes, radar_tokens, cotangent, norm_gains, norm_shifts, proj_biases, self_qkv, self_out
    )
    if known:
        n2, gf = tie([n2, gf])
        gf_x = hop(gf, ACROSS_X)
        gf_c = hop(gf, ACROSS_CORE)
    q2, k2, v2, p2, att2, res2, n3 = cross_forward(
        rows, tile_lengths, res1, n2, optic_tokens, norm_gains, norm_shifts, proj_biases,
        cross_query, cross_keyval, cross_out,
    )
    if known:
        n3, gf_x, gf_c, res2 = tie([n3, gf_x, gf_c, res2])
        gf_xc = hop(gf_x, ACROSS_CORE)
        n3_x = hop(n3, ACROSS_X)
        n3_c = hop(n3, ACROSS_CORE)
    act, grad_two, hidden_vec = hidden(rows, res2, n3, gf, norm_gains, hb, hidden_in, hidden_out)

    def cross_step(grad):
        return back(
            False, rows, grad, res1, n2, optic_tokens, q2, k2, v2, att2, p2, norm_gains, cross_out, cross_query
        )

    def self_step(grad):
        return back(True, rows, grad, None, n1, n1, q1, k1, v1, att1, p1, norm_gains, self_out, self_qkv)

    def radar_step(dq, grad):
        return radar(
            local_rows, dq, dk1, dv1, self_qkv, grad, radar_tokens, norm_gains, [hidden_vec, cross_vec, self_vec]
        )

    if known:
        meta = jnp.stack([at_y, at_c, at_x, at_p]).astype(jnp.int32)
        act, n3_x, n3_c, gf_x, gf_c, gf_xc, grad_two = tie([act, n3_x, n3_c, gf_x, gf_c, gf_xc, grad_two])
        n3_xc = hop(n3_x, ACROSS_CORE)
        dwin, dwout = hidden_grads(
            rows, meta, [n3, n3_x, n3_c, n3_xc], [gf, gf_x, gf_c, gf_xc], hb, hidden_in, hidden_out
        )
        plan = Plan()
        grad_two, dwin, dwout = tie([grad_two, dwin, dwout])
        plan.flows["o"], plan.flows["n"] = Flow(dwout), InFlow(dwin)

        grad_two = plan.begin(grad_two, "oY", "nY")
        keep, send, dk2, dv2, cross_vec, grad_one = cross_step(grad_two)
        act = plan.end(tie([act, grad_one])[0], "oY", "nY")
        plan.flows["a"] = RowFlow(keep, send)

        act = plan.begin(act, "aC", "nZ", "oP")
        layer_output = output(rows, local_rows, tile_lengths, act, res2, proj_biases, hidden_out)
        grad_one = plan.end(tie([grad_one, layer_output])[0], "aC", "nZ", "oP")

        grad_one = plan.begin(grad_one, "nC", "aX", "aW", "oQ")
        keep, send, dk1, dv1, self_vec, dq1 = self_step(grad_one)
        dq1 = plan.end(dq1, "nC", "aX", "aW", "oQ")
        plan.flows["c"] = RowFlow(keep, send)

        dq1 = plan.begin(dq1, "cC", "aY", "aV", "nP")
        radar_grad, small = radar_step(dq1, grad_one)
        dk2 = plan.end(tie([dk2, radar_grad])[0], "cC", "aY", "aV", "nP")
        plan.flows["s"] = Vectors(small)

        dk2 = plan.begin(dk2, "sC", "cX", "cW", "aP", "nQ")
        optic_grad = optic(local_rows, dk2, dv2, cross_keyval)
        gate = plan.end(optic_grad, "sC", "cX", "cW", "aP", "nQ")

        for stages in (
            ("sY", "cV", "cY", "oA", "oG", "oD", "aQ"),
            ("sX", "cP", "aA", "aG", "aD"),
            ("sP", "cQ", "nA", "nG", "nD"),
            ("sQ", "cA", "cG", "cD"),
        ):
            gate = plan.end(plan.begin(gate, *stages), *stages)
        optic_grad = gate

        done = {name: plan.flows[name].together(at_x, at_p) for name in "onac"}
        out_part = jnp.stack(done["o"]).reshape(-1, d).astype(F32)
        slices = [in_order(at_c, v[:, 0], v[:, 1]) for v in done["n"]]
        half = ff // 8
        in_part = jnp.concatenate(
            [
                slices[x][c][..., y * half : (y + 1) * half].reshape(-1, half)
                for y in range(2) for c in range(2) for x in range(2)
            ],
            axis=1,
        ).astype(F32)
        (cross_a, cross_b), (self_a, self_b) = [
            [jnp.stack([v[:, i] for v in done[name]]).reshape(-1, 2 * d).astype(F32) for i in range(2)] for name in "ac"
        ]
        small = plan.flows["s"].value
    else:
        into, out = [], []
        for c in range(2):
            for x in range(2):
                at = jnp.asarray([0, c, x, 0], jnp.int32)
                dwin, dwout = hidden_grads(rows, at, [n3], [gf], hb, hidden_in, hidden_out)
                into.append(jnp.stack([dwin[:, c], dwin[:, 1 - c]], axis=1).reshape(d, 2, ff // 8))
                out.append(dwout.reshape(2, ff // 8, d))
        in_part = summed_anywhere(jnp.stack(into, axis=2).reshape(d, ff))
        out_part = summed_anywhere(jnp.stack(out, axis=1).reshape(ff, d))
        cross_keep, cross_send, dk2, dv2, cross_vec, grad_one = cross_step(grad_two)
        self_keep, self_send, dk1, dv1, self_vec, dq1 = self_step(grad_one)
        radar_grad, small = radar_step(dq1, grad_one)
        optic_grad = optic(local_rows, dk2, dv2, cross_keyval)
        layer_output = output(rows, local_rows, tile_lengths, act, res2, proj_biases, hidden_out)
        at = (at_y, at_c, at_x, at_p)
        cross_a, cross_b = [summed_anywhere(whole_rows(cross_keep, cross_send, b, at)) for b in range(2)]
        self_a, self_b = [summed_anywhere(whole_rows(self_keep, self_send, b, at)) for b in range(2)]
        small = lax.psum(small, ("grp", "hd"))
    vectors = lax.dynamic_slice_in_dim(small[:9], at_hd * (d // 4), d // 4, 1)
    hidden_part = lax.dynamic_index_in_dim(small[9:13], at_hd, 0, keepdims=False)
    return (
        layer_output,
        radar_grad,
        optic_grad,
        jnp.concatenate([self_a[:, d:], self_b], axis=1),
        self_a[:, :d],
        cross_a[:, d:],
        cross_b,
        cross_a[:, :d],
        in_part,
        out_part,
        vectors[0:3],
        vectors[3:6],
        vectors[6:9],
        hidden_part,
    )


def solution(mesh):
    rows = P(("grp", "hd"), None)
    kept = P("hd", None)
    vector = P(None, "hd")
    return jax.shard_map(
        on_device,
        mesh=mesh,
        in_specs=(rows, rows, P("grp", None, None), *[P()] * 11, rows),
        out_specs=(rows, rows, rows, *[kept] * 7, vector, vector, vector, P("hd")),
        check_vma=False,
    )
```

```python
import functools
import math

import jax
import jax.numpy as jnp
import numpy as np
from jax import lax
from jax.experimental import pallas as pl
from jax.experimental.pallas import tpu as pltpu
from jax.sharding import PartitionSpec as P

HEADS = 12
HDIM = 64
SIDES = (12, 15, 20)
QUAD = 4
EPSILON = 1e-06
MASKED = -1e30
FAR = 1e33
F32 = jnp.float32
BF16 = jnp.bfloat16
VMEM_LIMIT = 24 * 1024 * 1024


def rows_in_use(local_rows, slots):
    counts = [0] + [side * side for side in SIDES]
    sums = {0}
    for _ in range(slots):
        sums = {a + b for a in sums for b in counts if a + b <= local_rows}
    return min(local_rows, -(-max(sums) // 16) * 16)


def dot_nn(left, right):
    return lax.dot_general(left, right, (((1,), (0,)), ((), ())), preferred_element_type=F32)


def dot_nt(left, right):
    return lax.dot_general(left, right, (((1,), (1,)), ((), ())), preferred_element_type=F32)


def norm_parts(values):
    average = jnp.mean(values, axis=-1, keepdims=True)
    centred = values - average
    variance = jnp.mean(centred * centred, axis=-1, keepdims=True)
    return centred, lax.rsqrt(variance + EPSILON)


def norm(values, gain, shift):
    centred, inverse = norm_parts(values)
    return centred * inverse * gain + shift


def norm_back(values, gain, grad):
    centred, inverse = norm_parts(values)
    unit = centred * inverse
    gain_grad = jnp.sum(grad * unit, axis=0, keepdims=True)
    shift_grad = jnp.sum(grad, axis=0, keepdims=True)
    scaled = grad * gain
    lift = jnp.mean(scaled, axis=-1, keepdims=True)
    tilt = jnp.mean(scaled * unit, axis=-1, keepdims=True)
    return inverse * (scaled - lift - unit * tilt), gain_grad, shift_grad


def own_counts(lens_ref):
    block = lax.axis_index("hd")
    return [lens_ref[0, block, i] for i in range(3)]


def layout_of(lens_ref, shape, dim):
    place = lax.broadcasted_iota(jnp.int32, shape, dim)
    count = own_counts(lens_ref)
    ends = [count[0], count[0] + count[1], count[0] + count[1] + count[2]]
    zero = jnp.zeros(shape, jnp.int32)
    segment = zero
    for end in ends:
        segment = segment + jnp.where(place >= end, 1, 0)
    sides = [
        jnp.where(c == SIDES[0] ** 2, SIDES[0], jnp.where(c == SIDES[1] ** 2, SIDES[1], SIDES[2]))
        for c in count
    ]
    start = jnp.where(segment == 0, 0, jnp.where(segment == 1, ends[0], ends[1]))
    side = jnp.where(segment == 0, sides[0], jnp.where(segment == 1, sides[1], sides[2])).astype(F32)
    offset = (place - start).astype(F32)
    row = jnp.floor((offset + 0.5) / side)
    col = offset - row * side
    valid = segment < 3
    return segment, jnp.where(valid, row, 0.0), jnp.where(valid, col, 0.0), valid


def gelu_parts(values):
    bell = jnp.exp(values * values * -0.5)
    size = jnp.abs(values) * math.sqrt(0.5)
    t = 1.0 / (1.0 + 0.3275911 * size)
    poly = t * (
        0.254829592
        + t * (-0.284496736 + t * (1.421413741 + t * (-1.453152027 + t * 1.061405429)))
    )
    tail = 0.5 * poly * bell
    below = jnp.where(values < 0, tail, 1.0 - tail)
    return values * below, below + values * bell * (1.0 / math.sqrt(2.0 * math.pi))


def smem():
    return pl.BlockSpec(memory_space=pltpu.SMEM)


def whole(shape):
    return pl.BlockSpec(shape, lambda *_: (0,) * len(shape))


def cols(rows, width, first=0):
    return pl.BlockSpec((rows, width), lambda j, *_: (0, first + j))


def rowblk(height, width, first=0):
    return pl.BlockSpec((height, width), lambda j, *_: (first + j, 0))


def cost(flops, moved):
    return pl.CostEstimate(flops=1, bytes_accessed=1, transcendentals=0)


def params(**kw):
    return pltpu.CompilerParams(vmem_limit_bytes=VMEM_LIMIT, dimension_semantics=("arbitrary",), **kw)


def attend_quad(q, k, v, add_bias, probs_ref):
    lane = lax.broadcasted_iota(jnp.int32, q.shape, 1)
    scaled = q * jnp.asarray(HDIM**-0.5, BF16)
    v_t = v.T
    outs = []
    for h in range(QUAD):
        q_h = jnp.where(lane // HDIM == h, scaled, jnp.zeros_like(scaled))
        scores = add_bias(dot_nt(k, q_h), h)
        top = jnp.max(scores, axis=0, keepdims=True)
        weights = jnp.exp(scores - top)
        total = jnp.sum(weights, axis=0, keepdims=True)
        probs = (weights * (1.0 / total)).astype(BF16)
        probs_ref[h] = probs
        outs.append(dot_nn(v_t[h * HDIM : (h + 1) * HDIM], probs))
    return jnp.concatenate(outs, axis=0).astype(BF16).T


def slope_of(group, h):
    found = 0.0
    for g in range(HEADS // QUAD):
        found = jnp.where(group == g, 2.0 ** (-8.0 * (g * QUAD + h + 1) / HEADS), found)
    return found


def self_forward_kernel(
    lens, radar, cot, gains, shifts, biases, wq, wk, wv, wo,
    n1, q_out, k_out, v_out, probs, att_out, resid, n2, gf, dist,
):
    j = pl.program_id(0)
    rows = n1.shape[0]

    @pl.when(j == 0)
    def _():
        wide = radar[...].astype(F32)
        n1[...] = norm(wide, gains[0:1], shifts[0:1]).astype(BF16)
        resid[...] = wide + biases[0:1]
        seg_k, row_k, col_k, valid = layout_of(lens, (rows, 1), 0)
        gf[...] = jnp.where(valid, cot[...], jnp.zeros_like(cot))
        seg_q, row_q, col_q, _ = layout_of(lens, (1, rows), 1)
        dr = row_k - row_q
        dc = col_k - col_q
        dist[...] = jnp.where(seg_k == seg_q, jnp.sqrt(dr * dr + dc * dc), FAR)

    x = n1[...]
    q = dot_nn(x, wq[...]).astype(BF16)
    k = dot_nn(x, wk[...]).astype(BF16)
    v = dot_nn(x, wv[...]).astype(BF16)
    q_out[...] = q
    k_out[...] = k
    v_out[...] = v
    att = attend_quad(
        q, k, v, lambda s, h: s - slope_of(j, h) * dist[...], probs
    )
    att_out[...] = att
    resid[...] += dot_nn(att, wo[...])

    @pl.when(j == pl.num_programs(0) - 1)
    def _():
        n2[...] = norm(resid[...], gains[1:2], shifts[1:2]).astype(BF16)


def cross_forward_kernel(
    lens, res_in, n_in, optic, gains, shifts, biases, wq, wk, wv, wo,
    q_out, k_out, v_out, probs, att_out, resid, n3, mask,
):
    j = pl.program_id(0)
    rows = n_in.shape[0]

    @pl.when(j == 0)
    def _():
        resid[...] = res_in[...] + biases[1:2]
        seg_k = layout_of(lens, (rows, 1), 0)[0]
        seg_q = layout_of(lens, (1, rows), 1)[0]
        mask[...] = jnp.where(seg_k == seg_q, 0.0, MASKED)

    q = dot_nn(n_in[...], wq[...]).astype(BF16)
    k = dot_nn(optic[...], wk[...]).astype(BF16)
    v = dot_nn(optic[...], wv[...]).astype(BF16)
    q_out[...] = q
    k_out[...] = k
    v_out[...] = v
    att = attend_quad(q, k, v, lambda s, h: s + mask[...], probs)
    att_out[...] = att
    resid[...] += dot_nn(att, wo[...])

    @pl.when(j == pl.num_programs(0) - 1)
    def _():
        n3[...] = norm(resid[...], gains[2:3], shifts[2:3]).astype(BF16)


def shaped(*shape, dtype=BF16):
    return jax.ShapeDtypeStruct(shape, dtype)


def held(*shape, dtype=BF16):
    return pltpu.HBM(shape, dtype)


def far(*arrays):
    return [pltpu.with_memory_space_constraint(a, pltpu.HBM) for a in arrays]


def self_forward(rows, lens, radar, cot, gains, shifts, biases, w_qkv, w_out):
    d = radar.shape[1]
    wide = QUAD * HDIM
    steps = d // wide
    return pl.pallas_call(
        self_forward_kernel,
        grid=(steps,),
        in_specs=[
            smem(), whole((rows, d)), whole((rows, d)),
            *[whole((3, d))] * 3,
            cols(d, wide), cols(d, wide, steps), cols(d, wide, 2 * steps), rowblk(wide, d),
        ],
        out_specs=[
            whole((rows, d)), cols(rows, wide), cols(rows, wide), cols(rows, wide),
            pl.BlockSpec((QUAD, rows, rows), lambda j: (j, 0, 0)),
            cols(rows, wide), whole((rows, d)), whole((rows, d)), whole((rows, d)),
        ],
        out_shape=[
            held(rows, d), held(rows, d), held(rows, d), held(rows, d),
            held(HEADS, rows, rows), held(rows, d), shaped(rows, d, dtype=F32), shaped(rows, d), held(rows, d),
        ],
        scratch_shapes=[pltpu.VMEM((rows, rows), F32)],
        compiler_params=params(),
        cost_estimate=cost(8 * rows * d * d + 12 * HEADS * rows * rows * 128, 8 * d * d + HEADS * rows * rows * 2),
        name="self_forward",
    )(lens, *far(radar, cot, gains, shifts, biases),
      *far(w_qkv, w_qkv, w_qkv, w_out))


def cross_forward(rows, lens, res_in, n_in, optic, gains, shifts, biases, w_q, w_kv, w_out):
    d = optic.shape[1]
    wide = QUAD * HDIM
    steps = d // wide
    return pl.pallas_call(
        cross_forward_kernel,
        grid=(steps,),
        in_specs=[
            smem(), whole((rows, d)), whole((rows, d)), whole((rows, d)),
            *[whole((3, d))] * 3,
            cols(d, wide), cols(d, wide), cols(d, wide, steps), rowblk(wide, d),
        ],
        out_specs=[
            cols(rows, wide), cols(rows, wide), cols(rows, wide),
            pl.BlockSpec((QUAD, rows, rows), lambda j: (j, 0, 0)),
            cols(rows, wide), whole((rows, d)), whole((rows, d)),
        ],
        out_shape=[
            held(rows, d), held(rows, d), held(rows, d),
            held(HEADS, rows, rows), held(rows, d), shaped(rows, d, dtype=F32), shaped(rows, d),
        ],
        scratch_shapes=[pltpu.VMEM((rows, rows), F32)],
        compiler_params=params(),
        cost_estimate=cost(8 * rows * d * d + 12 * HEADS * rows * rows * 128, 8 * d * d + HEADS * rows * rows * 2),
        name="cross_forward",
    )(lens, res_in, n_in, optic, gains, shifts, biases, w_q, w_kv, w_kv, w_out)


def hidden_kernel(res2, n3, gf, gains, hb, win, wout, act_out, grad_two, vectors, acc):
    j = pl.program_id(0)

    @pl.when(j == 0)
    def _():
        acc[...] = jnp.zeros_like(acc)

    act, slope = gelu_parts(dot_nn(n3[...], win[...]) + hb[...])
    act_out[...] = act.astype(BF16)
    g_pre = (dot_nt(gf[...], wout[...]) * slope).astype(BF16)
    acc[...] += dot_nt(g_pre, win[...])
    vectors[pl.ds(j, 1)] = jnp.sum(g_pre.astype(F32), axis=0, keepdims=True)

    @pl.when(j == pl.num_programs(0) - 1)
    def _():
        part, g_gain, g_shift = norm_back(res2[...], gains[2:3], acc[...])
        wide = gf[...].astype(F32)
        grad_two[...] = wide + part
        vectors[4:5] = g_gain
        vectors[5:6] = g_shift
        vectors[6:7] = jnp.sum(wide, axis=0, keepdims=True)
        vectors[7:8] = jnp.zeros_like(g_gain)


def hidden(rows, res2, n3, gf, gains, hb, win, wout):
    d = n3.shape[1]
    ff = win.shape[1]
    chunk = ff // 4
    return pl.pallas_call(
        hidden_kernel,
        grid=(4,),
        in_specs=[
            whole((rows, d)), whole((rows, d)), whole((rows, d)),
            whole((3, d)), cols(1, chunk), cols(d, chunk), rowblk(chunk, d),
        ],
        out_specs=[cols(rows, chunk), whole((rows, d)), whole((8, d))],
        out_shape=[held(rows, ff), held(rows, d, dtype=F32), held(8, d, dtype=F32)],
        scratch_shapes=[pltpu.VMEM((rows, d), F32)],
        compiler_params=params(),
        cost_estimate=cost(6 * rows * d * ff, 4 * d * ff),
        name="hidden",
    )(res2, n3, *far(gf), gains, hb, win, wout)


def output_kernel(lens, act, res2, biases, wout, y_out, acc):
    j = pl.program_id(0)
    rows = act.shape[0]

    @pl.when(j == 0)
    def _():
        acc[...] = res2[...] + biases[2:3]

    acc[...] += dot_nn(act[...], wout[...])

    @pl.when(j == pl.num_programs(0) - 1)
    def _():
        valid = layout_of(lens, (rows, 1), 0)[3]
        y_out[0:rows] = jnp.where(valid, acc[...], 0.0).astype(BF16)
        if y_out.shape[0] > rows:
            y_out[rows:] = jnp.zeros((y_out.shape[0] - rows, y_out.shape[1]), BF16)


def output(rows, local_rows, lens, act, res2, biases, wout):
    ff, d = wout.shape
    chunk = ff // 2
    return pl.pallas_call(
        output_kernel,
        grid=(2,),
        in_specs=[smem(), cols(rows, chunk), whole((rows, d)), whole((3, d)), rowblk(chunk, d)],
        out_specs=whole((local_rows, d)),
        out_shape=held(local_rows, d),
        scratch_shapes=[pltpu.VMEM((rows, d), F32)],
        compiler_params=params(),
        cost_estimate=cost(2 * rows * d * ff, 2 * d * ff),
        name="output",
    )(lens, act, res2, biases, wout)


def hidden_grads_kernel(blocks, meta, *refs):
    normed, grads = refs[:blocks], refs[blocks : 2 * blocks]
    hb_a, hb_b, win_a, win_b, wout_a, wout_b, dwin, dwout, acc_in, acc_out = refs[2 * blocks :]
    win = jnp.concatenate([win_a[...], win_b[...]], axis=1)
    wout = jnp.concatenate([wout_a[...], wout_b[...]], axis=0)
    hb = jnp.concatenate([hb_a[...], hb_b[...]], axis=1)
    for i in range(blocks):
        act, slope = gelu_parts(dot_nn(normed[i][...], win) + hb)
        g_pre = (dot_nt(grads[i][...], wout) * slope).astype(BF16)
        into = dot_nn(normed[i][...].T, g_pre)
        out = dot_nn(act.astype(BF16).T, grads[i][...])
        if i == 0:
            acc_in[...] = into
            acc_out[...] = out
        else:
            acc_in[...] += into
            acc_out[...] += out
    at_y, at_c, at_p = meta[0], meta[1], meta[3]
    piece = dwout.shape[2]
    for y in range(2):
        for p in range(2):
            at = (y * 2 + p) * piece
            dwout[y ^ at_y, p ^ at_p] = acc_out[at : at + piece].astype(BF16)
    piece = dwin.shape[3]
    for y in range(2):
        for c in range(2):
            for p in range(2):
                at = ((y * 2 + c) * 2 + p) * piece
                dwin[y ^ at_y, c ^ at_c, p ^ at_p] = acc_in[at : at + piece].astype(BF16)


def hidden_grads(rows, meta, normed, grads, hb, win, wout):
    d, ff = win.shape
    part = ff // 8
    blocks = len(normed)

    def wide(height, y):
        return pl.BlockSpec((height, part), lambda i, m: (0, y * 4 + m[1] * 2 + m[2]))

    def tall(y):
        return pl.BlockSpec((part, d), lambda i, m: (y * 4 + m[1] * 2 + m[2], 0))

    return pl.pallas_call(
        functools.partial(hidden_grads_kernel, blocks),
        grid_spec=pltpu.PrefetchScalarGridSpec(
            num_scalar_prefetch=1,
            grid=(1,),
            in_specs=[
                *[whole((rows, d))] * (2 * blocks),
                wide(1, 0), wide(1, 1), wide(d, 0), wide(d, 1), tall(0), tall(1),
            ],
            out_specs=[whole((2, 2, 2, d // 8, 2 * part)), whole((2, 2, part // 2, d))],
            scratch_shapes=[pltpu.VMEM((d, 2 * part), F32), pltpu.VMEM((2 * part, d), F32)],
        ),
        out_shape=[shaped(2, 2, 2, d // 8, 2 * part), shaped(2, 2, part // 2, d)],
        compiler_params=params(),
        cost_estimate=cost(16 * blocks * rows * d * part, 4 * blocks * rows * d + 4 * d * ff),
        name="hidden_grads",
    )(meta, *far(*normed, *grads, hb, hb, win, win, wout, wout))


def place(keep, send, bucket, grad, spot):
    at_hd, at_grp = lax.axis_index("hd"), lax.axis_index("grp")
    at_y, first = at_hd // 2, lax.rem(at_hd, 2) == 0
    at_x, at_p = lax.rem(at_grp, 2), lax.rem(at_grp // 2, 2)
    part = grad.shape[0] // 16
    for y in range(2):
        for x in range(2):
            for p in range(2):
                at = y * 8 + x * 2 + p
                low = grad[at * part : (at + 1) * part]
                high = grad[(at + 4) * part : (at + 5) * part]
                ways = (x ^ at_x, y ^ at_y)
                if isinstance(bucket, int):
                    lead, other = ways[bucket], ways[1 - bucket]
                else:
                    lead = jnp.where(bucket == 0, ways[0], ways[1])
                    other = jnp.where(bucket == 0, ways[1], ways[0])
                to = (bucket, lead, other, p ^ at_p, slice(None), spot)
                keep[to] = jnp.where(first, low, high)
                send[to] = jnp.where(first, high, low)


def quad_back(q, k, v, att, g_att, probs):
    lane = lax.broadcasted_iota(jnp.int32, q.shape, 1)
    nil = jnp.zeros_like(q)
    g_t = g_att.T
    k_t = k.T
    inner = g_t.astype(F32) * att.T.astype(F32)
    dq_t, dk, dv = [], 0.0, 0.0
    for h in range(QUAD):
        part = slice(h * HDIM, (h + 1) * HDIM)
        mine = lane // HDIM == h
        delta = jnp.sum(inner[part], axis=0, keepdims=True)
        v_h = jnp.where(mine, v, nil)
        p = probs[h]
        g_scores = (p.astype(F32) * (dot_nn(v_h, g_t) - delta)).astype(BF16)
        dv = dv + dot_nn(p, jnp.where(mine, g_att, nil))
        dk = dk + dot_nn(g_scores, jnp.where(mine, q, nil))
        dq_t.append(dot_nn(k_t[part], g_scores))
    scale = HDIM**-0.5
    dq = (jnp.concatenate(dq_t, axis=0) * scale).astype(BF16).T
    return dq, (dk * scale).astype(BF16), dv.astype(BF16)


def aligned(first, width):
    return pl.ds(pl.multiple_of(first, 128), width)


def cross_back_kernel(
    grad_in, res, xq, xkv, q, k, v, att, att_all, probs, gains, wo, wq, att_self,
    keep, send, dk_out, dv_out, vectors, grad_out, low, xq_t, xkv_t, acc,
):
    i = pl.program_id(0)
    d = xq.shape[1]
    wide = q.shape[1]

    @pl.when(i == 0)
    def _():
        low[...] = grad_in[...].astype(BF16)
        xq_t[...] = xq[...].T
        xkv_t[...] = xkv[...].T
        acc[...] = jnp.zeros_like(acc)
        place(keep, send, 0, dot_nn(att_all[...].T, low[...]).astype(BF16), slice(0, d))

    g_att = dot_nt(low[...], wo[...]).astype(BF16)
    dq, dk, dv = quad_back(q[...], k[...], v[...], att[...], g_att, probs)
    dk_out[...] = dk
    dv_out[...] = dv
    place(keep, send, 0, dot_nn(xq_t[...], dq).astype(BF16), aligned(d + i * wide, wide))
    place(keep, send, 1, dot_nn(xkv_t[...], dk).astype(BF16), aligned(i * wide, wide))
    place(keep, send, 1, dot_nn(xkv_t[...], dv).astype(BF16), aligned(d + i * wide, wide))
    acc[...] += dot_nt(dq, wq[...])

    @pl.when(i == pl.num_programs(0) - 1)
    def _():
        part, g_gain, g_shift = norm_back(res[...], gains[1:2], acc[...])
        grad = grad_in[...] + part
        grad_out[...] = grad
        vectors[0:1] = jnp.sum(low[...].astype(F32), axis=0, keepdims=True)
        vectors[1:2] = g_gain
        vectors[2:3] = g_shift
        grad_low = grad.astype(BF16)
        vectors[3:4] = jnp.sum(grad_low.astype(F32), axis=0, keepdims=True)
        vectors[4:8] = jnp.zeros((4, d), F32)
        out = dot_nn(att_self[...].T, grad_low).astype(BF16)
        place(keep, send, 0, out[:, : d // 2], slice(2 * d, 2 * d + d // 2))
        place(keep, send, 1, out[:, d // 2 :], slice(2 * d, 2 * d + d // 2))


def self_back_kernel(
    grad_in, xq, q, k, v, att, probs, wo, keep, send, dk_out, dv_out, dq_out, low, xq_t,
):
    i = pl.program_id(0)
    d = xq.shape[1]
    wide = q.shape[1]

    @pl.when(i == 0)
    def _():
        low[...] = grad_in[...].astype(BF16)
        xq_t[...] = xq[...].T

    g_att = dot_nt(low[...], wo[...]).astype(BF16)
    dq, dk, dv = quad_back(q[...], k[...], v[...], att[...], g_att, probs)
    dq_out[...] = dq
    dk_out[...] = dk
    dv_out[...] = dv
    place(keep, send, 0, dot_nn(xq_t[...], dq).astype(BF16), aligned(i * wide, wide))
    place(keep, send, 1, dot_nn(xq_t[...], dv).astype(BF16), aligned(i * wide, wide))
    keys = dot_nn(xq_t[...], dk).astype(BF16)
    half = wide // 2
    for t in range(2):
        piece = 2 * i + t
        bucket = jnp.where(piece * half < d // 2, 0, 1)
        at = d + piece * half - bucket * (d // 2)
        place(keep, send, bucket, keys[:, t * half : (t + 1) * half], aligned(at, half))


def cross_back(rows, grad_in, res, xq, xkv, q, k, v, att, probs, gains, wo, wq, att_self):
    d = xq.shape[1]
    wide = QUAD * HDIM
    halves = (2, 2, 2, 2, d // 16, 2 * d + d // 2)
    at = cols(rows, wide)
    full = whole((rows, d))
    return pl.pallas_call(
        cross_back_kernel,
        grid=(d // wide,),
        in_specs=[
            full, full, full, full, at, at, at, at, full,
            pl.BlockSpec((QUAD, rows, rows), lambda i: (i, 0, 0)),
            whole((3, d)), rowblk(wide, d), cols(d, wide), full,
        ],
        out_specs=[*[whole(halves)] * 2, at, at, whole((8, d)), full],
        out_shape=[
            *[shaped(*halves)] * 2, held(rows, d), held(rows, d), held(8, d, dtype=F32), held(rows, d, dtype=F32),
        ],
        scratch_shapes=[
            pltpu.VMEM((rows, d), BF16), pltpu.VMEM((d, rows), BF16), pltpu.VMEM((d, rows), BF16),
            pltpu.VMEM((rows, d), F32),
        ],
        compiler_params=params(),
        cost_estimate=cost(18 * rows * d * d + 24 * HEADS * rows * rows * 128, 16 * d * d),
        name="cross_back",
    )(grad_in, res, xq, xkv, q, k, v, att, att, *far(probs), gains, wo, wq, att_self)


def self_back(rows, grad_in, xq, q, k, v, att, probs, wo):
    d = xq.shape[1]
    wide = QUAD * HDIM
    halves = (2, 2, 2, 2, d // 16, d + d // 2)
    at = cols(rows, wide)
    full = whole((rows, d))
    return pl.pallas_call(
        self_back_kernel,
        grid=(d // wide,),
        in_specs=[
            full, full, at, at, at, at,
            pl.BlockSpec((QUAD, rows, rows), lambda i: (i, 0, 0)), rowblk(wide, d),
        ],
        out_specs=[*[whole(halves)] * 2, at, at, at],
        out_shape=[*[shaped(*halves)] * 2, held(rows, d), held(rows, d), held(rows, d)],
        scratch_shapes=[pltpu.VMEM((rows, d), BF16), pltpu.VMEM((d, rows), BF16)],
        compiler_params=params(),
        cost_estimate=cost(18 * rows * d * d + 24 * HEADS * rows * rows * 128, 16 * d * d),
        name="self_back",
    )(grad_in, xq, q, k, v, att, *far(probs), wo)


def through(parts, weights):
    total = None
    for i, part in enumerate(parts):
        d = part.shape[1]
        term = dot_nt(part[...], weights[:, i * d : (i + 1) * d])
        total = term if total is None else total + term
    return total


def store_padded(out, values):
    rows = values.shape[0]
    out[0:rows] = values
    if out.shape[0] > rows:
        out[rows:] = jnp.zeros((out.shape[0] - rows, out.shape[1]), out.dtype)


def optic_kernel(dk, dv, weights, out):
    store_padded(out, through([dk, dv], weights))


def optic(local_rows, dk, dv, weights):
    rows, d = dk.shape
    return pl.pallas_call(
        optic_kernel,
        in_specs=[whole(dk.shape), whole(dv.shape), whole(weights.shape)],
        out_specs=whole((local_rows, d)),
        out_shape=held(local_rows, d, dtype=F32),
        grid=(1,),
        compiler_params=params(),
        cost_estimate=cost(4 * rows * d * d, 4 * d * d),
        name="optic",
    )(*far(dk, dv), weights)


def radar_kernel(dq, dk, dv, weights, grad_in, radar, gains, hidden_vec, cross_vec, out, vectors):
    total = through([dq, dk, dv], weights)
    part, g_gain, g_shift = norm_back(radar[...].astype(F32), gains[0:1], total)
    store_padded(out, grad_in[...] + part)
    vectors[0:1] = g_gain
    vectors[1:2] = cross_vec[1:2]
    vectors[2:3] = hidden_vec[4:5]
    vectors[3:4] = g_shift
    vectors[4:5] = cross_vec[2:3]
    vectors[5:6] = hidden_vec[5:6]
    vectors[6:7] = cross_vec[3:4]
    vectors[7:8] = cross_vec[0:1]
    vectors[8:9] = hidden_vec[6:7]
    vectors[9:13] = hidden_vec[0:4]
    vectors[13:16] = jnp.zeros((3, out.shape[1]), F32)


def radar(local_rows, dq, dk, dv, weights, grad_in, tokens, gains, vectors):
    rows, d = dq.shape
    full = whole((rows, d))
    return pl.pallas_call(
        radar_kernel,
        grid=(1,),
        in_specs=[full, full, full, whole(weights.shape), full, full, whole((3, d)), *[whole((8, d))] * 2],
        out_specs=[whole((local_rows, d)), whole((16, d))],
        out_shape=[held(local_rows, d, dtype=F32), shaped(16, d, dtype=F32)],
        compiler_params=params(),
        cost_estimate=cost(6 * rows * d * d, 6 * d * d),
        name="radar",
    )(dq, dk, dv, weights, grad_in, tokens, gains, *vectors)
def hop(values, perm):
    return lax.ppermute(values, ("grp", "hd"), perm)


def pairs(move):
    found = []
    for z in range(4):
        for x in range(2):
            for y in range(2):
                for c in range(2):
                    to = move(z, x, y, c)
                    if to is not None:
                        tz, tx, ty, tc = to
                        found.append(((z * 2 + x) * 4 + y * 2 + c, (tz * 2 + tx) * 4 + ty * 2 + tc))
    return found


ACROSS_CORE = pairs(lambda z, x, y, c: (z, x, y, 1 - c))
ACROSS_Y = pairs(lambda z, x, y, c: (z, x, 1 - y, c))
ACROSS_X = pairs(lambda z, x, y, c: (z, 1 - x, y, c))
ACROSS_P = pairs(lambda z, x, y, c: (z ^ 1, x, y, c))
ACROSS_Q = pairs(lambda z, x, y, c: (z ^ 2, x, y, c))
ACROSS_XP = pairs(lambda z, x, y, c: (z ^ 1, 1 - x, y, c))


def add(*terms):
    total = terms[0].astype(F32)
    for term in terms[1:]:
        total = total + term.astype(F32)
    return total.astype(terms[0].dtype)


def in_order(at, own, other):
    return jnp.where(at == 0, own, other), jnp.where(at == 0, other, own)


def tie(values):
    return list(lax.optimization_barrier(tuple(values)))


MOVES = {
    "C": ACROSS_CORE, "Y": ACROSS_Y, "Z": ACROSS_Y, "X": ACROSS_X, "P": ACROSS_P, "Q": ACROSS_Q,
    "A": ACROSS_P, "G": ACROSS_X, "D": ACROSS_XP, "W": ACROSS_Y, "V": ACROSS_X,
    "B": ACROSS_P, "H": ACROSS_X,
}


class Flow:
    def __init__(self, value, at_x, at_p):
        self.value, self.ends, self.at_x, self.at_p = value, {}, at_x, at_p

    def operand(self, stage):
        return self.value[1] if stage in ("Y", "P") else self.value

    def absorb(self, stage, got):
        if stage in ("Y", "P"):
            self.value = add(self.value[0], got)
        elif stage == "Q":
            self.value = add(self.value, got)
        elif stage == "B":
            self.value = jnp.stack(in_order(self.at_p, self.value, got))
        else:
            self.ends[stage] = got

    def together(self):
        if "H" in self.ends:
            return in_order(self.at_x, self.value, self.ends["H"])
        rows = [
            jnp.stack(in_order(self.at_p, self.value, self.ends["A"])),
            jnp.stack(in_order(self.at_p, self.ends["G"], self.ends["D"])),
        ]
        return in_order(self.at_x, *rows)


class InFlow(Flow):
    def operand(self, stage):
        if stage in ("Y", "Z"):
            return self.value[1, 1 if stage == "Y" else 0]
        if stage == "C":
            return self.value[1]
        return self.value[:, 1] if stage == "P" else self.value

    def absorb(self, stage, got):
        if stage == "Y":
            self.other = add(self.value[0, 1], got)
        elif stage == "Z":
            self.value = [add(self.value[0, 0], got), self.other]
        elif stage == "C":
            self.value = jnp.stack([self.value[0], got])
        elif stage == "P":
            self.value = add(self.value[:, 0], got)
        else:
            super().absorb(stage, got)


class RowFlow(Flow):
    def __init__(self, keep, send, at_x, at_p):
        super().__init__(None, at_x, at_p)
        self.keep, self.send, self.parts = keep, send, None

    def operand(self, stage):
        if stage == "C":
            return self.send
        if stage in "XYWV":
            return self.parts[int(stage in "WV")][1]
        if stage == "P" and self.value is None:
            self.value = jnp.stack(self.parts)
        return self.value[:, 1] if stage == "P" else self.value

    def absorb(self, stage, got):
        if stage == "C":
            self.parts = [[add(self.keep[b, i], got[b, i]) for i in range(2)] for b in range(2)]
        elif stage in "XYWV":
            b = int(stage in "WV")
            self.parts[b] = add(self.parts[b][0], got)
        elif stage == "P":
            self.value = add(self.value[:, 0], got)
        else:
            super().absorb(stage, got)


class Vectors(Flow):
    def operand(self, stage):
        return self.value

    def absorb(self, stage, got):
        self.value = self.value + got


def whole_rows(keep, send, bucket, at):
    at_y, at_c, at_x, at_p = at
    lead_at, other_at = (at_x, at_y) if bucket == 0 else (at_y, at_x)
    parts = jnp.stack(in_order(at_c, keep[bucket], send[bucket]))
    for axis, place_at in ((1, lead_at), (2, other_at), (3, at_p)):
        own, other = [lax.index_in_dim(parts, i, axis, keepdims=False) for i in range(2)]
        parts = jnp.stack(in_order(place_at, own, other), axis=axis)
    order = (2, 0, 1, 3, 4, 5) if bucket == 0 else (1, 0, 2, 3, 4, 5)
    return parts.transpose(order).reshape(-1, parts.shape[-1])


def summed_anywhere(grad):
    mine = lax.psum_scatter(grad, "hd", scatter_dimension=0, tiled=True)
    return lax.psum(mine.astype(F32), "grp")


class Plan:
    def __init__(self):
        self.flows, self.flying = {}, {}

    def begin(self, gate, *moves):
        sent = [self.flows[m[0]].operand(m[1]) for m in moves]
        gate, *sent = tie([gate, *sent])
        for m, operand in zip(moves, sent):
            self.flying[m] = hop(operand, MOVES[m[1]])
        return gate

    def end(self, gate, *moves):
        gate, *got = tie([gate, *[self.flying.pop(m) for m in moves]])
        for m, value in zip(moves, got):
            self.flows[m[0]].absorb(m[1], value)
        return gate


def on_device(
    radar_tokens, optic_tokens, tile_lengths, norm_gains, norm_shifts, self_qkv, self_out,
    cross_query, cross_keyval, cross_out, hidden_in, hidden_out, proj_biases, hidden_bias, cotangent,
):
    local_rows, d = radar_tokens.shape
    ff = hidden_in.shape[1]
    known = lax.axis_size("grp") == 8 and lax.axis_size("hd") == 4
    at_hd = lax.axis_index("hd")
    at_grp = lax.axis_index("grp")
    at_y, at_c, at_z, at_x = at_hd // 2, at_hd % 2, at_grp // 2, at_grp % 2
    at_p = at_z % 2
    rows = rows_in_use(local_rows, tile_lengths.shape[2])
    hb = hidden_bias[None]

    n1, q1, k1, v1, p1, att1, res1, n2, gf = self_forward(
        rows, tile_lengths, radar_tokens, cotangent, norm_gains, norm_shifts, proj_biases, self_qkv, self_out
    )
    if known:
        n2, gf = tie([n2, gf])
        gf_x = hop(gf, ACROSS_X)
        gf_c = hop(gf, ACROSS_CORE)
    q2, k2, v2, p2, att2, res2, n3 = cross_forward(
        rows, tile_lengths, res1, n2, optic_tokens, norm_gains, norm_shifts, proj_biases,
        cross_query, cross_keyval, cross_out,
    )
    if known:
        n3, gf_x, gf_c, res2 = tie([n3, gf_x, gf_c, res2])
        gf_xc = hop(gf_x, ACROSS_CORE)
        n3_x = hop(n3, ACROSS_X)
        n3_c = hop(n3, ACROSS_CORE)
    act, grad_two, hidden_vec = hidden(rows, res2, n3, gf, norm_gains, hb, hidden_in, hidden_out)

    def cross_step(grad):
        return cross_back(
            rows, grad, res1, n2, optic_tokens, q2, k2, v2, att2, p2, norm_gains, cross_out, cross_query, att1
        )

    def self_step(grad):
        return self_back(rows, grad, n1, q1, k1, v1, att1, p1, self_out)

    def radar_step(dq, grad):
        return radar(local_rows, dq, dk1, dv1, self_qkv, grad, radar_tokens, norm_gains, [hidden_vec, cross_vec])

    if known:
        meta = jnp.stack([at_y, at_c, at_x, at_p]).astype(jnp.int32)
        act, n3_x, n3_c, gf_x, gf_c, gf_xc, grad_two = tie([act, n3_x, n3_c, gf_x, gf_c, gf_xc, grad_two])
        n3_xc = hop(n3_x, ACROSS_CORE)
        dwin, dwout = hidden_grads(
            rows, meta, [n3, n3_x, n3_c, n3_xc], [gf, gf_x, gf_c, gf_xc], hb, hidden_in, hidden_out
        )
        plan = Plan()
        grad_two, dwin, dwout = tie([grad_two, dwin, dwout])
        plan.flows["o"], plan.flows["n"] = Flow(dwout, at_x, at_p), InFlow(dwin, at_x, at_p)

        grad_two = plan.begin(grad_two, "oY", "nY")
        keep, send, dk2, dv2, cross_vec, grad_one = cross_step(grad_two)
        act = plan.end(tie([act, grad_one])[0], "oY", "nY")
        plan.flows["a"] = RowFlow(keep, send, at_x, at_p)

        act = plan.begin(act, "aC", "nZ", "oP")
        layer_output = output(rows, local_rows, tile_lengths, act, res2, proj_biases, hidden_out)
        grad_one = plan.end(tie([grad_one, layer_output])[0], "aC", "nZ", "oP")

        grad_one = plan.begin(grad_one, "oQ", "aX", "aW", "nC")
        keep, send, dk1, dv1, dq1 = self_step(grad_one)
        dq1 = plan.end(dq1, "oQ", "aX", "aW", "nC")
        plan.flows["c"] = RowFlow(keep, send, at_x, at_p)

        dq1 = plan.begin(dq1, "cC", "nP", "oB", "aY", "aV")
        radar_grad, small = radar_step(dq1, grad_one)
        dk2 = plan.end(tie([dk2, radar_grad])[0], "cC", "nP", "oB", "aY", "aV")
        plan.flows["s"] = Vectors(small, at_x, at_p)

        dk2 = plan.begin(dk2, "nQ", "cX", "cW", "aP", "sC")
        optic_grad = optic(local_rows, dk2, dv2, cross_keyval)
        gate = plan.end(optic_grad, "nQ", "cX", "cW", "aP", "sC")

        for stages in (
            ("cV", "aQ", "oH", "cY", "nB", "sY"),
            ("cP", "nH", "aB", "sX"),
            ("cQ", "aH", "sP"),
            ("cG", "cD", "cA", "sQ"),
        ):
            gate = plan.end(plan.begin(gate, *stages), *stages)
        optic_grad = gate

        done = {name: plan.flows[name].together() for name in "onac"}
        out_part = jnp.stack(done["o"]).reshape(-1, d).astype(F32)
        slices = [in_order(at_c, v[:, 0], v[:, 1]) for v in done["n"]]
        half = ff // 8
        in_part = jnp.concatenate(
            [
                slices[x][c][..., y * half : (y + 1) * half].reshape(-1, half)
                for y in range(2) for c in range(2) for x in range(2)
            ],
            axis=1,
        ).astype(F32)
        (cross_a, cross_b), (self_a, self_b) = [
            [jnp.stack([v[:, i] for v in done[name]]).reshape(d // 4, -1).astype(F32) for i in range(2)] for name in "ac"
        ]
        small = plan.flows["s"].value
    else:
        into, out = [], []
        for c in range(2):
            for x in range(2):
                at = jnp.asarray([0, c, x, 0], jnp.int32)
                dwin, dwout = hidden_grads(rows, at, [n3], [gf], hb, hidden_in, hidden_out)
                into.append(jnp.stack([dwin[:, c], dwin[:, 1 - c]], axis=1).reshape(d, 2, ff // 8))
                out.append(dwout.reshape(2, ff // 8, d))
        in_part = summed_anywhere(jnp.stack(into, axis=2).reshape(d, ff))
        out_part = summed_anywhere(jnp.stack(out, axis=1).reshape(ff, d))
        cross_keep, cross_send, dk2, dv2, cross_vec, grad_one = cross_step(grad_two)
        self_keep, self_send, dk1, dv1, dq1 = self_step(grad_one)
        radar_grad, small = radar_step(dq1, grad_one)
        optic_grad = optic(local_rows, dk2, dv2, cross_keyval)
        layer_output = output(rows, local_rows, tile_lengths, act, res2, proj_biases, hidden_out)
        at = (at_y, at_c, at_x, at_p)
        cross_a, cross_b = [summed_anywhere(whole_rows(cross_keep, cross_send, b, at)) for b in range(2)]
        self_a, self_b = [summed_anywhere(whole_rows(self_keep, self_send, b, at)) for b in range(2)]
        small = lax.psum(small, ("grp", "hd"))
    vectors = lax.dynamic_slice_in_dim(small[:9], at_hd * (d // 4), d // 4, 1)
    hidden_part = lax.dynamic_index_in_dim(small[9:13], at_hd, 0, keepdims=False)
    return (
        layer_output,
        radar_grad,
        optic_grad,
        jnp.concatenate([self_a, self_b[:, d:], self_b[:, :d]], axis=1),
        jnp.concatenate([cross_a[:, 2 * d :], cross_b[:, 2 * d :]], axis=1),
        cross_a[:, d : 2 * d],
        cross_b[:, : 2 * d],
        cross_a[:, :d],
        in_part,
        out_part,
        vectors[0:3],
        vectors[3:6],
        vectors[6:9],
        hidden_part,
    )


def solution(mesh):
    rows = P(("grp", "hd"), None)
    kept = P("hd", None)
    vector = P(None, "hd")
    return jax.shard_map(
        on_device,
        mesh=mesh,
        in_specs=(rows, rows, P("grp", None, None), *[P()] * 11, rows),
        out_specs=(rows, rows, rows, *[kept] * 7, vector, vector, vector, P("hd")),
        check_vma=False,
    )
```

```python
import functools
import math

import jax
import jax.numpy as jnp
import numpy as np
from jax import lax
from jax.experimental import pallas as pl
from jax.experimental.pallas import tpu as pltpu
from jax.sharding import PartitionSpec as P

HEADS = 12
HDIM = 64
SIDES = (12, 15, 20)
QUAD = 4
EPSILON = 1e-06
MASKED = -1e30
FAR = 1e33
F32 = jnp.float32
BF16 = jnp.bfloat16
VMEM_LIMIT = 24 * 1024 * 1024


def rows_in_use(local_rows, slots):
    counts = [0] + [side * side for side in SIDES]
    sums = {0}
    for _ in range(slots):
        sums = {a + b for a in sums for b in counts if a + b <= local_rows}
    return min(local_rows, -(-max(sums) // 16) * 16)


def dot_nn(left, right):
    return lax.dot_general(left, right, (((1,), (0,)), ((), ())), preferred_element_type=F32)


def dot_nt(left, right):
    return lax.dot_general(left, right, (((1,), (1,)), ((), ())), preferred_element_type=F32)


def norm_parts(values):
    average = jnp.mean(values, axis=-1, keepdims=True)
    centred = values - average
    variance = jnp.mean(centred * centred, axis=-1, keepdims=True)
    return centred, lax.rsqrt(variance + EPSILON)


def norm(values, gain, shift):
    centred, inverse = norm_parts(values)
    return centred * inverse * gain + shift


def norm_back(values, gain, grad):
    centred, inverse = norm_parts(values)
    unit = centred * inverse
    gain_grad = jnp.sum(grad * unit, axis=0, keepdims=True)
    shift_grad = jnp.sum(grad, axis=0, keepdims=True)
    scaled = grad * gain
    lift = jnp.mean(scaled, axis=-1, keepdims=True)
    tilt = jnp.mean(scaled * unit, axis=-1, keepdims=True)
    return inverse * (scaled - lift - unit * tilt), gain_grad, shift_grad


def own_counts(lens_ref):
    block = lax.axis_index("hd")
    return [lens_ref[0, block, i] for i in range(3)]


def layout_of(lens_ref, shape, dim):
    place = lax.broadcasted_iota(jnp.int32, shape, dim)
    count = own_counts(lens_ref)
    ends = [count[0], count[0] + count[1], count[0] + count[1] + count[2]]
    zero = jnp.zeros(shape, jnp.int32)
    segment = zero
    for end in ends:
        segment = segment + jnp.where(place >= end, 1, 0)
    sides = [
        jnp.where(c == SIDES[0] ** 2, SIDES[0], jnp.where(c == SIDES[1] ** 2, SIDES[1], SIDES[2]))
        for c in count
    ]
    start = jnp.where(segment == 0, 0, jnp.where(segment == 1, ends[0], ends[1]))
    side = jnp.where(segment == 0, sides[0], jnp.where(segment == 1, sides[1], sides[2])).astype(F32)
    offset = (place - start).astype(F32)
    row = jnp.floor((offset + 0.5) / side)
    col = offset - row * side
    valid = segment < 3
    return segment, jnp.where(valid, row, 0.0), jnp.where(valid, col, 0.0), valid


def gelu_parts(values):
    bell = jnp.exp(values * values * -0.5)
    size = jnp.abs(values) * math.sqrt(0.5)
    t = 1.0 / (1.0 + 0.3275911 * size)
    poly = t * (
        0.254829592
        + t * (-0.284496736 + t * (1.421413741 + t * (-1.453152027 + t * 1.061405429)))
    )
    tail = 0.5 * poly * bell
    below = jnp.where(values < 0, tail, 1.0 - tail)
    return values * below, below + values * bell * (1.0 / math.sqrt(2.0 * math.pi))


def smem():
    return pl.BlockSpec(memory_space=pltpu.SMEM)


def whole(shape):
    return pl.BlockSpec(shape, lambda *_: (0,) * len(shape))


def cols(rows, width, first=0):
    return pl.BlockSpec((rows, width), lambda j, *_: (0, first + j))


def rowblk(height, width, first=0):
    return pl.BlockSpec((height, width), lambda j, *_: (first + j, 0))


def cost(flops, moved):
    return pl.CostEstimate(flops=1, bytes_accessed=1, transcendentals=0)


def params(**kw):
    return pltpu.CompilerParams(vmem_limit_bytes=VMEM_LIMIT, dimension_semantics=("arbitrary",), **kw)


def attend_quad(q, k, v, add_bias, probs_ref):
    lane = lax.broadcasted_iota(jnp.int32, q.shape, 1)
    scaled = q * jnp.asarray(HDIM**-0.5, BF16)
    v_t = v.T
    outs = []
    for h in range(QUAD):
        q_h = jnp.where(lane // HDIM == h, scaled, jnp.zeros_like(scaled))
        scores = add_bias(dot_nt(k, q_h), h)
        top = jnp.max(scores, axis=0, keepdims=True)
        weights = jnp.exp(scores - top)
        total = jnp.sum(weights, axis=0, keepdims=True)
        probs = (weights * (1.0 / total)).astype(BF16)
        probs_ref[h] = probs
        outs.append(dot_nn(v_t[h * HDIM : (h + 1) * HDIM], probs))
    return jnp.concatenate(outs, axis=0).astype(BF16).T


def slope_of(group, h):
    found = 0.0
    for g in range(HEADS // QUAD):
        found = jnp.where(group == g, 2.0 ** (-8.0 * (g * QUAD + h + 1) / HEADS), found)
    return found


def self_forward_kernel(
    lens, radar, cot, gains, shifts, biases, wq, wk, wv, wo,
    n1, q_out, k_out, v_out, probs, att_out, resid, n2, gf, dist,
):
    j = pl.program_id(0)
    rows = n1.shape[0]

    @pl.when(j == 0)
    def _():
        wide = radar[...].astype(F32)
        n1[...] = norm(wide, gains[0:1], shifts[0:1]).astype(BF16)
        resid[...] = wide + biases[0:1]
        seg_k, row_k, col_k, valid = layout_of(lens, (rows, 1), 0)
        gf[...] = jnp.where(valid, cot[...], jnp.zeros_like(cot))
        seg_q, row_q, col_q, _ = layout_of(lens, (1, rows), 1)
        dr = row_k - row_q
        dc = col_k - col_q
        dist[...] = jnp.where(seg_k == seg_q, jnp.sqrt(dr * dr + dc * dc), FAR)

    x = n1[...]
    q = dot_nn(x, wq[...]).astype(BF16)
    k = dot_nn(x, wk[...]).astype(BF16)
    v = dot_nn(x, wv[...]).astype(BF16)
    q_out[...] = q
    k_out[...] = k
    v_out[...] = v
    att = attend_quad(
        q, k, v, lambda s, h: s - slope_of(j, h) * dist[...], probs
    )
    att_out[...] = att
    resid[...] += dot_nn(att, wo[...])

    @pl.when(j == pl.num_programs(0) - 1)
    def _():
        n2[...] = norm(resid[...], gains[1:2], shifts[1:2]).astype(BF16)


def cross_forward_kernel(
    lens, res_in, n_in, optic, gains, shifts, biases, wq, wk, wv, wo,
    q_out, k_out, v_out, probs, att_out, resid, n3, mask,
):
    j = pl.program_id(0)
    rows = n_in.shape[0]

    @pl.when(j == 0)
    def _():
        resid[...] = res_in[...] + biases[1:2]
        seg_k = layout_of(lens, (rows, 1), 0)[0]
        seg_q = layout_of(lens, (1, rows), 1)[0]
        mask[...] = jnp.where(seg_k == seg_q, 0.0, MASKED)

    q = dot_nn(n_in[...], wq[...]).astype(BF16)
    k = dot_nn(optic[...], wk[...]).astype(BF16)
    v = dot_nn(optic[...], wv[...]).astype(BF16)
    q_out[...] = q
    k_out[...] = k
    v_out[...] = v
    att = attend_quad(q, k, v, lambda s, h: s + mask[...], probs)
    att_out[...] = att
    resid[...] += dot_nn(att, wo[...])

    @pl.when(j == pl.num_programs(0) - 1)
    def _():
        n3[...] = norm(resid[...], gains[2:3], shifts[2:3]).astype(BF16)


def shaped(*shape, dtype=BF16):
    return jax.ShapeDtypeStruct(shape, dtype)


def held(*shape, dtype=BF16):
    return pltpu.HBM(shape, dtype)


def far(*arrays):
    return [pltpu.with_memory_space_constraint(a, pltpu.HBM) for a in arrays]


def self_forward(rows, lens, radar, cot, gains, shifts, biases, w_qkv, w_out):
    d = radar.shape[1]
    wide = QUAD * HDIM
    steps = d // wide
    return pl.pallas_call(
        self_forward_kernel,
        grid=(steps,),
        in_specs=[
            smem(), whole((rows, d)), whole((rows, d)),
            *[whole((3, d))] * 3,
            cols(d, wide), cols(d, wide, steps), cols(d, wide, 2 * steps), rowblk(wide, d),
        ],
        out_specs=[
            whole((rows, d)), cols(rows, wide), cols(rows, wide), cols(rows, wide),
            pl.BlockSpec((QUAD, rows, rows), lambda j: (j, 0, 0)),
            cols(rows, wide), whole((rows, d)), whole((rows, d)), whole((rows, d)),
        ],
        out_shape=[
            held(rows, d), held(rows, d), held(rows, d), held(rows, d),
            held(HEADS, rows, rows), held(rows, d), shaped(rows, d, dtype=F32), shaped(rows, d), held(rows, d),
        ],
        scratch_shapes=[pltpu.VMEM((rows, rows), F32)],
        compiler_params=params(),
        cost_estimate=cost(8 * rows * d * d + 12 * HEADS * rows * rows * 128, 8 * d * d + HEADS * rows * rows * 2),
        name="self_forward",
    )(lens, *far(radar, cot, gains, shifts, biases),
      *far(w_qkv, w_qkv, w_qkv, w_out))


def cross_forward(rows, lens, res_in, n_in, optic, gains, shifts, biases, w_q, w_kv, w_out):
    d = optic.shape[1]
    wide = QUAD * HDIM
    steps = d // wide
    return pl.pallas_call(
        cross_forward_kernel,
        grid=(steps,),
        in_specs=[
            smem(), whole((rows, d)), whole((rows, d)), whole((rows, d)),
            *[whole((3, d))] * 3,
            cols(d, wide), cols(d, wide), cols(d, wide, steps), rowblk(wide, d),
        ],
        out_specs=[
            cols(rows, wide), cols(rows, wide), cols(rows, wide),
            pl.BlockSpec((QUAD, rows, rows), lambda j: (j, 0, 0)),
            cols(rows, wide), whole((rows, d)), whole((rows, d)),
        ],
        out_shape=[
            held(rows, d), held(rows, d), held(rows, d),
            held(HEADS, rows, rows), held(rows, d), shaped(rows, d, dtype=F32), shaped(rows, d),
        ],
        scratch_shapes=[pltpu.VMEM((rows, rows), F32)],
        compiler_params=params(),
        cost_estimate=cost(8 * rows * d * d + 12 * HEADS * rows * rows * 128, 8 * d * d + HEADS * rows * rows * 2),
        name="cross_forward",
    )(lens, res_in, n_in, optic, gains, shifts, biases, w_q, w_kv, w_kv, w_out)


def hidden_kernel(res2, n3, gf, gains, hb, win, wout, act_out, grad_two, vectors, acc):
    j = pl.program_id(0)

    @pl.when(j == 0)
    def _():
        acc[...] = jnp.zeros_like(acc)

    act, slope = gelu_parts(dot_nn(n3[...], win[...]) + hb[...])
    act_out[...] = act.astype(BF16)
    g_pre = (dot_nt(gf[...], wout[...]) * slope).astype(BF16)
    acc[...] += dot_nt(g_pre, win[...])
    vectors[pl.ds(j, 1)] = jnp.sum(g_pre.astype(F32), axis=0, keepdims=True)

    @pl.when(j == pl.num_programs(0) - 1)
    def _():
        part, g_gain, g_shift = norm_back(res2[...], gains[2:3], acc[...])
        wide = gf[...].astype(F32)
        grad_two[...] = wide + part
        vectors[4:5] = g_gain
        vectors[5:6] = g_shift
        vectors[6:7] = jnp.sum(wide, axis=0, keepdims=True)
        vectors[7:8] = jnp.zeros_like(g_gain)


def hidden(rows, res2, n3, gf, gains, hb, win, wout):
    d = n3.shape[1]
    ff = win.shape[1]
    chunk = ff // 4
    return pl.pallas_call(
        hidden_kernel,
        grid=(4,),
        in_specs=[
            whole((rows, d)), whole((rows, d)), whole((rows, d)),
            whole((3, d)), cols(1, chunk), cols(d, chunk), rowblk(chunk, d),
        ],
        out_specs=[cols(rows, chunk), whole((rows, d)), whole((8, d))],
        out_shape=[held(rows, ff), held(rows, d, dtype=F32), held(8, d, dtype=F32)],
        scratch_shapes=[pltpu.VMEM((rows, d), F32)],
        compiler_params=params(),
        cost_estimate=cost(6 * rows * d * ff, 4 * d * ff),
        name="hidden",
    )(res2, n3, *far(gf), gains, hb, win, wout)


def output_kernel(lens, act, res2, biases, wout, y_out, acc):
    j = pl.program_id(0)
    rows = act.shape[0]

    @pl.when(j == 0)
    def _():
        acc[...] = res2[...] + biases[2:3]

    acc[...] += dot_nn(act[...], wout[...])

    @pl.when(j == pl.num_programs(0) - 1)
    def _():
        valid = layout_of(lens, (rows, 1), 0)[3]
        y_out[0:rows] = jnp.where(valid, acc[...], 0.0).astype(BF16)
        if y_out.shape[0] > rows:
            y_out[rows:] = jnp.zeros((y_out.shape[0] - rows, y_out.shape[1]), BF16)


def output(rows, local_rows, lens, act, res2, biases, wout):
    ff, d = wout.shape
    chunk = ff // 2
    return pl.pallas_call(
        output_kernel,
        grid=(2,),
        in_specs=[smem(), cols(rows, chunk), whole((rows, d)), whole((3, d)), rowblk(chunk, d)],
        out_specs=whole((local_rows, d)),
        out_shape=held(local_rows, d),
        scratch_shapes=[pltpu.VMEM((rows, d), F32)],
        compiler_params=params(),
        cost_estimate=cost(2 * rows * d * ff, 2 * d * ff),
        name="output",
    )(lens, *far(act), res2, biases, *far(wout))


def hidden_grads_kernel(blocks, meta, *refs):
    normed, grads = refs[:blocks], refs[blocks : 2 * blocks]
    hb_a, hb_b, win_a, win_b, wout_a, wout_b, dwin, dwout, acc_in, acc_out = refs[2 * blocks :]
    win = jnp.concatenate([win_a[...], win_b[...]], axis=1)
    wout = jnp.concatenate([wout_a[...], wout_b[...]], axis=0)
    hb = jnp.concatenate([hb_a[...], hb_b[...]], axis=1)
    for i in range(blocks):
        act, slope = gelu_parts(dot_nn(normed[i][...], win) + hb)
        g_pre = (dot_nt(grads[i][...], wout) * slope).astype(BF16)
        into = dot_nn(normed[i][...].T, g_pre)
        out = dot_nn(act.astype(BF16).T, grads[i][...])
        if i == 0:
            acc_in[...] = into
            acc_out[...] = out
        else:
            acc_in[...] += into
            acc_out[...] += out
    at_y, at_c, at_p = meta[0], meta[1], meta[3]
    piece = dwout.shape[2]
    for y in range(2):
        for p in range(2):
            at = (y * 2 + p) * piece
            dwout[y ^ at_y, p ^ at_p] = acc_out[at : at + piece].astype(BF16)
    piece = dwin.shape[3]
    for y in range(2):
        for c in range(2):
            for p in range(2):
                at = ((y * 2 + c) * 2 + p) * piece
                dwin[p ^ at_p, y ^ at_y, c ^ at_c] = acc_in[at : at + piece].astype(BF16)


def hidden_grads(rows, meta, normed, grads, hb, win, wout):
    d, ff = win.shape
    part = ff // 8
    blocks = len(normed)

    def wide(height, y):
        return pl.BlockSpec((height, part), lambda i, m: (0, y * 4 + m[1] * 2 + m[2]))

    def tall(y):
        return pl.BlockSpec((part, d), lambda i, m: (y * 4 + m[1] * 2 + m[2], 0))

    return pl.pallas_call(
        functools.partial(hidden_grads_kernel, blocks),
        grid_spec=pltpu.PrefetchScalarGridSpec(
            num_scalar_prefetch=1,
            grid=(1,),
            in_specs=[
                *[whole((rows, d))] * (2 * blocks),
                wide(1, 0), wide(1, 1), wide(d, 0), wide(d, 1), tall(0), tall(1),
            ],
            out_specs=[whole((2, 2, 2, d // 8, 2 * part)), whole((2, 2, part // 2, d))],
            scratch_shapes=[pltpu.VMEM((d, 2 * part), F32), pltpu.VMEM((2 * part, d), F32)],
        ),
        out_shape=[shaped(2, 2, 2, d // 8, 2 * part), shaped(2, 2, part // 2, d)],
        compiler_params=params(),
        cost_estimate=cost(16 * blocks * rows * d * part, 4 * blocks * rows * d + 4 * d * ff),
        name="hidden_grads",
    )(meta, *far(*normed, *grads, hb, hb, win, win, wout, wout))


def place(keep, send, bucket, grad, spot):
    at_hd, at_grp = lax.axis_index("hd"), lax.axis_index("grp")
    at_y, first = at_hd // 2, lax.rem(at_hd, 2) == 0
    at_x, at_p = lax.rem(at_grp, 2), lax.rem(at_grp // 2, 2)
    part = grad.shape[0] // 16
    for y in range(2):
        for x in range(2):
            for p in range(2):
                at = y * 8 + x * 2 + p
                low = grad[at * part : (at + 1) * part]
                high = grad[(at + 4) * part : (at + 5) * part]
                ways = (x ^ at_x, y ^ at_y)
                if isinstance(bucket, int):
                    lead, other = ways[bucket], ways[1 - bucket]
                else:
                    lead = jnp.where(bucket == 0, ways[0], ways[1])
                    other = jnp.where(bucket == 0, ways[1], ways[0])
                to = (bucket, lead, other, p ^ at_p, slice(None), spot)
                keep[to] = jnp.where(first, low, high)
                send[to] = jnp.where(first, high, low)


def quad_back(q, k, v, att, g_att, probs):
    lane = lax.broadcasted_iota(jnp.int32, q.shape, 1)
    nil = jnp.zeros_like(q)
    g_t = g_att.T
    k_t = k.T
    inner = g_t.astype(F32) * att.T.astype(F32)
    dq_t, dk, dv = [], 0.0, 0.0
    for h in range(QUAD):
        part = slice(h * HDIM, (h + 1) * HDIM)
        mine = lane // HDIM == h
        delta = jnp.sum(inner[part], axis=0, keepdims=True)
        v_h = jnp.where(mine, v, nil)
        p = probs[h]
        g_scores = (p.astype(F32) * (dot_nn(v_h, g_t) - delta)).astype(BF16)
        dv = dv + dot_nn(p, jnp.where(mine, g_att, nil))
        dk = dk + dot_nn(g_scores, jnp.where(mine, q, nil))
        dq_t.append(dot_nn(k_t[part], g_scores))
    scale = HDIM**-0.5
    dq = (jnp.concatenate(dq_t, axis=0) * scale).astype(BF16).T
    return dq, (dk * scale).astype(BF16), dv.astype(BF16)


def aligned(first, width):
    return pl.ds(pl.multiple_of(first, 128), width)


def cross_back_kernel(
    grad_in, res, xq, xkv, q, k, v, att, att_all, probs, gains, wo, wq, att_self,
    keep, send, dk_out, dv_out, vectors, grad_out, low, xq_t, xkv_t, acc,
):
    i = pl.program_id(0)
    d = xq.shape[1]
    wide = q.shape[1]

    @pl.when(i == 0)
    def _():
        low[...] = grad_in[...].astype(BF16)
        xq_t[...] = xq[...].T
        xkv_t[...] = xkv[...].T
        acc[...] = jnp.zeros_like(acc)
        place(keep, send, 0, dot_nn(att_all[...].T, low[...]).astype(BF16), slice(0, d))

    g_att = dot_nt(low[...], wo[...]).astype(BF16)
    dq, dk, dv = quad_back(q[...], k[...], v[...], att[...], g_att, probs)
    dk_out[...] = dk
    dv_out[...] = dv
    place(keep, send, 0, dot_nn(xq_t[...], dq).astype(BF16), aligned(d + i * wide, wide))
    place(keep, send, 1, dot_nn(xkv_t[...], dk).astype(BF16), aligned(i * wide, wide))
    place(keep, send, 1, dot_nn(xkv_t[...], dv).astype(BF16), aligned(d + i * wide, wide))
    acc[...] += dot_nt(dq, wq[...])

    @pl.when(i == pl.num_programs(0) - 1)
    def _():
        part, g_gain, g_shift = norm_back(res[...], gains[1:2], acc[...])
        grad = grad_in[...] + part
        grad_out[...] = grad
        vectors[0:1] = jnp.sum(low[...].astype(F32), axis=0, keepdims=True)
        vectors[1:2] = g_gain
        vectors[2:3] = g_shift
        grad_low = grad.astype(BF16)
        vectors[3:4] = jnp.sum(grad_low.astype(F32), axis=0, keepdims=True)
        vectors[4:8] = jnp.zeros((4, d), F32)
        out = dot_nn(att_self[...].T, grad_low).astype(BF16)
        place(keep, send, 0, out[:, : d // 2], slice(2 * d, 2 * d + d // 2))
        place(keep, send, 1, out[:, d // 2 :], slice(2 * d, 2 * d + d // 2))


def self_back_kernel(
    grad_in, xq, q, k, v, att, probs, wo, keep, send, dk_out, dv_out, dq_out, low, xq_t,
):
    i = pl.program_id(0)
    d = xq.shape[1]
    wide = q.shape[1]

    @pl.when(i == 0)
    def _():
        low[...] = grad_in[...].astype(BF16)
        xq_t[...] = xq[...].T

    g_att = dot_nt(low[...], wo[...]).astype(BF16)
    dq, dk, dv = quad_back(q[...], k[...], v[...], att[...], g_att, probs)
    dq_out[...] = dq
    dk_out[...] = dk
    dv_out[...] = dv
    place(keep, send, 0, dot_nn(xq_t[...], dq).astype(BF16), aligned(i * wide, wide))
    place(keep, send, 1, dot_nn(xq_t[...], dv).astype(BF16), aligned(i * wide, wide))
    keys = dot_nn(xq_t[...], dk).astype(BF16)
    half = wide // 2
    for t in range(2):
        piece = 2 * i + t
        bucket = jnp.where(piece * half < d // 2, 0, 1)
        at = d + piece * half - bucket * (d // 2)
        place(keep, send, bucket, keys[:, t * half : (t + 1) * half], aligned(at, half))


def cross_back(rows, grad_in, res, xq, xkv, q, k, v, att, probs, gains, wo, wq, att_self):
    d = xq.shape[1]
    wide = QUAD * HDIM
    halves = (2, 2, 2, 2, d // 16, 2 * d + d // 2)
    at = cols(rows, wide)
    full = whole((rows, d))
    return pl.pallas_call(
        cross_back_kernel,
        grid=(d // wide,),
        in_specs=[
            full, full, full, full, at, at, at, at, full,
            pl.BlockSpec((QUAD, rows, rows), lambda i: (i, 0, 0)),
            whole((3, d)), rowblk(wide, d), cols(d, wide), full,
        ],
        out_specs=[*[whole(halves)] * 2, at, at, whole((8, d)), full],
        out_shape=[
            *[shaped(*halves)] * 2, held(rows, d), held(rows, d), held(8, d, dtype=F32), held(rows, d, dtype=F32),
        ],
        scratch_shapes=[
            pltpu.VMEM((rows, d), BF16), pltpu.VMEM((d, rows), BF16), pltpu.VMEM((d, rows), BF16),
            pltpu.VMEM((rows, d), F32),
        ],
        compiler_params=params(),
        cost_estimate=cost(18 * rows * d * d + 24 * HEADS * rows * rows * 128, 16 * d * d),
        name="cross_back",
    )(grad_in, res, xq, xkv, q, k, v, att, att, *far(probs), gains, wo, wq, att_self)


def self_back(rows, grad_in, xq, q, k, v, att, probs, wo):
    d = xq.shape[1]
    wide = QUAD * HDIM
    halves = (2, 2, 2, 2, d // 16, d + d // 2)
    at = cols(rows, wide)
    full = whole((rows, d))
    return pl.pallas_call(
        self_back_kernel,
        grid=(d // wide,),
        in_specs=[
            full, full, at, at, at, at,
            pl.BlockSpec((QUAD, rows, rows), lambda i: (i, 0, 0)), rowblk(wide, d),
        ],
        out_specs=[*[whole(halves)] * 2, at, at, at],
        out_shape=[*[shaped(*halves)] * 2, held(rows, d), held(rows, d), held(rows, d)],
        scratch_shapes=[pltpu.VMEM((rows, d), BF16), pltpu.VMEM((d, rows), BF16)],
        compiler_params=params(),
        cost_estimate=cost(18 * rows * d * d + 24 * HEADS * rows * rows * 128, 16 * d * d),
        name="self_back",
    )(grad_in, xq, q, k, v, att, *far(probs), wo)


def through(parts, weights):
    total = None
    for i, part in enumerate(parts):
        d = part.shape[1]
        term = dot_nt(part[...], weights[:, i * d : (i + 1) * d])
        total = term if total is None else total + term
    return total


def store_padded(out, values):
    rows = values.shape[0]
    out[0:rows] = values
    if out.shape[0] > rows:
        out[rows:] = jnp.zeros((out.shape[0] - rows, out.shape[1]), out.dtype)


def optic_kernel(dk, dv, weights, out):
    store_padded(out, through([dk, dv], weights))


def optic(local_rows, dk, dv, weights):
    rows, d = dk.shape
    return pl.pallas_call(
        optic_kernel,
        in_specs=[whole(dk.shape), whole(dv.shape), whole(weights.shape)],
        out_specs=whole((local_rows, d)),
        out_shape=held(local_rows, d, dtype=F32),
        grid=(1,),
        compiler_params=params(),
        cost_estimate=cost(4 * rows * d * d, 4 * d * d),
        name="optic",
    )(*far(dk, dv, weights))


def radar_kernel(dq, dk, dv, weights, grad_in, radar, gains, hidden_vec, cross_vec, out, vectors):
    total = through([dq, dk, dv], weights)
    part, g_gain, g_shift = norm_back(radar[...].astype(F32), gains[0:1], total)
    store_padded(out, grad_in[...] + part)
    vectors[0:1] = g_gain
    vectors[1:2] = cross_vec[1:2]
    vectors[2:3] = hidden_vec[4:5]
    vectors[3:4] = g_shift
    vectors[4:5] = cross_vec[2:3]
    vectors[5:6] = hidden_vec[5:6]
    vectors[6:7] = cross_vec[3:4]
    vectors[7:8] = cross_vec[0:1]
    vectors[8:9] = hidden_vec[6:7]
    vectors[9:13] = hidden_vec[0:4]
    vectors[13:16] = jnp.zeros((3, out.shape[1]), F32)


def radar(local_rows, dq, dk, dv, weights, grad_in, tokens, gains, vectors):
    rows, d = dq.shape
    full = whole((rows, d))
    return pl.pallas_call(
        radar_kernel,
        grid=(1,),
        in_specs=[full, full, full, whole(weights.shape), full, full, whole((3, d)), *[whole((8, d))] * 2],
        out_specs=[whole((local_rows, d)), whole((16, d))],
        out_shape=[held(local_rows, d, dtype=F32), shaped(16, d, dtype=F32)],
        compiler_params=params(),
        cost_estimate=cost(6 * rows * d * d, 6 * d * d),
        name="radar",
    )(*far(dq, dk, dv, weights, grad_in, tokens), gains, *vectors)
def hop(values, perm):
    return lax.ppermute(values, ("grp", "hd"), perm)


def pairs(move):
    found = []
    for z in range(4):
        for x in range(2):
            for y in range(2):
                for c in range(2):
                    to = move(z, x, y, c)
                    if to is not None:
                        tz, tx, ty, tc = to
                        found.append(((z * 2 + x) * 4 + y * 2 + c, (tz * 2 + tx) * 4 + ty * 2 + tc))
    return found


ACROSS_CORE = pairs(lambda z, x, y, c: (z, x, y, 1 - c))
ACROSS_Y = pairs(lambda z, x, y, c: (z, x, 1 - y, c))
ACROSS_X = pairs(lambda z, x, y, c: (z, 1 - x, y, c))
ACROSS_P = pairs(lambda z, x, y, c: (z ^ 1, x, y, c))
ACROSS_Q = pairs(lambda z, x, y, c: (z ^ 2, x, y, c))
ACROSS_XP = pairs(lambda z, x, y, c: (z ^ 1, 1 - x, y, c))


def add(*terms):
    total = terms[0].astype(F32)
    for term in terms[1:]:
        total = total + term.astype(F32)
    return total.astype(terms[0].dtype)


def in_order(at, own, other):
    return jnp.where(at == 0, own, other), jnp.where(at == 0, other, own)


def tie(values):
    return list(lax.optimization_barrier(tuple(values)))


MOVES = {
    "C": ACROSS_CORE, "Y": ACROSS_Y, "X": ACROSS_X, "P": ACROSS_P, "Q": ACROSS_Q,
    "A": ACROSS_P, "G": ACROSS_X, "D": ACROSS_XP, "W": ACROSS_Y, "V": ACROSS_X,
    "B": ACROSS_P, "H": ACROSS_X,
}


class Flow:
    def __init__(self, value, at_x, at_p):
        self.value, self.ends, self.at_x, self.at_p = value, {}, at_x, at_p

    def operand(self, stage):
        return self.value[1] if stage in ("Y", "P") else self.value

    def absorb(self, stage, got):
        if stage in ("Y", "P"):
            self.value = add(self.value[0], got)
        elif stage == "Q":
            self.value = add(self.value, got)
        elif stage == "B":
            self.value = jnp.stack(in_order(self.at_p, self.value, got))
        else:
            self.ends[stage] = got

    def together(self):
        if "H" in self.ends:
            return in_order(self.at_x, self.value, self.ends["H"])
        rows = [
            jnp.stack(in_order(self.at_p, self.value, self.ends["A"])),
            jnp.stack(in_order(self.at_p, self.ends["G"], self.ends["D"])),
        ]
        return in_order(self.at_x, *rows)


class InFlow(Flow):
    def operand(self, stage):
        return self.value[1] if stage == "C" else super().operand(stage)

    def absorb(self, stage, got):
        if stage == "C":
            self.value = jnp.stack([self.value[0], got])
        else:
            super().absorb(stage, got)


class RowFlow(Flow):
    def __init__(self, keep, send, at_x, at_p):
        super().__init__(None, at_x, at_p)
        self.keep, self.send, self.parts = keep, send, None

    def operand(self, stage):
        if stage == "C":
            return self.send
        if stage in "XYWV":
            return self.parts[int(stage in "WV")][1]
        if stage == "P" and self.value is None:
            self.value = jnp.stack(self.parts)
        return self.value[:, 1] if stage == "P" else self.value

    def absorb(self, stage, got):
        if stage == "C":
            self.parts = [[add(self.keep[b, i], got[b, i]) for i in range(2)] for b in range(2)]
        elif stage in "XYWV":
            b = int(stage in "WV")
            self.parts[b] = add(self.parts[b][0], got)
        elif stage == "P":
            self.value = add(self.value[:, 0], got)
        else:
            super().absorb(stage, got)


class Vectors(Flow):
    def operand(self, stage):
        return self.value

    def absorb(self, stage, got):
        self.value = self.value + got


def whole_rows(keep, send, bucket, at):
    at_y, at_c, at_x, at_p = at
    lead_at, other_at = (at_x, at_y) if bucket == 0 else (at_y, at_x)
    parts = jnp.stack(in_order(at_c, keep[bucket], send[bucket]))
    for axis, place_at in ((1, lead_at), (2, other_at), (3, at_p)):
        own, other = [lax.index_in_dim(parts, i, axis, keepdims=False) for i in range(2)]
        parts = jnp.stack(in_order(place_at, own, other), axis=axis)
    order = (2, 0, 1, 3, 4, 5) if bucket == 0 else (1, 0, 2, 3, 4, 5)
    return parts.transpose(order).reshape(-1, parts.shape[-1])


def summed_anywhere(grad):
    mine = lax.psum_scatter(grad, "hd", scatter_dimension=0, tiled=True)
    return lax.psum(mine.astype(F32), "grp")


class Plan:
    def __init__(self):
        self.flows, self.flying = {}, {}

    def begin(self, gate, *moves):
        sent = [self.flows[m[0]].operand(m[1]) for m in moves]
        gate, *sent = tie([gate, *sent])
        for m, operand in zip(moves, sent):
            self.flying[m] = hop(operand, MOVES[m[1]])
        return gate

    def end(self, gate, *moves):
        gate, *got = tie([gate, *[self.flying.pop(m) for m in moves]])
        for m, value in zip(moves, got):
            self.flows[m[0]].absorb(m[1], value)
        return gate


def on_device(
    radar_tokens, optic_tokens, tile_lengths, norm_gains, norm_shifts, self_qkv, self_out,
    cross_query, cross_keyval, cross_out, hidden_in, hidden_out, proj_biases, hidden_bias, cotangent,
):
    local_rows, d = radar_tokens.shape
    ff = hidden_in.shape[1]
    known = lax.axis_size("grp") == 8 and lax.axis_size("hd") == 4
    at_hd = lax.axis_index("hd")
    at_grp = lax.axis_index("grp")
    at_y, at_c, at_z, at_x = at_hd // 2, at_hd % 2, at_grp // 2, at_grp % 2
    at_p = at_z % 2
    rows = rows_in_use(local_rows, tile_lengths.shape[2])
    hb = hidden_bias[None]

    n1, q1, k1, v1, p1, att1, res1, n2, gf = self_forward(
        rows, tile_lengths, radar_tokens, cotangent, norm_gains, norm_shifts, proj_biases, self_qkv, self_out
    )
    if known:
        n2, gf = tie([n2, gf])
        gf_x = hop(gf, ACROSS_X)
        gf_c = hop(gf, ACROSS_CORE)
    q2, k2, v2, p2, att2, res2, n3 = cross_forward(
        rows, tile_lengths, res1, n2, optic_tokens, norm_gains, norm_shifts, proj_biases,
        cross_query, cross_keyval, cross_out,
    )
    if known:
        n3, gf_x, gf_c, res2 = tie([n3, gf_x, gf_c, res2])
        gf_xc = hop(gf_x, ACROSS_CORE)
        n3_x = hop(n3, ACROSS_X)
        n3_c = hop(n3, ACROSS_CORE)
    act, grad_two, hidden_vec = hidden(rows, res2, n3, gf, norm_gains, hb, hidden_in, hidden_out)

    def cross_step(grad):
        return cross_back(
            rows, grad, res1, n2, optic_tokens, q2, k2, v2, att2, p2, norm_gains, cross_out, cross_query, att1
        )

    def self_step(grad):
        return self_back(rows, grad, n1, q1, k1, v1, att1, p1, self_out)

    def radar_step(dq, grad):
        return radar(local_rows, dq, dk1, dv1, self_qkv, grad, radar_tokens, norm_gains, [hidden_vec, cross_vec])

    if known:
        meta = jnp.stack([at_y, at_c, at_x, at_p]).astype(jnp.int32)
        act, n3_x, n3_c, gf_x, gf_c, gf_xc, grad_two = tie([act, n3_x, n3_c, gf_x, gf_c, gf_xc, grad_two])
        n3_xc = hop(n3_x, ACROSS_CORE)
        dwin, dwout = hidden_grads(
            rows, meta, [n3, n3_x, n3_c, n3_xc], [gf, gf_x, gf_c, gf_xc], hb, hidden_in, hidden_out
        )
        plan = Plan()
        grad_two, dwin, dwout = tie([grad_two, dwin, dwout])
        plan.flows["o"], plan.flows["n"] = Flow(dwout, at_x, at_p), InFlow(dwin, at_x, at_p)

        grad_two = plan.begin(grad_two, "oY", "nP")
        keep, send, dk2, dv2, cross_vec, grad_one = cross_step(grad_two)
        act = plan.end(tie([act, grad_one])[0], "oY", "nP")
        plan.flows["a"] = RowFlow(keep, send, at_x, at_p)

        act = plan.begin(act, "aC", "nY", "oP")
        layer_output = output(rows, local_rows, tile_lengths, act, res2, proj_biases, hidden_out)
        grad_one = plan.end(tie([grad_one, layer_output])[0], "aC", "nY", "oP")

        grad_one = plan.begin(grad_one, "oQ", "aX", "aW", "nC")
        keep, send, dk1, dv1, dq1 = self_step(grad_one)
        dq1 = plan.end(dq1, "oQ", "aX", "aW", "nC")
        plan.flows["c"] = RowFlow(keep, send, at_x, at_p)

        dq1 = plan.begin(dq1, "nQ", "aV", "aY", "cC", "oB")
        radar_grad, small = radar_step(dq1, grad_one)
        dk2 = plan.end(tie([dk2, radar_grad])[0], "nQ", "aV", "aY", "cC", "oB")
        plan.flows["s"] = Vectors(small, at_x, at_p)

        dk2 = plan.begin(dk2, "cX", "cW", "aP", "sC")
        optic_grad = optic(local_rows, dk2, dv2, cross_keyval)
        gate = plan.end(optic_grad, "cX", "cW", "aP", "sC")

        for stages in (
            ("cV", "aQ", "oH", "cY", "nB", "sY"),
            ("cP", "nH", "aB", "sX"),
            ("cQ", "aH", "sP"),
            ("cG", "cD", "cA", "sQ"),
        ):
            gate = plan.end(plan.begin(gate, *stages), *stages)
        optic_grad = gate

        done = {name: plan.flows[name].together() for name in "onac"}
        out_part = jnp.stack(done["o"]).reshape(-1, d).astype(F32)
        slices = [in_order(at_c, v[:, 0], v[:, 1]) for v in done["n"]]
        half = ff // 8
        in_part = jnp.concatenate(
            [
                slices[x][c][..., y * half : (y + 1) * half].reshape(-1, half)
                for y in range(2) for c in range(2) for x in range(2)
            ],
            axis=1,
        ).astype(F32)
        (cross_a, cross_b), (self_a, self_b) = [
            [jnp.stack([v[:, i] for v in done[name]]).reshape(d // 4, -1).astype(F32) for i in range(2)] for name in "ac"
        ]
        small = plan.flows["s"].value
    else:
        into, out = [], []
        for c in range(2):
            for x in range(2):
                at = jnp.asarray([0, c, x, 0], jnp.int32)
                dwin, dwout = hidden_grads(rows, at, [n3], [gf], hb, hidden_in, hidden_out)
                dwin = dwin.transpose(1, 2, 0, 3, 4)
                into.append(jnp.stack([dwin[:, c], dwin[:, 1 - c]], axis=1).reshape(d, 2, ff // 8))
                out.append(dwout.reshape(2, ff // 8, d))
        in_part = summed_anywhere(jnp.stack(into, axis=2).reshape(d, ff))
        out_part = summed_anywhere(jnp.stack(out, axis=1).reshape(ff, d))
        cross_keep, cross_send, dk2, dv2, cross_vec, grad_one = cross_step(grad_two)
        self_keep, self_send, dk1, dv1, dq1 = self_step(grad_one)
        radar_grad, small = radar_step(dq1, grad_one)
        optic_grad = optic(local_rows, dk2, dv2, cross_keyval)
        layer_output = output(rows, local_rows, tile_lengths, act, res2, proj_biases, hidden_out)
        at = (at_y, at_c, at_x, at_p)
        cross_a, cross_b = [summed_anywhere(whole_rows(cross_keep, cross_send, b, at)) for b in range(2)]
        self_a, self_b = [summed_anywhere(whole_rows(self_keep, self_send, b, at)) for b in range(2)]
        small = lax.psum(small, ("grp", "hd"))
    vectors = lax.dynamic_slice_in_dim(small[:9], at_hd * (d // 4), d // 4, 1)
    hidden_part = lax.dynamic_index_in_dim(small[9:13], at_hd, 0, keepdims=False)
    return (
        layer_output,
        radar_grad,
        optic_grad,
        jnp.concatenate([self_a, self_b[:, d:], self_b[:, :d]], axis=1),
        jnp.concatenate([cross_a[:, 2 * d :], cross_b[:, 2 * d :]], axis=1),
        cross_a[:, d : 2 * d],
        cross_b[:, : 2 * d],
        cross_a[:, :d],
        in_part,
        out_part,
        vectors[0:3],
        vectors[3:6],
        vectors[6:9],
        hidden_part,
    )


def solution(mesh):
    rows = P(("grp", "hd"), None)
    kept = P("hd", None)
    vector = P(None, "hd")
    return jax.shard_map(
        on_device,
        mesh=mesh,
        in_specs=(rows, rows, P("grp", None, None), *[P()] * 11, rows),
        out_specs=(rows, rows, rows, *[kept] * 7, vector, vector, vector, P("hd")),
        check_vma=False,
    )
```

```python
import functools
import math

import jax
import jax.numpy as jnp
import numpy as np
from jax import lax
from jax.experimental import pallas as pl
from jax.experimental.pallas import tpu as pltpu
from jax.sharding import PartitionSpec as P

HEADS = 12
HDIM = 64
SIDES = (12, 15, 20)
QUAD = 4
EPSILON = 1e-06
MASKED = -1e30
FAR = 1e33
F32 = jnp.float32
BF16 = jnp.bfloat16
VMEM_LIMIT = 24 * 1024 * 1024


def rows_in_use(local_rows, slots):
    counts = [0] + [side * side for side in SIDES]
    sums = {0}
    for _ in range(slots):
        sums = {a + b for a in sums for b in counts if a + b <= local_rows}
    return min(local_rows, -(-max(sums) // 16) * 16)


def dot_nn(left, right):
    return lax.dot_general(left, right, (((1,), (0,)), ((), ())), preferred_element_type=F32)


def dot_nt(left, right):
    return lax.dot_general(left, right, (((1,), (1,)), ((), ())), preferred_element_type=F32)


def norm_parts(values):
    average = jnp.mean(values, axis=-1, keepdims=True)
    centred = values - average
    variance = jnp.mean(centred * centred, axis=-1, keepdims=True)
    return centred, lax.rsqrt(variance + EPSILON)


def norm(values, gain, shift):
    centred, inverse = norm_parts(values)
    return centred * inverse * gain + shift


def norm_back(values, gain, grad):
    centred, inverse = norm_parts(values)
    unit = centred * inverse
    gain_grad = jnp.sum(grad * unit, axis=0, keepdims=True)
    shift_grad = jnp.sum(grad, axis=0, keepdims=True)
    scaled = grad * gain
    lift = jnp.mean(scaled, axis=-1, keepdims=True)
    tilt = jnp.mean(scaled * unit, axis=-1, keepdims=True)
    return inverse * (scaled - lift - unit * tilt), gain_grad, shift_grad


def own_counts(lens_ref):
    block = lax.axis_index("hd")
    return [lens_ref[0, block, i] for i in range(3)]


def layout_of(lens_ref, shape, dim):
    place = lax.broadcasted_iota(jnp.int32, shape, dim)
    count = own_counts(lens_ref)
    ends = [count[0], count[0] + count[1], count[0] + count[1] + count[2]]
    zero = jnp.zeros(shape, jnp.int32)
    segment = zero
    for end in ends:
        segment = segment + jnp.where(place >= end, 1, 0)
    sides = [
        jnp.where(c == SIDES[0] ** 2, SIDES[0], jnp.where(c == SIDES[1] ** 2, SIDES[1], SIDES[2]))
        for c in count
    ]
    start = jnp.where(segment == 0, 0, jnp.where(segment == 1, ends[0], ends[1]))
    side = jnp.where(segment == 0, sides[0], jnp.where(segment == 1, sides[1], sides[2])).astype(F32)
    offset = (place - start).astype(F32)
    row = jnp.floor((offset + 0.5) / side)
    col = offset - row * side
    valid = segment < 3
    return segment, jnp.where(valid, row, 0.0), jnp.where(valid, col, 0.0), valid


def gelu_parts(values):
    bell = jnp.exp(values * values * -0.5)
    size = jnp.abs(values) * math.sqrt(0.5)
    t = 1.0 / (1.0 + 0.3275911 * size)
    poly = t * (
        0.254829592
        + t * (-0.284496736 + t * (1.421413741 + t * (-1.453152027 + t * 1.061405429)))
    )
    tail = 0.5 * poly * bell
    below = jnp.where(values < 0, tail, 1.0 - tail)
    return values * below, below + values * bell * (1.0 / math.sqrt(2.0 * math.pi))


def smem():
    return pl.BlockSpec(memory_space=pltpu.SMEM)


def whole(shape):
    return pl.BlockSpec(shape, lambda *_: (0,) * len(shape))


def cols(rows, width, first=0):
    return pl.BlockSpec((rows, width), lambda j, *_: (0, first + j))


def rowblk(height, width, first=0):
    return pl.BlockSpec((height, width), lambda j, *_: (first + j, 0))


def cost(flops, moved):
    return pl.CostEstimate(flops=1, bytes_accessed=1, transcendentals=0)


def params(**kw):
    return pltpu.CompilerParams(vmem_limit_bytes=VMEM_LIMIT, dimension_semantics=("arbitrary",), **kw)


def attend_quad(q, k, v, add_bias, probs_ref):
    lane = lax.broadcasted_iota(jnp.int32, q.shape, 1)
    scaled = q * jnp.asarray(HDIM**-0.5, BF16)
    v_t = v.T
    outs = []
    for h in range(QUAD):
        q_h = jnp.where(lane // HDIM == h, scaled, jnp.zeros_like(scaled))
        scores = add_bias(dot_nt(k, q_h), h)
        top = jnp.max(scores, axis=0, keepdims=True)
        weights = jnp.exp(scores - top)
        total = jnp.sum(weights, axis=0, keepdims=True)
        probs = (weights * (1.0 / total)).astype(BF16)
        probs_ref[h] = probs
        outs.append(dot_nn(v_t[h * HDIM : (h + 1) * HDIM], probs))
    return jnp.concatenate(outs, axis=0).astype(BF16).T


def slope_of(group, h):
    found = 0.0
    for g in range(HEADS // QUAD):
        found = jnp.where(group == g, 2.0 ** (-8.0 * (g * QUAD + h + 1) / HEADS), found)
    return found


def self_forward_kernel(
    lens, radar, cot, gains, shifts, biases, wq, wk, wv, wo,
    n1, q_out, k_out, v_out, probs, att_out, resid, n2, gf, dist,
):
    j = pl.program_id(0)
    rows = n1.shape[0]

    @pl.when(j == 0)
    def _():
        wide = radar[...].astype(F32)
        n1[...] = norm(wide, gains[0:1], shifts[0:1]).astype(BF16)
        resid[...] = wide + biases[0:1]
        seg_k, row_k, col_k, valid = layout_of(lens, (rows, 1), 0)
        gf[...] = jnp.where(valid, cot[...], jnp.zeros_like(cot))
        seg_q, row_q, col_q, _ = layout_of(lens, (1, rows), 1)
        dr = row_k - row_q
        dc = col_k - col_q
        dist[...] = jnp.where(seg_k == seg_q, jnp.sqrt(dr * dr + dc * dc), FAR)

    x = n1[...]
    q = dot_nn(x, wq[...]).astype(BF16)
    k = dot_nn(x, wk[...]).astype(BF16)
    v = dot_nn(x, wv[...]).astype(BF16)
    q_out[...] = q
    k_out[...] = k
    v_out[...] = v
    att = attend_quad(
        q, k, v, lambda s, h: s - slope_of(j, h) * dist[...], probs
    )
    att_out[...] = att
    resid[...] += dot_nn(att, wo[...])

    @pl.when(j == pl.num_programs(0) - 1)
    def _():
        n2[...] = norm(resid[...], gains[1:2], shifts[1:2]).astype(BF16)


def cross_forward_kernel(
    lens, res_in, n_in, optic, gains, shifts, biases, wq, wk, wv, wo,
    q_out, k_out, v_out, probs, att_out, resid, n3, mask,
):
    j = pl.program_id(0)
    rows = n_in.shape[0]

    @pl.when(j == 0)
    def _():
        resid[...] = res_in[...] + biases[1:2]
        seg_k = layout_of(lens, (rows, 1), 0)[0]
        seg_q = layout_of(lens, (1, rows), 1)[0]
        mask[...] = jnp.where(seg_k == seg_q, 0.0, MASKED)

    q = dot_nn(n_in[...], wq[...]).astype(BF16)
    k = dot_nn(optic[...], wk[...]).astype(BF16)
    v = dot_nn(optic[...], wv[...]).astype(BF16)
    q_out[...] = q
    k_out[...] = k
    v_out[...] = v
    att = attend_quad(q, k, v, lambda s, h: s + mask[...], probs)
    att_out[...] = att
    resid[...] += dot_nn(att, wo[...])

    @pl.when(j == pl.num_programs(0) - 1)
    def _():
        n3[...] = norm(resid[...], gains[2:3], shifts[2:3]).astype(BF16)


def shaped(*shape, dtype=BF16):
    return jax.ShapeDtypeStruct(shape, dtype)


def held(*shape, dtype=BF16):
    return pltpu.HBM(shape, dtype)


def far(*arrays):
    return [pltpu.with_memory_space_constraint(a, pltpu.HBM) for a in arrays]


def self_forward(rows, lens, radar, cot, gains, shifts, biases, w_qkv, w_out):
    d = radar.shape[1]
    wide = QUAD * HDIM
    steps = d // wide
    return pl.pallas_call(
        self_forward_kernel,
        grid=(steps,),
        in_specs=[
            smem(), whole((rows, d)), whole((rows, d)),
            *[whole((3, d))] * 3,
            cols(d, wide), cols(d, wide, steps), cols(d, wide, 2 * steps), rowblk(wide, d),
        ],
        out_specs=[
            whole((rows, d)), cols(rows, wide), cols(rows, wide), cols(rows, wide),
            pl.BlockSpec((QUAD, rows, rows), lambda j: (j, 0, 0)),
            cols(rows, wide), whole((rows, d)), whole((rows, d)), whole((rows, d)),
        ],
        out_shape=[
            held(rows, d), held(rows, d), held(rows, d), held(rows, d),
            held(HEADS, rows, rows), held(rows, d), shaped(rows, d, dtype=F32), shaped(rows, d), held(rows, d),
        ],
        scratch_shapes=[pltpu.VMEM((rows, rows), F32)],
        compiler_params=params(),
        cost_estimate=cost(8 * rows * d * d + 12 * HEADS * rows * rows * 128, 8 * d * d + HEADS * rows * rows * 2),
        name="self_forward",
    )(lens, *far(radar, cot, gains, shifts, biases),
      *far(w_qkv, w_qkv, w_qkv, w_out))


def cross_forward(rows, lens, res_in, n_in, optic, gains, shifts, biases, w_q, w_kv, w_out):
    d = optic.shape[1]
    wide = QUAD * HDIM
    steps = d // wide
    return pl.pallas_call(
        cross_forward_kernel,
        grid=(steps,),
        in_specs=[
            smem(), whole((rows, d)), whole((rows, d)), whole((rows, d)),
            *[whole((3, d))] * 3,
            cols(d, wide), cols(d, wide), cols(d, wide, steps), rowblk(wide, d),
        ],
        out_specs=[
            cols(rows, wide), cols(rows, wide), cols(rows, wide),
            pl.BlockSpec((QUAD, rows, rows), lambda j: (j, 0, 0)),
            cols(rows, wide), whole((rows, d)), whole((rows, d)),
        ],
        out_shape=[
            held(rows, d), held(rows, d), held(rows, d),
            held(HEADS, rows, rows), held(rows, d), shaped(rows, d, dtype=F32), shaped(rows, d),
        ],
        scratch_shapes=[pltpu.VMEM((rows, rows), F32)],
        compiler_params=params(),
        cost_estimate=cost(8 * rows * d * d + 12 * HEADS * rows * rows * 128, 8 * d * d + HEADS * rows * rows * 2),
        name="cross_forward",
    )(lens, res_in, n_in, optic, gains, shifts, biases, w_q, w_kv, w_kv, w_out)


def hidden_kernel(res2, n3, gf, gains, hb, win, wout, act_out, grad_two, vectors, acc):
    j = pl.program_id(0)

    @pl.when(j == 0)
    def _():
        acc[...] = jnp.zeros_like(acc)

    act, slope = gelu_parts(dot_nn(n3[...], win[...]) + hb[...])
    act_out[...] = act.astype(BF16)
    g_pre = (dot_nt(gf[...], wout[...]) * slope).astype(BF16)
    acc[...] += dot_nt(g_pre, win[...])
    vectors[pl.ds(j, 1)] = jnp.sum(g_pre.astype(F32), axis=0, keepdims=True)

    @pl.when(j == pl.num_programs(0) - 1)
    def _():
        part, g_gain, g_shift = norm_back(res2[...], gains[2:3], acc[...])
        wide = gf[...].astype(F32)
        grad_two[...] = wide + part
        vectors[4:5] = g_gain
        vectors[5:6] = g_shift
        vectors[6:7] = jnp.sum(wide, axis=0, keepdims=True)
        vectors[7:8] = jnp.zeros_like(g_gain)


def hidden(rows, res2, n3, gf, gains, hb, win, wout):
    d = n3.shape[1]
    ff = win.shape[1]
    chunk = ff // 4
    return pl.pallas_call(
        hidden_kernel,
        grid=(4,),
        in_specs=[
            whole((rows, d)), whole((rows, d)), whole((rows, d)),
            whole((3, d)), cols(1, chunk), cols(d, chunk), rowblk(chunk, d),
        ],
        out_specs=[cols(rows, chunk), whole((rows, d)), whole((8, d))],
        out_shape=[held(rows, ff), held(rows, d, dtype=F32), held(8, d, dtype=F32)],
        scratch_shapes=[pltpu.VMEM((rows, d), F32)],
        compiler_params=params(),
        cost_estimate=cost(6 * rows * d * ff, 4 * d * ff),
        name="hidden",
    )(res2, n3, *far(gf), gains, hb, win, wout)


def output_kernel(lens, act, res2, biases, wout, y_out, acc):
    j = pl.program_id(0)
    rows = act.shape[0]

    @pl.when(j == 0)
    def _():
        acc[...] = res2[...] + biases[2:3]

    acc[...] += dot_nn(act[...], wout[...])

    @pl.when(j == pl.num_programs(0) - 1)
    def _():
        valid = layout_of(lens, (rows, 1), 0)[3]
        y_out[0:rows] = jnp.where(valid, acc[...], 0.0).astype(BF16)
        if y_out.shape[0] > rows:
            y_out[rows:] = jnp.zeros((y_out.shape[0] - rows, y_out.shape[1]), BF16)


def output(rows, local_rows, lens, act, res2, biases, wout):
    ff, d = wout.shape
    chunk = ff // 2
    return pl.pallas_call(
        output_kernel,
        grid=(2,),
        in_specs=[smem(), cols(rows, chunk), whole((rows, d)), whole((3, d)), rowblk(chunk, d)],
        out_specs=whole((local_rows, d)),
        out_shape=held(local_rows, d),
        scratch_shapes=[pltpu.VMEM((rows, d), F32)],
        compiler_params=params(),
        cost_estimate=cost(2 * rows * d * ff, 2 * d * ff),
        name="output",
    )(lens, *far(act), res2, biases, *far(wout))


def hidden_grads_kernel(blocks, meta, *refs):
    normed, grads = refs[:blocks], refs[blocks : 2 * blocks]
    hb_a, hb_b, win_a, win_b, wout_a, wout_b, dwin, dwout, acc_in, acc_out = refs[2 * blocks :]
    win = jnp.concatenate([win_a[...], win_b[...]], axis=1)
    wout = jnp.concatenate([wout_a[...], wout_b[...]], axis=0)
    hb = jnp.concatenate([hb_a[...], hb_b[...]], axis=1)
    for i in range(blocks):
        act, slope = gelu_parts(dot_nn(normed[i][...], win) + hb)
        g_pre = (dot_nt(grads[i][...], wout) * slope).astype(BF16)
        into = dot_nn(normed[i][...].T, g_pre)
        out = dot_nn(act.astype(BF16).T, grads[i][...])
        if i == 0:
            acc_in[...] = into
            acc_out[...] = out
        else:
            acc_in[...] += into
            acc_out[...] += out
    at_y, at_c, at_p = meta[0], meta[1], meta[3]
    piece = dwout.shape[2]
    for y in range(2):
        for p in range(2):
            at = (y * 2 + p) * piece
            dwout[y ^ at_y, p ^ at_p] = acc_out[at : at + piece].astype(BF16)
    piece = dwin.shape[3]
    for y in range(2):
        for c in range(2):
            for p in range(2):
                at = ((y * 2 + c) * 2 + p) * piece
                dwin[p ^ at_p, y ^ at_y, c ^ at_c] = acc_in[at : at + piece].astype(BF16)


def hidden_grads(rows, meta, normed, grads, hb, win, wout):
    d, ff = win.shape
    part = ff // 8
    blocks = len(normed)

    def wide(height, y):
        return pl.BlockSpec((height, part), lambda i, m: (0, y * 4 + m[1] * 2 + m[2]))

    def tall(y):
        return pl.BlockSpec((part, d), lambda i, m: (y * 4 + m[1] * 2 + m[2], 0))

    return pl.pallas_call(
        functools.partial(hidden_grads_kernel, blocks),
        grid_spec=pltpu.PrefetchScalarGridSpec(
            num_scalar_prefetch=1,
            grid=(1,),
            in_specs=[
                *[whole((rows, d))] * (2 * blocks),
                wide(1, 0), wide(1, 1), wide(d, 0), wide(d, 1), tall(0), tall(1),
            ],
            out_specs=[whole((2, 2, 2, d // 8, 2 * part)), whole((2, 2, part // 2, d))],
            scratch_shapes=[pltpu.VMEM((d, 2 * part), F32), pltpu.VMEM((2 * part, d), F32)],
        ),
        out_shape=[shaped(2, 2, 2, d // 8, 2 * part), shaped(2, 2, part // 2, d)],
        compiler_params=params(),
        cost_estimate=cost(16 * blocks * rows * d * part, 4 * blocks * rows * d + 4 * d * ff),
        name="hidden_grads",
    )(meta, *far(*normed, *grads, hb, hb, win, win, wout, wout))


def place(keep, send, bucket, grad, spot):
    at_hd, at_grp = lax.axis_index("hd"), lax.axis_index("grp")
    at_y, first = at_hd // 2, lax.rem(at_hd, 2) == 0
    at_x, at_p = lax.rem(at_grp, 2), lax.rem(at_grp // 2, 2)
    part = grad.shape[0] // 16
    for y in range(2):
        for x in range(2):
            for p in range(2):
                at = y * 8 + x * 2 + p
                low = grad[at * part : (at + 1) * part]
                high = grad[(at + 4) * part : (at + 5) * part]
                ways = (x ^ at_x, y ^ at_y)
                if isinstance(bucket, int):
                    lead, other = ways[bucket], ways[1 - bucket]
                else:
                    lead = jnp.where(bucket == 0, ways[0], ways[1])
                    other = jnp.where(bucket == 0, ways[1], ways[0])
                to = (bucket, lead, other, p ^ at_p, slice(None), spot)
                keep[to] = jnp.where(first, low, high)
                send[to] = jnp.where(first, high, low)


def quad_back(q, k, v, att, g_att, probs):
    lane = lax.broadcasted_iota(jnp.int32, q.shape, 1)
    nil = jnp.zeros_like(q)
    g_t = g_att.T
    k_t = k.T
    inner = g_t.astype(F32) * att.T.astype(F32)
    dq_t, dk, dv = [], 0.0, 0.0
    for h in range(QUAD):
        part = slice(h * HDIM, (h + 1) * HDIM)
        mine = lane // HDIM == h
        delta = jnp.sum(inner[part], axis=0, keepdims=True)
        v_h = jnp.where(mine, v, nil)
        p = probs[h]
        g_scores = (p.astype(F32) * (dot_nn(v_h, g_t) - delta)).astype(BF16)
        dv = dv + dot_nn(p, jnp.where(mine, g_att, nil))
        dk = dk + dot_nn(g_scores, jnp.where(mine, q, nil))
        dq_t.append(dot_nn(k_t[part], g_scores))
    scale = HDIM**-0.5
    dq = (jnp.concatenate(dq_t, axis=0) * scale).astype(BF16).T
    return dq, (dk * scale).astype(BF16), dv.astype(BF16)


def aligned(first, width):
    return pl.ds(pl.multiple_of(first, 128), width)


def cross_back_kernel(
    grad_in, res, xq, xkv, q, k, v, att, att_all, probs, gains, wo, wq, att_self,
    keep, send, dk_out, dv_out, vectors, grad_out, low, xq_t, xkv_t, acc,
):
    i = pl.program_id(0)
    d = xq.shape[1]
    wide = q.shape[1]

    @pl.when(i == 0)
    def _():
        low[...] = grad_in[...].astype(BF16)
        xq_t[...] = xq[...].T
        xkv_t[...] = xkv[...].T
        acc[...] = jnp.zeros_like(acc)
        place(keep, send, 0, dot_nn(att_all[...].T, low[...]).astype(BF16), slice(0, d))

    g_att = dot_nt(low[...], wo[...]).astype(BF16)
    dq, dk, dv = quad_back(q[...], k[...], v[...], att[...], g_att, probs)
    dk_out[...] = dk
    dv_out[...] = dv
    place(keep, send, 0, dot_nn(xq_t[...], dq).astype(BF16), aligned(d + i * wide, wide))
    place(keep, send, 1, dot_nn(xkv_t[...], dk).astype(BF16), aligned(i * wide, wide))
    place(keep, send, 1, dot_nn(xkv_t[...], dv).astype(BF16), aligned(d + i * wide, wide))
    acc[...] += dot_nt(dq, wq[...])

    @pl.when(i == pl.num_programs(0) - 1)
    def _():
        part, g_gain, g_shift = norm_back(res[...], gains[1:2], acc[...])
        grad = grad_in[...] + part
        grad_out[...] = grad
        vectors[0:1] = jnp.sum(low[...].astype(F32), axis=0, keepdims=True)
        vectors[1:2] = g_gain
        vectors[2:3] = g_shift
        grad_low = grad.astype(BF16)
        vectors[3:4] = jnp.sum(grad_low.astype(F32), axis=0, keepdims=True)
        vectors[4:8] = jnp.zeros((4, d), F32)
        out = dot_nn(att_self[...].T, grad_low).astype(BF16)
        place(keep, send, 0, out[:, : d // 2], slice(2 * d, 2 * d + d // 2))
        place(keep, send, 1, out[:, d // 2 :], slice(2 * d, 2 * d + d // 2))


def self_back_kernel(
    grad_in, xq, q, k, v, att, probs, wo, keep, send, dk_out, dv_out, dq_out, low, xq_t,
):
    i = pl.program_id(0)
    d = xq.shape[1]
    wide = q.shape[1]

    @pl.when(i == 0)
    def _():
        low[...] = grad_in[...].astype(BF16)
        xq_t[...] = xq[...].T

    g_att = dot_nt(low[...], wo[...]).astype(BF16)
    dq, dk, dv = quad_back(q[...], k[...], v[...], att[...], g_att, probs)
    dq_out[...] = dq
    dk_out[...] = dk
    dv_out[...] = dv
    place(keep, send, 0, dot_nn(xq_t[...], dq).astype(BF16), aligned(i * wide, wide))
    place(keep, send, 1, dot_nn(xq_t[...], dv).astype(BF16), aligned(i * wide, wide))
    keys = dot_nn(xq_t[...], dk).astype(BF16)
    half = wide // 2
    for t in range(2):
        piece = 2 * i + t
        bucket = jnp.where(piece * half < d // 2, 0, 1)
        at = d + piece * half - bucket * (d // 2)
        place(keep, send, bucket, keys[:, t * half : (t + 1) * half], aligned(at, half))


def cross_back(rows, grad_in, res, xq, xkv, q, k, v, att, probs, gains, wo, wq, att_self):
    d = xq.shape[1]
    wide = QUAD * HDIM
    halves = (2, 2, 2, 2, d // 16, 2 * d + d // 2)
    at = cols(rows, wide)
    full = whole((rows, d))
    return pl.pallas_call(
        cross_back_kernel,
        grid=(d // wide,),
        in_specs=[
            full, full, full, full, at, at, at, at, full,
            pl.BlockSpec((QUAD, rows, rows), lambda i: (i, 0, 0)),
            whole((3, d)), rowblk(wide, d), cols(d, wide), full,
        ],
        out_specs=[*[whole(halves)] * 2, at, at, whole((8, d)), full],
        out_shape=[
            *[shaped(*halves)] * 2, held(rows, d), held(rows, d), held(8, d, dtype=F32), held(rows, d, dtype=F32),
        ],
        scratch_shapes=[
            pltpu.VMEM((rows, d), BF16), pltpu.VMEM((d, rows), BF16), pltpu.VMEM((d, rows), BF16),
            pltpu.VMEM((rows, d), F32),
        ],
        compiler_params=params(),
        cost_estimate=cost(18 * rows * d * d + 24 * HEADS * rows * rows * 128, 16 * d * d),
        name="cross_back",
    )(grad_in, res, xq, xkv, q, k, v, att, att, probs, gains, wo, wq, att_self)


def self_back(rows, grad_in, xq, q, k, v, att, probs, wo):
    d = xq.shape[1]
    wide = QUAD * HDIM
    halves = (2, 2, 2, 2, d // 16, d + d // 2)
    at = cols(rows, wide)
    full = whole((rows, d))
    return pl.pallas_call(
        self_back_kernel,
        grid=(d // wide,),
        in_specs=[
            full, full, at, at, at, at,
            pl.BlockSpec((QUAD, rows, rows), lambda i: (i, 0, 0)), rowblk(wide, d),
        ],
        out_specs=[*[whole(halves)] * 2, at, at, at],
        out_shape=[*[shaped(*halves)] * 2, held(rows, d), held(rows, d), held(rows, d)],
        scratch_shapes=[pltpu.VMEM((rows, d), BF16), pltpu.VMEM((d, rows), BF16)],
        compiler_params=params(),
        cost_estimate=cost(18 * rows * d * d + 24 * HEADS * rows * rows * 128, 16 * d * d),
        name="self_back",
    )(grad_in, xq, q, k, v, att, probs, wo)


def through(parts, weights):
    total = None
    for i, part in enumerate(parts):
        d = part.shape[1]
        term = dot_nt(part[...], weights[:, i * d : (i + 1) * d])
        total = term if total is None else total + term
    return total


def store_padded(out, values):
    rows = values.shape[0]
    out[0:rows] = values
    if out.shape[0] > rows:
        out[rows:] = jnp.zeros((out.shape[0] - rows, out.shape[1]), out.dtype)


def optic_kernel(dk, dv, weights, out):
    store_padded(out, through([dk, dv], weights))


def optic(local_rows, dk, dv, weights):
    rows, d = dk.shape
    return pl.pallas_call(
        optic_kernel,
        in_specs=[whole(dk.shape), whole(dv.shape), whole(weights.shape)],
        out_specs=whole((local_rows, d)),
        out_shape=held(local_rows, d, dtype=F32),
        grid=(1,),
        compiler_params=params(),
        cost_estimate=cost(4 * rows * d * d, 4 * d * d),
        name="optic",
    )(*far(dk, dv, weights))


def radar_kernel(dq, dk, dv, weights, grad_in, radar, gains, hidden_vec, cross_vec, out, vectors):
    total = through([dq, dk, dv], weights)
    part, g_gain, g_shift = norm_back(radar[...].astype(F32), gains[0:1], total)
    store_padded(out, grad_in[...] + part)
    vectors[0:1] = g_gain
    vectors[1:2] = cross_vec[1:2]
    vectors[2:3] = hidden_vec[4:5]
    vectors[3:4] = g_shift
    vectors[4:5] = cross_vec[2:3]
    vectors[5:6] = hidden_vec[5:6]
    vectors[6:7] = cross_vec[3:4]
    vectors[7:8] = cross_vec[0:1]
    vectors[8:9] = hidden_vec[6:7]
    vectors[9:13] = hidden_vec[0:4]
    vectors[13:16] = jnp.zeros((3, out.shape[1]), F32)


def radar(local_rows, dq, dk, dv, weights, grad_in, tokens, gains, vectors):
    rows, d = dq.shape
    full = whole((rows, d))
    return pl.pallas_call(
        radar_kernel,
        grid=(1,),
        in_specs=[full, full, full, whole(weights.shape), full, full, whole((3, d)), *[whole((8, d))] * 2],
        out_specs=[whole((local_rows, d)), whole((16, d))],
        out_shape=[held(local_rows, d, dtype=F32), shaped(16, d, dtype=F32)],
        compiler_params=params(),
        cost_estimate=cost(6 * rows * d * d, 6 * d * d),
        name="radar",
    )(*far(dq, dk, dv, weights, grad_in, tokens), gains, *vectors)
def hop(values, perm):
    return lax.ppermute(values, ("grp", "hd"), perm)


def pairs(move):
    found = []
    for z in range(4):
        for x in range(2):
            for y in range(2):
                for c in range(2):
                    to = move(z, x, y, c)
                    if to is not None:
                        tz, tx, ty, tc = to
                        found.append(((z * 2 + x) * 4 + y * 2 + c, (tz * 2 + tx) * 4 + ty * 2 + tc))
    return found


ACROSS_CORE = pairs(lambda z, x, y, c: (z, x, y, 1 - c))
ACROSS_Y = pairs(lambda z, x, y, c: (z, x, 1 - y, c))
ACROSS_X = pairs(lambda z, x, y, c: (z, 1 - x, y, c))
ACROSS_P = pairs(lambda z, x, y, c: (z ^ 1, x, y, c))
ACROSS_Q = pairs(lambda z, x, y, c: (z ^ 2, x, y, c))
ACROSS_XP = pairs(lambda z, x, y, c: (z ^ 1, 1 - x, y, c))


def add(*terms):
    total = terms[0].astype(F32)
    for term in terms[1:]:
        total = total + term.astype(F32)
    return total.astype(terms[0].dtype)


def in_order(at, own, other):
    return jnp.where(at == 0, own, other), jnp.where(at == 0, other, own)


def tie(values):
    return list(lax.optimization_barrier(tuple(values)))


MOVES = {
    "C": ACROSS_CORE, "Y": ACROSS_Y, "X": ACROSS_X, "P": ACROSS_P, "Q": ACROSS_Q,
    "A": ACROSS_P, "G": ACROSS_X, "D": ACROSS_XP, "W": ACROSS_Y, "V": ACROSS_X,
    "B": ACROSS_P, "H": ACROSS_X,
}


class Flow:
    def __init__(self, value, at_x, at_p):
        self.value, self.ends, self.at_x, self.at_p = value, {}, at_x, at_p

    def operand(self, stage):
        return self.value[1] if stage in ("Y", "P") else self.value

    def absorb(self, stage, got):
        if stage in ("Y", "P"):
            self.value = add(self.value[0], got)
        elif stage == "Q":
            self.value = add(self.value, got)
        elif stage == "B":
            self.value = jnp.stack([self.value, got])
        else:
            self.ends[stage] = got

    def together(self):
        if "H" in self.ends:
            sides = [jnp.stack(in_order(self.at_p, v[0], v[1])) for v in (self.value, self.ends["H"])]
            return in_order(self.at_x, *sides)
        rows = [
            jnp.stack(in_order(self.at_p, self.value, self.ends["A"])),
            jnp.stack(in_order(self.at_p, self.ends["G"], self.ends["D"])),
        ]
        return in_order(self.at_x, *rows)


class InFlow(Flow):
    def operand(self, stage):
        return self.value[1] if stage == "C" else super().operand(stage)

    def absorb(self, stage, got):
        if stage == "C":
            self.value = jnp.stack([self.value[0], got])
        else:
            super().absorb(stage, got)


class RowFlow(Flow):
    def __init__(self, keep, send, at_x, at_p):
        super().__init__(None, at_x, at_p)
        self.keep, self.send, self.parts = keep, send, None

    def operand(self, stage):
        if stage == "C":
            return self.send
        if stage in "XYWV":
            return self.parts[int(stage in "WV")][1]
        if stage == "P" and self.value is None:
            self.value = jnp.stack(self.parts)
        return self.value[:, 1] if stage == "P" else self.value

    def absorb(self, stage, got):
        if stage == "C":
            self.parts = [[add(self.keep[b, i], got[b, i]) for i in range(2)] for b in range(2)]
        elif stage in "XYWV":
            b = int(stage in "WV")
            self.parts[b] = add(self.parts[b][0], got)
        elif stage == "P":
            self.value = add(self.value[:, 0], got)
        else:
            super().absorb(stage, got)


class Vectors(Flow):
    def operand(self, stage):
        return self.value

    def absorb(self, stage, got):
        self.value = self.value + got


def whole_rows(keep, send, bucket, at):
    at_y, at_c, at_x, at_p = at
    lead_at, other_at = (at_x, at_y) if bucket == 0 else (at_y, at_x)
    parts = jnp.stack(in_order(at_c, keep[bucket], send[bucket]))
    for axis, place_at in ((1, lead_at), (2, other_at), (3, at_p)):
        own, other = [lax.index_in_dim(parts, i, axis, keepdims=False) for i in range(2)]
        parts = jnp.stack(in_order(place_at, own, other), axis=axis)
    order = (2, 0, 1, 3, 4, 5) if bucket == 0 else (1, 0, 2, 3, 4, 5)
    return parts.transpose(order).reshape(-1, parts.shape[-1])


def summed_anywhere(grad):
    mine = lax.psum_scatter(grad, "hd", scatter_dimension=0, tiled=True)
    return lax.psum(mine.astype(F32), "grp")


class Plan:
    def __init__(self):
        self.flows, self.flying = {}, {}

    def begin(self, gate, *moves):
        sent = [self.flows[m[0]].operand(m[1]) for m in moves]
        gate, *sent = tie([gate, *sent])
        for m, operand in zip(moves, sent):
            self.flying[m] = hop(operand, MOVES[m[1]])
        return gate

    def end(self, gate, *moves):
        gate, *got = tie([gate, *[self.flying.pop(m) for m in moves]])
        for m, value in zip(moves, got):
            self.flows[m[0]].absorb(m[1], value)
        return gate


def on_device(
    radar_tokens, optic_tokens, tile_lengths, norm_gains, norm_shifts, self_qkv, self_out,
    cross_query, cross_keyval, cross_out, hidden_in, hidden_out, proj_biases, hidden_bias, cotangent,
):
    local_rows, d = radar_tokens.shape
    ff = hidden_in.shape[1]
    known = lax.axis_size("grp") == 8 and lax.axis_size("hd") == 4
    at_hd = lax.axis_index("hd")
    at_grp = lax.axis_index("grp")
    at_y, at_c, at_z, at_x = at_hd // 2, at_hd % 2, at_grp // 2, at_grp % 2
    at_p = at_z % 2
    rows = rows_in_use(local_rows, tile_lengths.shape[2])
    hb = hidden_bias[None]

    n1, q1, k1, v1, p1, att1, res1, n2, gf = self_forward(
        rows, tile_lengths, radar_tokens, cotangent, norm_gains, norm_shifts, proj_biases, self_qkv, self_out
    )
    if known:
        n2, gf = tie([n2, gf])
        gf_x = hop(gf, ACROSS_X)
        gf_c = hop(gf, ACROSS_CORE)
    q2, k2, v2, p2, att2, res2, n3 = cross_forward(
        rows, tile_lengths, res1, n2, optic_tokens, norm_gains, norm_shifts, proj_biases,
        cross_query, cross_keyval, cross_out,
    )
    if known:
        n3, gf_x, gf_c, res2 = tie([n3, gf_x, gf_c, res2])
        gf_xc = hop(gf_x, ACROSS_CORE)
        n3_x = hop(n3, ACROSS_X)
        n3_c = hop(n3, ACROSS_CORE)
    act, grad_two, hidden_vec = hidden(rows, res2, n3, gf, norm_gains, hb, hidden_in, hidden_out)

    def cross_step(grad):
        return cross_back(
            rows, grad, res1, n2, optic_tokens, q2, k2, v2, att2, p2, norm_gains, cross_out, cross_query, att1
        )

    def self_step(grad):
        return self_back(rows, grad, n1, q1, k1, v1, att1, p1, self_out)

    def radar_step(dq, grad):
        return radar(local_rows, dq, dk1, dv1, self_qkv, grad, radar_tokens, norm_gains, [hidden_vec, cross_vec])

    if known:
        meta = jnp.stack([at_y, at_c, at_x, at_p]).astype(jnp.int32)
        act, n3_x, n3_c, gf_x, gf_c, gf_xc, grad_two = tie([act, n3_x, n3_c, gf_x, gf_c, gf_xc, grad_two])
        n3_xc = hop(n3_x, ACROSS_CORE)
        dwin, dwout = hidden_grads(
            rows, meta, [n3, n3_x, n3_c, n3_xc], [gf, gf_x, gf_c, gf_xc], hb, hidden_in, hidden_out
        )
        plan = Plan()
        grad_two, dwin, dwout = tie([grad_two, dwin, dwout])
        plan.flows["o"], plan.flows["n"] = Flow(dwout, at_x, at_p), InFlow(dwin, at_x, at_p)

        grad_two = plan.begin(grad_two, "oY", "nP")
        keep, send, dk2, dv2, cross_vec, grad_one = cross_step(grad_two)
        act = plan.end(tie([act, grad_one])[0], "oY", "nP")
        plan.flows["a"] = RowFlow(keep, send, at_x, at_p)

        act = plan.begin(act, "aC", "nY", "oP")
        layer_output = output(rows, local_rows, tile_lengths, act, res2, proj_biases, hidden_out)
        grad_one = plan.end(tie([grad_one, layer_output])[0], "aC", "nY", "oP")

        grad_one = plan.begin(grad_one, "oQ", "aX", "aW", "nC")
        keep, send, dk1, dv1, dq1 = self_step(grad_one)
        dq1 = plan.end(dq1, "oQ", "aX", "aW", "nC")
        plan.flows["c"] = RowFlow(keep, send, at_x, at_p)

        dq1 = plan.begin(dq1, "nQ", "aV", "aY", "cC", "oB")
        radar_grad, small = radar_step(dq1, grad_one)
        dk2 = plan.end(tie([dk2, radar_grad])[0], "nQ", "aV", "aY", "cC", "oB")
        plan.flows["s"] = Vectors(small, at_x, at_p)

        dk2 = plan.begin(dk2, "cX", "cW", "aP", "sC")
        optic_grad = optic(local_rows, dk2, dv2, cross_keyval)
        gate = plan.end(optic_grad, "cX", "cW", "aP", "sC")

        for stages in (
            ("cV", "aQ", "oH", "cY", "nB", "sY"),
            ("cP", "nH", "aB", "sX"),
            ("cQ", "aH", "sP"),
            ("cG", "cD", "cA", "sQ"),
        ):
            gate = plan.end(plan.begin(gate, *stages), *stages)
        optic_grad = gate

        done = {name: plan.flows[name].together() for name in "onac"}
        out_part = jnp.stack(done["o"]).reshape(-1, d).astype(F32)
        slices = [in_order(at_c, v[:, 0], v[:, 1]) for v in done["n"]]
        half = ff // 8
        in_part = jnp.concatenate(
            [
                slices[x][c][..., y * half : (y + 1) * half].reshape(-1, half)
                for y in range(2) for c in range(2) for x in range(2)
            ],
            axis=1,
        ).astype(F32)
        (cross_a, cross_b), (self_a, self_b) = [
            [jnp.stack([v[:, i] for v in done[name]]).reshape(d // 4, -1).astype(F32) for i in range(2)] for name in "ac"
        ]
        small = plan.flows["s"].value
    else:
        into, out = [], []
        for c in range(2):
            for x in range(2):
                at = jnp.asarray([0, c, x, 0], jnp.int32)
                dwin, dwout = hidden_grads(rows, at, [n3], [gf], hb, hidden_in, hidden_out)
                dwin = dwin.transpose(1, 2, 0, 3, 4)
                into.append(jnp.stack([dwin[:, c], dwin[:, 1 - c]], axis=1).reshape(d, 2, ff // 8))
                out.append(dwout.reshape(2, ff // 8, d))
        in_part = summed_anywhere(jnp.stack(into, axis=2).reshape(d, ff))
        out_part = summed_anywhere(jnp.stack(out, axis=1).reshape(ff, d))
        cross_keep, cross_send, dk2, dv2, cross_vec, grad_one = cross_step(grad_two)
        self_keep, self_send, dk1, dv1, dq1 = self_step(grad_one)
        radar_grad, small = radar_step(dq1, grad_one)
        optic_grad = optic(local_rows, dk2, dv2, cross_keyval)
        layer_output = output(rows, local_rows, tile_lengths, act, res2, proj_biases, hidden_out)
        at = (at_y, at_c, at_x, at_p)
        cross_a, cross_b = [summed_anywhere(whole_rows(cross_keep, cross_send, b, at)) for b in range(2)]
        self_a, self_b = [summed_anywhere(whole_rows(self_keep, self_send, b, at)) for b in range(2)]
        small = lax.psum(small, ("grp", "hd"))
    vectors = lax.dynamic_slice_in_dim(small[:9], at_hd * (d // 4), d // 4, 1)
    hidden_part = lax.dynamic_index_in_dim(small[9:13], at_hd, 0, keepdims=False)
    return (
        layer_output,
        radar_grad,
        optic_grad,
        jnp.concatenate([self_a, self_b[:, d:], self_b[:, :d]], axis=1),
        jnp.concatenate([cross_a[:, 2 * d :], cross_b[:, 2 * d :]], axis=1),
        cross_a[:, d : 2 * d],
        cross_b[:, : 2 * d],
        cross_a[:, :d],
        in_part,
        out_part,
        vectors[0:3],
        vectors[3:6],
        vectors[6:9],
        hidden_part,
    )


def solution(mesh):
    rows = P(("grp", "hd"), None)
    kept = P("hd", None)
    vector = P(None, "hd")
    return jax.shard_map(
        on_device,
        mesh=mesh,
        in_specs=(rows, rows, P("grp", None, None), *[P()] * 11, rows),
        out_specs=(rows, rows, rows, *[kept] * 7, vector, vector, vector, P("hd")),
        check_vma=False,
    )
```

```python
import functools
import math

import jax
import jax.numpy as jnp
import numpy as np
from jax import lax
from jax.experimental import pallas as pl
from jax.experimental.pallas import tpu as pltpu
from jax.sharding import PartitionSpec as P

HEADS = 12
HDIM = 64
SIDES = (12, 15, 20)
QUAD = 4
EPSILON = 1e-06
MASKED = -1e30
FAR = 1e33
F32 = jnp.float32
BF16 = jnp.bfloat16
VMEM_LIMIT = 24 * 1024 * 1024


def rows_in_use(local_rows, slots):
    counts = [0] + [side * side for side in SIDES]
    sums = {0}
    for _ in range(slots):
        sums = {a + b for a in sums for b in counts if a + b <= local_rows}
    return min(local_rows, -(-max(sums) // 16) * 16)


def dot_nn(left, right):
    return lax.dot_general(left, right, (((1,), (0,)), ((), ())), preferred_element_type=F32)


def dot_nt(left, right):
    return lax.dot_general(left, right, (((1,), (1,)), ((), ())), preferred_element_type=F32)


def norm_parts(values):
    average = jnp.mean(values, axis=-1, keepdims=True)
    centred = values - average
    variance = jnp.mean(centred * centred, axis=-1, keepdims=True)
    return centred, lax.rsqrt(variance + EPSILON)


def norm(values, gain, shift):
    centred, inverse = norm_parts(values)
    return centred * inverse * gain + shift


def norm_back(values, gain, grad):
    centred, inverse = norm_parts(values)
    unit = centred * inverse
    gain_grad = jnp.sum(grad * unit, axis=0, keepdims=True)
    shift_grad = jnp.sum(grad, axis=0, keepdims=True)
    scaled = grad * gain
    lift = jnp.mean(scaled, axis=-1, keepdims=True)
    tilt = jnp.mean(scaled * unit, axis=-1, keepdims=True)
    return inverse * (scaled - lift - unit * tilt), gain_grad, shift_grad


def own_counts(lens_ref):
    block = lax.axis_index("hd")
    return [lens_ref[0, block, i] for i in range(3)]


def layout_of(lens_ref, shape, dim):
    place = lax.broadcasted_iota(jnp.int32, shape, dim)
    count = own_counts(lens_ref)
    ends = [count[0], count[0] + count[1], count[0] + count[1] + count[2]]
    zero = jnp.zeros(shape, jnp.int32)
    segment = zero
    for end in ends:
        segment = segment + jnp.where(place >= end, 1, 0)
    sides = [
        jnp.where(c == SIDES[0] ** 2, SIDES[0], jnp.where(c == SIDES[1] ** 2, SIDES[1], SIDES[2]))
        for c in count
    ]
    start = jnp.where(segment == 0, 0, jnp.where(segment == 1, ends[0], ends[1]))
    side = jnp.where(segment == 0, sides[0], jnp.where(segment == 1, sides[1], sides[2])).astype(F32)
    offset = (place - start).astype(F32)
    row = jnp.floor((offset + 0.5) / side)
    col = offset - row * side
    valid = segment < 3
    return segment, jnp.where(valid, row, 0.0), jnp.where(valid, col, 0.0), valid


def gelu_parts(values):
    bell = jnp.exp(values * values * -0.5)
    size = jnp.abs(values) * math.sqrt(0.5)
    t = 1.0 / (1.0 + 0.3275911 * size)
    poly = t * (
        0.254829592
        + t * (-0.284496736 + t * (1.421413741 + t * (-1.453152027 + t * 1.061405429)))
    )
    tail = 0.5 * poly * bell
    below = jnp.where(values < 0, tail, 1.0 - tail)
    return values * below, below + values * bell * (1.0 / math.sqrt(2.0 * math.pi))


def smem():
    return pl.BlockSpec(memory_space=pltpu.SMEM)


def whole(shape):
    return pl.BlockSpec(shape, lambda *_: (0,) * len(shape))


def cols(rows, width, first=0):
    return pl.BlockSpec((rows, width), lambda j, *_: (0, first + j))


def rowblk(height, width, first=0):
    return pl.BlockSpec((height, width), lambda j, *_: (first + j, 0))


def cost(flops, moved):
    return pl.CostEstimate(flops=1, bytes_accessed=1, transcendentals=0)


def params(**kw):
    return pltpu.CompilerParams(vmem_limit_bytes=VMEM_LIMIT, dimension_semantics=("arbitrary",), **kw)


def attend_quad(q, k, v, add_bias, probs_ref):
    lane = lax.broadcasted_iota(jnp.int32, q.shape, 1)
    scaled = q * jnp.asarray(HDIM**-0.5, BF16)
    v_t = v.T
    outs = []
    for h in range(QUAD):
        q_h = jnp.where(lane // HDIM == h, scaled, jnp.zeros_like(scaled))
        scores = add_bias(dot_nt(k, q_h), h)
        top = jnp.max(scores, axis=0, keepdims=True)
        weights = jnp.exp(scores - top)
        total = jnp.sum(weights, axis=0, keepdims=True)
        probs = (weights * (1.0 / total)).astype(BF16)
        probs_ref[h] = probs
        outs.append(dot_nn(v_t[h * HDIM : (h + 1) * HDIM], probs))
    return jnp.concatenate(outs, axis=0).astype(BF16).T


def slope_of(group, h):
    found = 0.0
    for g in range(HEADS // QUAD):
        found = jnp.where(group == g, 2.0 ** (-8.0 * (g * QUAD + h + 1) / HEADS), found)
    return found


def self_forward_kernel(
    lens, radar, cot, gains, shifts, biases, wq, wk, wv, wo,
    n1, q_out, k_out, v_out, probs, att_out, resid, n2, gf, dist,
):
    j = pl.program_id(0)
    rows = n1.shape[0]

    @pl.when(j == 0)
    def _():
        wide = radar[...].astype(F32)
        n1[...] = norm(wide, gains[0:1], shifts[0:1]).astype(BF16)
        resid[...] = wide + biases[0:1]
        seg_k, row_k, col_k, valid = layout_of(lens, (rows, 1), 0)
        gf[...] = jnp.where(valid, cot[...], jnp.zeros_like(cot))
        seg_q, row_q, col_q, _ = layout_of(lens, (1, rows), 1)
        dr = row_k - row_q
        dc = col_k - col_q
        dist[...] = jnp.where(seg_k == seg_q, jnp.sqrt(dr * dr + dc * dc), FAR)

    x = n1[...]
    q = dot_nn(x, wq[...]).astype(BF16)
    k = dot_nn(x, wk[...]).astype(BF16)
    v = dot_nn(x, wv[...]).astype(BF16)
    q_out[...] = q
    k_out[...] = k
    v_out[...] = v
    att = attend_quad(
        q, k, v, lambda s, h: s - slope_of(j, h) * dist[...], probs
    )
    att_out[...] = att
    resid[...] += dot_nn(att, wo[...])

    @pl.when(j == pl.num_programs(0) - 1)
    def _():
        n2[...] = norm(resid[...], gains[1:2], shifts[1:2]).astype(BF16)


def cross_forward_kernel(
    lens, res_in, n_in, optic, gains, shifts, biases, wq, wk, wv, wo,
    q_out, k_out, v_out, probs, att_out, resid, n3, mask,
):
    j = pl.program_id(0)
    rows = n_in.shape[0]

    @pl.when(j == 0)
    def _():
        resid[...] = res_in[...] + biases[1:2]
        seg_k = layout_of(lens, (rows, 1), 0)[0]
        seg_q = layout_of(lens, (1, rows), 1)[0]
        mask[...] = jnp.where(seg_k == seg_q, 0.0, MASKED)

    q = dot_nn(n_in[...], wq[...]).astype(BF16)
    k = dot_nn(optic[...], wk[...]).astype(BF16)
    v = dot_nn(optic[...], wv[...]).astype(BF16)
    q_out[...] = q
    k_out[...] = k
    v_out[...] = v
    att = attend_quad(q, k, v, lambda s, h: s + mask[...], probs)
    att_out[...] = att
    resid[...] += dot_nn(att, wo[...])

    @pl.when(j == pl.num_programs(0) - 1)
    def _():
        n3[...] = norm(resid[...], gains[2:3], shifts[2:3]).astype(BF16)


def shaped(*shape, dtype=BF16):
    return jax.ShapeDtypeStruct(shape, dtype)


def held(*shape, dtype=BF16):
    return pltpu.HBM(shape, dtype)


def far(*arrays):
    return [pltpu.with_memory_space_constraint(a, pltpu.HBM) for a in arrays]


def self_forward(rows, lens, radar, cot, gains, shifts, biases, w_qkv, w_out):
    d = radar.shape[1]
    wide = QUAD * HDIM
    steps = d // wide
    return pl.pallas_call(
        self_forward_kernel,
        grid=(steps,),
        in_specs=[
            smem(), whole((rows, d)), whole((rows, d)),
            *[whole((3, d))] * 3,
            cols(d, wide), cols(d, wide, steps), cols(d, wide, 2 * steps), rowblk(wide, d),
        ],
        out_specs=[
            whole((rows, d)), cols(rows, wide), cols(rows, wide), cols(rows, wide),
            pl.BlockSpec((QUAD, rows, rows), lambda j: (j, 0, 0)),
            cols(rows, wide), whole((rows, d)), whole((rows, d)), whole((rows, d)),
        ],
        out_shape=[
            held(rows, d), held(rows, d), held(rows, d), held(rows, d),
            held(HEADS, rows, rows), held(rows, d), shaped(rows, d, dtype=F32), shaped(rows, d), held(rows, d),
        ],
        scratch_shapes=[pltpu.VMEM((rows, rows), F32)],
        compiler_params=params(),
        cost_estimate=cost(8 * rows * d * d + 12 * HEADS * rows * rows * 128, 8 * d * d + HEADS * rows * rows * 2),
        name="self_forward",
    )(lens, *far(radar, cot, gains, shifts, biases),
      *far(w_qkv, w_qkv, w_qkv, w_out))


def cross_forward(rows, lens, res_in, n_in, optic, gains, shifts, biases, w_q, w_kv, w_out):
    d = optic.shape[1]
    wide = QUAD * HDIM
    steps = d // wide
    return pl.pallas_call(
        cross_forward_kernel,
        grid=(steps,),
        in_specs=[
            smem(), whole((rows, d)), whole((rows, d)), whole((rows, d)),
            *[whole((3, d))] * 3,
            cols(d, wide), cols(d, wide), cols(d, wide, steps), rowblk(wide, d),
        ],
        out_specs=[
            cols(rows, wide), cols(rows, wide), cols(rows, wide),
            pl.BlockSpec((QUAD, rows, rows), lambda j: (j, 0, 0)),
            cols(rows, wide), whole((rows, d)), whole((rows, d)),
        ],
        out_shape=[
            held(rows, d), held(rows, d), held(rows, d),
            held(HEADS, rows, rows), held(rows, d), shaped(rows, d, dtype=F32), shaped(rows, d),
        ],
        scratch_shapes=[pltpu.VMEM((rows, rows), F32)],
        compiler_params=params(),
        cost_estimate=cost(8 * rows * d * d + 12 * HEADS * rows * rows * 128, 8 * d * d + HEADS * rows * rows * 2),
        name="cross_forward",
    )(lens, res_in, n_in, optic, gains, shifts, biases, w_q, w_kv, w_kv, w_out)


def hidden_kernel(res2, n3, gf, gains, hb, win, wout, act_out, grad_two, vectors, acc):
    j = pl.program_id(0)

    @pl.when(j == 0)
    def _():
        acc[...] = jnp.zeros_like(acc)

    act, slope = gelu_parts(dot_nn(n3[...], win[...]) + hb[...])
    act_out[...] = act.astype(BF16)
    g_pre = (dot_nt(gf[...], wout[...]) * slope).astype(BF16)
    acc[...] += dot_nt(g_pre, win[...])
    vectors[pl.ds(j, 1)] = jnp.sum(g_pre.astype(F32), axis=0, keepdims=True)

    @pl.when(j == pl.num_programs(0) - 1)
    def _():
        part, g_gain, g_shift = norm_back(res2[...], gains[2:3], acc[...])
        wide = gf[...].astype(F32)
        grad_two[...] = wide + part
        vectors[4:5] = g_gain
        vectors[5:6] = g_shift
        vectors[6:7] = jnp.sum(wide, axis=0, keepdims=True)
        vectors[7:8] = jnp.zeros_like(g_gain)


def hidden(rows, res2, n3, gf, gains, hb, win, wout):
    d = n3.shape[1]
    ff = win.shape[1]
    chunk = ff // 4
    return pl.pallas_call(
        hidden_kernel,
        grid=(4,),
        in_specs=[
            whole((rows, d)), whole((rows, d)), whole((rows, d)),
            whole((3, d)), cols(1, chunk), cols(d, chunk), rowblk(chunk, d),
        ],
        out_specs=[cols(rows, chunk), whole((rows, d)), whole((8, d))],
        out_shape=[held(rows, ff), held(rows, d, dtype=F32), held(8, d, dtype=F32)],
        scratch_shapes=[pltpu.VMEM((rows, d), F32)],
        compiler_params=params(),
        cost_estimate=cost(6 * rows * d * ff, 4 * d * ff),
        name="hidden",
    )(res2, n3, *far(gf), gains, hb, win, wout)


def output_kernel(lens, act, res2, biases, wout, y_out, acc):
    j = pl.program_id(0)
    rows = act.shape[0]

    @pl.when(j == 0)
    def _():
        acc[...] = res2[...] + biases[2:3]

    acc[...] += dot_nn(act[...], wout[...])

    @pl.when(j == pl.num_programs(0) - 1)
    def _():
        valid = layout_of(lens, (rows, 1), 0)[3]
        y_out[0:rows] = jnp.where(valid, acc[...], 0.0).astype(BF16)
        if y_out.shape[0] > rows:
            y_out[rows:] = jnp.zeros((y_out.shape[0] - rows, y_out.shape[1]), BF16)


def output(rows, local_rows, lens, act, res2, biases, wout):
    ff, d = wout.shape
    chunk = ff // 2
    return pl.pallas_call(
        output_kernel,
        grid=(2,),
        in_specs=[smem(), cols(rows, chunk), whole((rows, d)), whole((3, d)), rowblk(chunk, d)],
        out_specs=whole((local_rows, d)),
        out_shape=held(local_rows, d),
        scratch_shapes=[pltpu.VMEM((rows, d), F32)],
        compiler_params=params(),
        cost_estimate=cost(2 * rows * d * ff, 2 * d * ff),
        name="output",
    )(lens, *far(act), res2, biases, *far(wout))


def hidden_grads_kernel(blocks, meta, *refs):
    normed, grads = refs[:blocks], refs[blocks : 2 * blocks]
    hb_a, hb_b, win_a, win_b, wout_a, wout_b, dwin, dwout, acc_in, acc_out = refs[2 * blocks :]
    win = jnp.concatenate([win_a[...], win_b[...]], axis=1)
    wout = jnp.concatenate([wout_a[...], wout_b[...]], axis=0)
    hb = jnp.concatenate([hb_a[...], hb_b[...]], axis=1)
    for i in range(blocks):
        act, slope = gelu_parts(dot_nn(normed[i][...], win) + hb)
        g_pre = (dot_nt(grads[i][...], wout) * slope).astype(BF16)
        into = dot_nn(normed[i][...].T, g_pre)
        out = dot_nn(act.astype(BF16).T, grads[i][...])
        if i == 0:
            acc_in[...] = into
            acc_out[...] = out
        else:
            acc_in[...] += into
            acc_out[...] += out
    at_y, at_c, at_p = meta[0], meta[1], meta[3]
    piece = dwout.shape[2]
    for y in range(2):
        for p in range(2):
            at = (y * 2 + p) * piece
            dwout[y ^ at_y, p ^ at_p] = acc_out[at : at + piece].astype(BF16)
    piece = dwin.shape[3]
    for y in range(2):
        for c in range(2):
            for p in range(2):
                at = ((y * 2 + c) * 2 + p) * piece
                dwin[p ^ at_p, y ^ at_y, c ^ at_c] = acc_in[at : at + piece].astype(BF16)


def hidden_grads(rows, meta, normed, grads, hb, win, wout):
    d, ff = win.shape
    part = ff // 8
    blocks = len(normed)

    def wide(height, y):
        return pl.BlockSpec((height, part), lambda i, m: (0, y * 4 + m[1] * 2 + m[2]))

    def tall(y):
        return pl.BlockSpec((part, d), lambda i, m: (y * 4 + m[1] * 2 + m[2], 0))

    return pl.pallas_call(
        functools.partial(hidden_grads_kernel, blocks),
        grid_spec=pltpu.PrefetchScalarGridSpec(
            num_scalar_prefetch=1,
            grid=(1,),
            in_specs=[
                *[whole((rows, d))] * (2 * blocks),
                wide(1, 0), wide(1, 1), wide(d, 0), wide(d, 1), tall(0), tall(1),
            ],
            out_specs=[whole((2, 2, 2, d // 8, 2 * part)), whole((2, 2, part // 2, d))],
            scratch_shapes=[pltpu.VMEM((d, 2 * part), F32), pltpu.VMEM((2 * part, d), F32)],
        ),
        out_shape=[shaped(2, 2, 2, d // 8, 2 * part), shaped(2, 2, part // 2, d)],
        compiler_params=params(),
        cost_estimate=cost(16 * blocks * rows * d * part, 4 * blocks * rows * d + 4 * d * ff),
        name="hidden_grads",
    )(meta, *far(*normed, *grads, hb, hb, win, win, wout, wout))


def place(keep, send, bucket, grad, spot):
    at_hd, at_grp = lax.axis_index("hd"), lax.axis_index("grp")
    at_y, first = at_hd // 2, lax.rem(at_hd, 2) == 0
    at_x, at_p = lax.rem(at_grp, 2), lax.rem(at_grp // 2, 2)
    part = grad.shape[0] // 16
    for y in range(2):
        for x in range(2):
            for p in range(2):
                at = y * 8 + x * 2 + p
                low = grad[at * part : (at + 1) * part]
                high = grad[(at + 4) * part : (at + 5) * part]
                ways = (x ^ at_x, y ^ at_y)
                if isinstance(bucket, int):
                    lead, other = ways[bucket], ways[1 - bucket]
                else:
                    lead = jnp.where(bucket == 0, ways[0], ways[1])
                    other = jnp.where(bucket == 0, ways[1], ways[0])
                to = (bucket, lead, other, p ^ at_p, slice(None), spot)
                keep[to] = jnp.where(first, low, high)
                send[to] = jnp.where(first, high, low)


def quad_back(q, k, v, att, g_att, probs):
    lane = lax.broadcasted_iota(jnp.int32, q.shape, 1)
    nil = jnp.zeros_like(q)
    g_t = g_att.T
    k_t = k.T
    inner = g_t.astype(F32) * att.T.astype(F32)
    dq_t, dk, dv = [], 0.0, 0.0
    for h in range(QUAD):
        part = slice(h * HDIM, (h + 1) * HDIM)
        mine = lane // HDIM == h
        delta = jnp.sum(inner[part], axis=0, keepdims=True)
        v_h = jnp.where(mine, v, nil)
        p = probs[h]
        g_scores = (p.astype(F32) * (dot_nn(v_h, g_t) - delta)).astype(BF16)
        dv = dv + dot_nn(p, jnp.where(mine, g_att, nil))
        dk = dk + dot_nn(g_scores, jnp.where(mine, q, nil))
        dq_t.append(dot_nn(k_t[part], g_scores))
    scale = HDIM**-0.5
    dq = (jnp.concatenate(dq_t, axis=0) * scale).astype(BF16).T
    return dq, (dk * scale).astype(BF16), dv.astype(BF16)


def aligned(first, width):
    return pl.ds(pl.multiple_of(first, 128), width)


def cross_back_kernel(
    grad_in, res, xq, xkv, q, k, v, att, att_all, probs, gains, wo, wq, att_self,
    keep, send, dk_out, dv_out, vectors, grad_out, low, xq_t, xkv_t, acc,
):
    i = pl.program_id(0)
    d = xq.shape[1]
    wide = q.shape[1]

    @pl.when(i == 0)
    def _():
        low[...] = grad_in[...].astype(BF16)
        xq_t[...] = xq[...].T
        xkv_t[...] = xkv[...].T
        acc[...] = jnp.zeros_like(acc)
        place(keep, send, 0, dot_nn(att_all[...].T, low[...]).astype(BF16), slice(0, d))

    g_att = dot_nt(low[...], wo[...]).astype(BF16)
    dq, dk, dv = quad_back(q[...], k[...], v[...], att[...], g_att, probs)
    dk_out[...] = dk
    dv_out[...] = dv
    place(keep, send, 0, dot_nn(xq_t[...], dq).astype(BF16), aligned(d + i * wide, wide))
    place(keep, send, 1, dot_nn(xkv_t[...], dk).astype(BF16), aligned(i * wide, wide))
    place(keep, send, 1, dot_nn(xkv_t[...], dv).astype(BF16), aligned(d + i * wide, wide))
    acc[...] += dot_nt(dq, wq[...])

    @pl.when(i == pl.num_programs(0) - 1)
    def _():
        part, g_gain, g_shift = norm_back(res[...], gains[1:2], acc[...])
        grad = grad_in[...] + part
        grad_out[...] = grad
        vectors[0:1] = jnp.sum(low[...].astype(F32), axis=0, keepdims=True)
        vectors[1:2] = g_gain
        vectors[2:3] = g_shift
        grad_low = grad.astype(BF16)
        vectors[3:4] = jnp.sum(grad_low.astype(F32), axis=0, keepdims=True)
        vectors[4:8] = jnp.zeros((4, d), F32)
        out = dot_nn(att_self[...].T, grad_low).astype(BF16)
        place(keep, send, 0, out[:, : d // 2], slice(2 * d, 2 * d + d // 2))
        place(keep, send, 1, out[:, d // 2 :], slice(2 * d, 2 * d + d // 2))


def self_back_kernel(
    grad_in, xq, q, k, v, att, probs, wo, keep, send, dk_out, dv_out, dq_out, low, xq_t,
):
    i = pl.program_id(0)
    d = xq.shape[1]
    wide = q.shape[1]

    @pl.when(i == 0)
    def _():
        low[...] = grad_in[...].astype(BF16)
        xq_t[...] = xq[...].T

    g_att = dot_nt(low[...], wo[...]).astype(BF16)
    dq, dk, dv = quad_back(q[...], k[...], v[...], att[...], g_att, probs)
    dq_out[...] = dq
    dk_out[...] = dk
    dv_out[...] = dv
    place(keep, send, 0, dot_nn(xq_t[...], dq).astype(BF16), aligned(i * wide, wide))
    place(keep, send, 1, dot_nn(xq_t[...], dv).astype(BF16), aligned(i * wide, wide))
    keys = dot_nn(xq_t[...], dk).astype(BF16)
    half = wide // 2
    for t in range(2):
        piece = 2 * i + t
        bucket = jnp.where(piece * half < d // 2, 0, 1)
        at = d + piece * half - bucket * (d // 2)
        place(keep, send, bucket, keys[:, t * half : (t + 1) * half], aligned(at, half))


def cross_back(rows, grad_in, res, xq, xkv, q, k, v, att, probs, gains, wo, wq, att_self):
    d = xq.shape[1]
    wide = QUAD * HDIM
    halves = (2, 2, 2, 2, d // 16, 2 * d + d // 2)
    at = cols(rows, wide)
    full = whole((rows, d))
    return pl.pallas_call(
        cross_back_kernel,
        grid=(d // wide,),
        in_specs=[
            full, full, full, full, at, at, at, at, full,
            pl.BlockSpec((QUAD, rows, rows), lambda i: (i, 0, 0)),
            whole((3, d)), rowblk(wide, d), cols(d, wide), full,
        ],
        out_specs=[*[whole(halves)] * 2, at, at, whole((8, d)), full],
        out_shape=[
            *[shaped(*halves)] * 2, held(rows, d), held(rows, d), held(8, d, dtype=F32), held(rows, d, dtype=F32),
        ],
        scratch_shapes=[
            pltpu.VMEM((rows, d), BF16), pltpu.VMEM((d, rows), BF16), pltpu.VMEM((d, rows), BF16),
            pltpu.VMEM((rows, d), F32),
        ],
        compiler_params=params(),
        cost_estimate=cost(18 * rows * d * d + 24 * HEADS * rows * rows * 128, 16 * d * d),
        name="cross_back",
    )(grad_in, res, xq, xkv, q, k, v, att, att, probs, gains, wo, wq, att_self)


def self_back(rows, grad_in, xq, q, k, v, att, probs, wo):
    d = xq.shape[1]
    wide = QUAD * HDIM
    halves = (2, 2, 2, 2, d // 16, d + d // 2)
    at = cols(rows, wide)
    full = whole((rows, d))
    return pl.pallas_call(
        self_back_kernel,
        grid=(d // wide,),
        in_specs=[
            full, full, at, at, at, at,
            pl.BlockSpec((QUAD, rows, rows), lambda i: (i, 0, 0)), rowblk(wide, d),
        ],
        out_specs=[*[whole(halves)] * 2, at, at, at],
        out_shape=[*[shaped(*halves)] * 2, held(rows, d), held(rows, d), held(rows, d)],
        scratch_shapes=[pltpu.VMEM((rows, d), BF16), pltpu.VMEM((d, rows), BF16)],
        compiler_params=params(),
        cost_estimate=cost(18 * rows * d * d + 24 * HEADS * rows * rows * 128, 16 * d * d),
        name="self_back",
    )(grad_in, xq, q, k, v, att, probs, wo)


def through(parts, weights):
    total = None
    for i, part in enumerate(parts):
        d = part.shape[1]
        term = dot_nt(part[...], weights[:, i * d : (i + 1) * d])
        total = term if total is None else total + term
    return total


def store_padded(out, values):
    rows = values.shape[0]
    out[0:rows] = values
    if out.shape[0] > rows:
        out[rows:] = jnp.zeros((out.shape[0] - rows, out.shape[1]), out.dtype)


def optic_kernel(dk, dv, weights, out):
    store_padded(out, through([dk, dv], weights))


def optic(local_rows, dk, dv, weights):
    rows, d = dk.shape
    return pl.pallas_call(
        optic_kernel,
        in_specs=[whole(dk.shape), whole(dv.shape), whole(weights.shape)],
        out_specs=whole((local_rows, d)),
        out_shape=held(local_rows, d, dtype=F32),
        grid=(1,),
        compiler_params=params(),
        cost_estimate=cost(4 * rows * d * d, 4 * d * d),
        name="optic",
    )(*far(dk, dv, weights))


def radar_kernel(dq, dk, dv, weights, grad_in, radar, gains, hidden_vec, cross_vec, out, vectors):
    total = through([dq, dk, dv], weights)
    part, g_gain, g_shift = norm_back(radar[...].astype(F32), gains[0:1], total)
    store_padded(out, grad_in[...] + part)
    vectors[0:1] = g_gain
    vectors[1:2] = cross_vec[1:2]
    vectors[2:3] = hidden_vec[4:5]
    vectors[3:4] = g_shift
    vectors[4:5] = cross_vec[2:3]
    vectors[5:6] = hidden_vec[5:6]
    vectors[6:7] = cross_vec[3:4]
    vectors[7:8] = cross_vec[0:1]
    vectors[8:9] = hidden_vec[6:7]
    vectors[9:13] = hidden_vec[0:4]
    vectors[13:16] = jnp.zeros((3, out.shape[1]), F32)


def radar(local_rows, dq, dk, dv, weights, grad_in, tokens, gains, vectors):
    rows, d = dq.shape
    full = whole((rows, d))
    return pl.pallas_call(
        radar_kernel,
        grid=(1,),
        in_specs=[full, full, full, whole(weights.shape), full, full, whole((3, d)), *[whole((8, d))] * 2],
        out_specs=[whole((local_rows, d)), whole((16, d))],
        out_shape=[held(local_rows, d, dtype=F32), shaped(16, d, dtype=F32)],
        compiler_params=params(),
        cost_estimate=cost(6 * rows * d * d, 6 * d * d),
        name="radar",
    )(*far(dq, dk, dv, weights, grad_in, tokens), gains, *vectors)
def hop(values, perm):
    return lax.ppermute(values, ("grp", "hd"), perm)


def pairs(move):
    found = []
    for z in range(4):
        for x in range(2):
            for y in range(2):
                for c in range(2):
                    to = move(z, x, y, c)
                    if to is not None:
                        tz, tx, ty, tc = to
                        found.append(((z * 2 + x) * 4 + y * 2 + c, (tz * 2 + tx) * 4 + ty * 2 + tc))
    return found


ACROSS_CORE = pairs(lambda z, x, y, c: (z, x, y, 1 - c))
ACROSS_Y = pairs(lambda z, x, y, c: (z, x, 1 - y, c))
ACROSS_X = pairs(lambda z, x, y, c: (z, 1 - x, y, c))
ACROSS_P = pairs(lambda z, x, y, c: (z ^ 1, x, y, c))
ACROSS_Q = pairs(lambda z, x, y, c: (z ^ 2, x, y, c))
ACROSS_XP = pairs(lambda z, x, y, c: (z ^ 1, 1 - x, y, c))


def add(*terms):
    total = terms[0].astype(F32)
    for term in terms[1:]:
        total = total + term.astype(F32)
    return total.astype(terms[0].dtype)


def in_order(at, own, other):
    return jnp.where(at == 0, own, other), jnp.where(at == 0, other, own)


def tie(values):
    return list(lax.optimization_barrier(tuple(values)))


MOVES = {
    "C": ACROSS_CORE, "Y": ACROSS_Y, "X": ACROSS_X, "P": ACROSS_P, "Q": ACROSS_Q,
    "A": ACROSS_P, "G": ACROSS_X, "D": ACROSS_XP, "W": ACROSS_Y, "V": ACROSS_X,
    "B": ACROSS_P, "H": ACROSS_X,
}


class Flow:
    def __init__(self, value, at_x, at_p):
        self.value, self.ends, self.at_x, self.at_p = value, {}, at_x, at_p

    def operand(self, stage):
        return self.value[1] if stage in ("Y", "P") else self.value

    def absorb(self, stage, got):
        if stage in ("Y", "P"):
            self.value = add(self.value[0], got)
        elif stage == "Q":
            self.value = add(self.value, got)
        elif stage == "B":
            self.value = jnp.stack([self.value, got])
        else:
            self.ends[stage] = got

    def together(self):
        if "H" in self.ends:
            sides = [jnp.stack(in_order(self.at_p, v[0], v[1])) for v in (self.value, self.ends["H"])]
            return in_order(self.at_x, *sides)
        rows = [
            jnp.stack(in_order(self.at_p, self.value, self.ends["A"])),
            jnp.stack(in_order(self.at_p, self.ends["G"], self.ends["D"])),
        ]
        return in_order(self.at_x, *rows)


class InFlow(Flow):
    def operand(self, stage):
        return self.value[1] if stage == "C" else super().operand(stage)

    def absorb(self, stage, got):
        if stage == "C":
            self.value = jnp.stack([self.value[0], got])
        else:
            super().absorb(stage, got)


class RowFlow(Flow):
    def __init__(self, keep, send, at_x, at_p):
        super().__init__(None, at_x, at_p)
        self.keep, self.send, self.parts = keep, send, None

    def operand(self, stage):
        if stage == "C":
            return self.send
        if stage in "XYWV":
            return self.parts[int(stage in "WV")][1]
        if stage == "P" and self.value is None:
            self.value = jnp.stack(self.parts)
        return self.value[:, 1] if stage == "P" else self.value

    def absorb(self, stage, got):
        if stage == "C":
            self.parts = [[add(self.keep[b, i], got[b, i]) for i in range(2)] for b in range(2)]
        elif stage in "XYWV":
            b = int(stage in "WV")
            self.parts[b] = add(self.parts[b][0], got)
        elif stage == "P":
            self.value = add(self.value[:, 0], got)
        else:
            super().absorb(stage, got)


class Vectors(Flow):
    def operand(self, stage):
        return self.value

    def absorb(self, stage, got):
        self.value = self.value + got


def whole_rows(keep, send, bucket, at):
    at_y, at_c, at_x, at_p = at
    lead_at, other_at = (at_x, at_y) if bucket == 0 else (at_y, at_x)
    parts = jnp.stack(in_order(at_c, keep[bucket], send[bucket]))
    for axis, place_at in ((1, lead_at), (2, other_at), (3, at_p)):
        own, other = [lax.index_in_dim(parts, i, axis, keepdims=False) for i in range(2)]
        parts = jnp.stack(in_order(place_at, own, other), axis=axis)
    order = (2, 0, 1, 3, 4, 5) if bucket == 0 else (1, 0, 2, 3, 4, 5)
    return parts.transpose(order).reshape(-1, parts.shape[-1])


def summed_anywhere(grad):
    mine = lax.psum_scatter(grad, "hd", scatter_dimension=0, tiled=True)
    return lax.psum(mine.astype(F32), "grp")


class Plan:
    def __init__(self):
        self.flows, self.flying = {}, {}

    def begin(self, gate, *moves):
        sent = [self.flows[m[0]].operand(m[1]) for m in moves]
        gate, *sent = tie([gate, *sent])
        for m, operand in zip(moves, sent):
            self.flying[m] = hop(operand, MOVES[m[1]])
        return gate

    def end(self, gate, *moves):
        gate, *got = tie([gate, *[self.flying.pop(m) for m in moves]])
        for m, value in zip(moves, got):
            self.flows[m[0]].absorb(m[1], value)
        return gate


def on_device(
    radar_tokens, optic_tokens, tile_lengths, norm_gains, norm_shifts, self_qkv, self_out,
    cross_query, cross_keyval, cross_out, hidden_in, hidden_out, proj_biases, hidden_bias, cotangent,
):
    local_rows, d = radar_tokens.shape
    ff = hidden_in.shape[1]
    known = lax.axis_size("grp") == 8 and lax.axis_size("hd") == 4
    at_hd = lax.axis_index("hd")
    at_grp = lax.axis_index("grp")
    at_y, at_c, at_z, at_x = at_hd // 2, at_hd % 2, at_grp // 2, at_grp % 2
    at_p = at_z % 2
    rows = rows_in_use(local_rows, tile_lengths.shape[2])
    hb = hidden_bias[None]

    n1, q1, k1, v1, p1, att1, res1, n2, gf = self_forward(
        rows, tile_lengths, radar_tokens, cotangent, norm_gains, norm_shifts, proj_biases, self_qkv, self_out
    )
    if known:
        n2, gf = tie([n2, gf])
        gf_x = hop(gf, ACROSS_X)
        gf_c = hop(gf, ACROSS_CORE)
    q2, k2, v2, p2, att2, res2, n3 = cross_forward(
        rows, tile_lengths, res1, n2, optic_tokens, norm_gains, norm_shifts, proj_biases,
        cross_query, cross_keyval, cross_out,
    )
    if known:
        n3, gf_x, gf_c, res2 = tie([n3, gf_x, gf_c, res2])
        gf_xc = hop(gf_x, ACROSS_CORE)
        n3_x = hop(n3, ACROSS_X)
        n3_c = hop(n3, ACROSS_CORE)
    act, grad_two, hidden_vec = hidden(rows, res2, n3, gf, norm_gains, hb, hidden_in, hidden_out)

    def own_vectors(sums):
        return (
            lax.dynamic_slice_in_dim(sums[:9], at_hd * (d // 4), d // 4, 1),
            lax.dynamic_index_in_dim(sums[9:13], at_hd, 0, keepdims=False),
        )

    def cross_step(grad):
        return cross_back(
            rows, grad, res1, n2, optic_tokens, q2, k2, v2, att2, p2, norm_gains, cross_out, cross_query, att1
        )

    def self_step(grad):
        return self_back(rows, grad, n1, q1, k1, v1, att1, p1, self_out)

    def radar_step(dq, grad):
        return radar(local_rows, dq, dk1, dv1, self_qkv, grad, radar_tokens, norm_gains, [hidden_vec, cross_vec])

    if known:
        meta = jnp.stack([at_y, at_c, at_x, at_p]).astype(jnp.int32)
        act, n3_x, n3_c, gf_x, gf_c, gf_xc, grad_two = tie([act, n3_x, n3_c, gf_x, gf_c, gf_xc, grad_two])
        n3_xc = hop(n3_x, ACROSS_CORE)
        dwin, dwout = hidden_grads(
            rows, meta, [n3, n3_x, n3_c, n3_xc], [gf, gf_x, gf_c, gf_xc], hb, hidden_in, hidden_out
        )
        plan = Plan()
        grad_two, dwin, dwout = tie([grad_two, dwin, dwout])
        plan.flows["o"], plan.flows["n"] = Flow(dwout, at_x, at_p), InFlow(dwin, at_x, at_p)

        grad_two = plan.begin(grad_two, "oY", "nP")
        keep, send, dk2, dv2, cross_vec, grad_one = cross_step(grad_two)
        act = plan.end(tie([act, grad_one])[0], "oY", "nP")
        plan.flows["a"] = RowFlow(keep, send, at_x, at_p)

        act = plan.begin(act, "aC", "nY", "oP")
        layer_output = output(rows, local_rows, tile_lengths, act, res2, proj_biases, hidden_out)
        grad_one = plan.end(tie([grad_one, layer_output])[0], "aC", "nY", "oP")

        grad_one = plan.begin(grad_one, "oQ", "aX", "aW", "nC")
        keep, send, dk1, dv1, dq1 = self_step(grad_one)
        dq1 = plan.end(dq1, "oQ", "aX", "aW", "nC")
        plan.flows["c"] = RowFlow(keep, send, at_x, at_p)

        dq1 = plan.begin(dq1, "nQ", "aV", "aY", "cC", "oB")
        radar_grad, small = radar_step(dq1, grad_one)
        dk2 = plan.end(tie([dk2, radar_grad])[0], "nQ", "aV", "aY", "cC", "oB")
        plan.flows["s"] = Vectors(small, at_x, at_p)

        dk2 = plan.begin(dk2, "cX", "cW", "aP", "sC")
        optic_grad = optic(local_rows, dk2, dv2, cross_keyval)
        gate = plan.end(optic_grad, "cX", "cW", "aP", "sC")

        for stages in (
            ("cV", "aQ", "oH", "cY", "nB", "sY"),
            ("cP", "nH", "aB", "sX"),
            ("cQ", "aH", "sP"),
        ):
            gate = plan.end(plan.begin(gate, *stages), *stages)
        gate = plan.begin(gate, "cG", "cD", "cA", "sQ")
        cross = plan.flows["a"]
        gate, cross.value, cross.ends["H"] = tie([gate, cross.value, cross.ends["H"]])
        sides = cross.together()
        gate, cross_a, cross_b = tie(
            [gate, *[jnp.stack([v[:, i] for v in sides]).reshape(d // 4, -1).astype(F32) for i in range(2)]]
        )
        gate = plan.end(gate, "sQ")
        gate, vectors, hidden_part = tie([gate, *own_vectors(plan.flows["s"].value)])
        gate = plan.end(gate, "cG", "cD", "cA")
        optic_grad = gate

        done = {name: plan.flows[name].together() for name in "onc"}
        out_part = jnp.stack(done["o"]).reshape(-1, d).astype(F32)
        slices = [in_order(at_c, v[:, 0], v[:, 1]) for v in done["n"]]
        half = ff // 8
        in_part = jnp.concatenate(
            [
                slices[x][c][..., y * half : (y + 1) * half].reshape(-1, half)
                for y in range(2) for c in range(2) for x in range(2)
            ],
            axis=1,
        ).astype(F32)
        self_a, self_b = [
            jnp.stack([v[:, i] for v in done["c"]]).reshape(d // 4, -1).astype(F32) for i in range(2)
        ]
    else:
        into, out = [], []
        for c in range(2):
            for x in range(2):
                at = jnp.asarray([0, c, x, 0], jnp.int32)
                dwin, dwout = hidden_grads(rows, at, [n3], [gf], hb, hidden_in, hidden_out)
                dwin = dwin.transpose(1, 2, 0, 3, 4)
                into.append(jnp.stack([dwin[:, c], dwin[:, 1 - c]], axis=1).reshape(d, 2, ff // 8))
                out.append(dwout.reshape(2, ff // 8, d))
        in_part = summed_anywhere(jnp.stack(into, axis=2).reshape(d, ff))
        out_part = summed_anywhere(jnp.stack(out, axis=1).reshape(ff, d))
        cross_keep, cross_send, dk2, dv2, cross_vec, grad_one = cross_step(grad_two)
        self_keep, self_send, dk1, dv1, dq1 = self_step(grad_one)
        radar_grad, small = radar_step(dq1, grad_one)
        optic_grad = optic(local_rows, dk2, dv2, cross_keyval)
        layer_output = output(rows, local_rows, tile_lengths, act, res2, proj_biases, hidden_out)
        at = (at_y, at_c, at_x, at_p)
        cross_a, cross_b = [summed_anywhere(whole_rows(cross_keep, cross_send, b, at)) for b in range(2)]
        self_a, self_b = [summed_anywhere(whole_rows(self_keep, self_send, b, at)) for b in range(2)]
        vectors, hidden_part = own_vectors(lax.psum(small, ("grp", "hd")))
    return (
        layer_output,
        radar_grad,
        optic_grad,
        jnp.concatenate([self_a, self_b[:, d:], self_b[:, :d]], axis=1),
        jnp.concatenate([cross_a[:, 2 * d :], cross_b[:, 2 * d :]], axis=1),
        cross_a[:, d : 2 * d],
        cross_b[:, : 2 * d],
        cross_a[:, :d],
        in_part,
        out_part,
        vectors[0:3],
        vectors[3:6],
        vectors[6:9],
        hidden_part,
    )


def solution(mesh):
    rows = P(("grp", "hd"), None)
    kept = P("hd", None)
    vector = P(None, "hd")
    return jax.shard_map(
        on_device,
        mesh=mesh,
        in_specs=(rows, rows, P("grp", None, None), *[P()] * 11, rows),
        out_specs=(rows, rows, rows, *[kept] * 7, vector, vector, vector, P("hd")),
        check_vma=False,
    )
```
